32 devices in a mesh: pipe: 4 (over x, core), tx: 4 (over z), ty: 2 (over y).
Axes of the slice: x: 2, y: 2, z: 4, core: 2. Of those that a mesh axis runs over, the one named last changes fastest.
Arguments:
- stored: bfloat16 [4, 2, 4, 2, 256, 512], P('pipe', None, 'tx', 'ty'), may hold values from -6 to 6
- cotangent: bfloat16 [2, 4, 2, 256, 512], P(None, 'tx', 'ty'), may hold values from -6 to 6
- weight: bfloat16 [4, 512, 512], P('pipe'), may hold values from -0.25 to 0.25
- local_edges: bfloat16 [2, 4, 2, 2, 2, 128, 128], P(None, 'tx', 'ty'), may hold values from -0.21875 to 0.21875
- halo_edges: bfloat16 [2, 4, 2, 4, 2, 128, 128], P(None, 'tx', 'ty'), may hold values from -0.21875 to 0.21875
- pattern: int32 [2, 4, 2, 2, 6], P(None, 'tx', 'ty'), may hold values 0 or 1
- pick: int32 [2, 4, 2, 4], P(None, 'tx', 'ty'), may hold values from 0 to 1
Outputs:
- grad_weight: float32 [4, 512, 512], P('pipe', ('tx', 'ty'))
- grad_input: bfloat16 [4, 2, 4, 2, 256, 512], P('pipe', None, 'tx', 'ty')
The draws below stay inside these ranges and needn't reach their ends.
Inputs may be any that keep to these rules, and one draw needn't show every extreme that they name: `pattern`: 1 where a block of edges is present, 0 where it is absent. `pick`: a block index of the sending tile.
All inputs are finite; a program needn't handle non-finite values.
Results may differ from the reference program's by a relative error of at most 0.015.
Values may be sent and summed in bfloat16 or wider, within the bound.
No kernel may reach another device: no remote copies, remote signals or barrier semaphores. Data moves between devices by JAX's collectives and lax.ppermute only.
A program may use at most 64 MiB of HBM per device.

```python
import math
import jax
import jax.numpy as jnp
from jax import lax

D = 512
BLK = 128
NB = 2
MB = 2
SECTIONS = 4
TILES_X = 4
TILES_Y = 2
NT = 256
TOTAL_NODES = 4096


def with_ends(array, key, smallest, largest):
    index_at = [jax.random.randint(jax.random.fold_in(key, axis), (), 0, length) for axis, length in enumerate(array.shape)]
    main_axis = array.shape.index(max(array.shape))
    neighbour = index_at[:main_axis] + [(index_at[main_axis] + 1) % array.shape[main_axis]] + index_at[main_axis + 1:]
    return array.at[tuple(index_at)].set(smallest).at[tuple(neighbour)].set(largest)


def strengthened(drawn, own_key, source, target, parts, factor):
    owner, partner = [(jnp.arange(drawn.shape[axis_at]) // (drawn.shape[axis_at] // parts)).reshape([-1 if axis == axis_at else 1 for axis in range(drawn.ndim)]) for axis_at in (source, target)]
    chosen = jax.random.permutation(own_key, parts)[partner]
    strong = (owner == chosen) | (owner == (partner + parts // 2) % parts)
    return jnp.where(strong, factor * drawn, drawn)


def block_levels(own_key, dims, pieces, low, high):
    gain = 1.0
    for axis_at, parts in pieces:
        steps = jax.random.uniform(jax.random.fold_in(jax.random.fold_in(own_key, 6), axis_at), (parts,), jnp.float32, low / len(pieces), high / len(pieces))
        gain = gain * jnp.repeat(jnp.exp(steps), dims[axis_at] // parts).reshape((-1,) + (1,) * (len(dims) - 1 - axis_at))
    return gain


def scatter_about(stream_key, dims, width, reach, cuts=(), held_as=jnp.bfloat16):
    result = jax.random.normal(stream_key, dims, jnp.float32) * width
    if len(cuts) > 0:
        result = block_levels(stream_key, dims, cuts, -0.22, 0.18) * result
    return jnp.clip(result, min=-reach, max=reach).astype(held_as)


def gaussian_with(key, shape, spread, limit, split, heavy, held_as=jnp.bfloat16):
    array = spread * jax.random.normal(key, shape, jnp.float32)
    if split:
        array = array * block_levels(key, shape, split, -0.22, 0.18)
    return jnp.clip(strengthened(array, jax.random.fold_in(key, 3), *heavy), -limit, limit).astype(held_as)


def setup_inputs(seed: int = 0) -> dict:
    key_of = jax.random.split(jax.random.key(seed), 8)
    stored = gaussian_with(key_of[0], (SECTIONS, MB, TILES_X, TILES_Y, NT, D), 1.0, 6.0, ((0, 4), (2, 4), (3, 2)), (3, 5, 2, 2.0))
    cotangent = scatter_about(key_of[1], (MB, TILES_X, TILES_Y, NT, D), 1.0, 6.0, ((1, 4), (2, 2)))
    weight = scatter_about(key_of[2], (SECTIONS, D, D), D ** -0.5, 0.25, ((0, 4),))
    local_edges = scatter_about(key_of[3], (MB, TILES_X, TILES_Y, NB, NB, BLK, BLK), (BLK * (NB + 4)) ** -0.5, 0.21875, ((1, 4), (2, 2)))
    halo_edges = scatter_about(key_of[4], (MB, TILES_X, TILES_Y, 4, NB, BLK, BLK), (BLK * (NB + 4)) ** -0.5, 0.21875, ((1, 4), (2, 2)))
    pattern = with_ends((jax.random.randint(key_of[5], (MB, TILES_X, TILES_Y, NB, NB + 4), 0, 4) < 3).astype(jnp.int32), jax.random.fold_in(key_of[5], 1), 0, 1)
    pick = with_ends(jax.random.randint(key_of[6], (MB, TILES_X, TILES_Y, 4), 0, NB), jax.random.fold_in(key_of[6], 1), 0, NB - 1).astype(jnp.int32)
    return {"stored": stored, "cotangent": cotangent, "weight": weight, "local_edges": local_edges, "halo_edges": halo_edges, "pattern": pattern, "pick": pick}


def silu_slope(value):
    sigma = jax.nn.sigmoid(value)
    return sigma * (1.0 + value * (1.0 - sigma))

def rounded(values):
    return lax.optimization_barrier(values.astype(jnp.bfloat16)).astype(jnp.float32)

def reference(stored, cotangent, weight, local_edges, halo_edges, pattern, pick):
    block_mask = pattern.astype(jnp.float32)
    local_masked = local_edges.astype(jnp.float32) * block_mask[..., :NB, None, None]
    halo_masked = halo_edges.astype(jnp.float32) * jnp.swapaxes(block_mask[..., NB:], -1, -2)[..., None, None]
    placing = (pick[..., None] == jnp.arange(NB, dtype=jnp.int32)).astype(jnp.float32)
    scale = 1.0 / math.sqrt(TOTAL_NODES)
    upstream = cotangent.astype(jnp.float32)
    grads_in = [None] * SECTIONS
    grads_weight = [None] * SECTIONS
    for section in reversed(range(SECTIONS)):
        features = stored[section].astype(jnp.float32)
        matrix = weight[section].astype(jnp.float32)
        pre_activation = jnp.einsum('mxynd,de->mxyne', features, matrix)
        slope_grad = rounded(upstream * silu_slope(pre_activation))
        grads_weight[section] = jnp.einsum('mxynd,mxyne->de', features, slope_grad) * scale
        message_grad = rounded(jnp.einsum('mxyne,de->mxynd', slope_grad, matrix))
        grad_blocks = message_grad.reshape(MB, TILES_X, TILES_Y, NB, BLK, D)
        inner = jnp.einsum('mxybcij,mxybik->mxycjk', local_masked, grad_blocks)
        outward = rounded(jnp.einsum('mxyebij,mxybik->mxyejk', halo_masked, grad_blocks))
        zero_x = jnp.zeros_like(outward[:, :1, :, 0])
        from_upper_x = jnp.concatenate([outward[:, 1:, :, 0], zero_x], axis=1)
        from_lower_x = jnp.concatenate([zero_x, outward[:, :-1, :, 1]], axis=1)
        zero_y = jnp.zeros_like(outward[:, :, :1, 2])
        from_upper_y = jnp.concatenate([outward[:, :, 1:, 2], zero_y], axis=2)
        from_lower_y = jnp.concatenate([zero_y, outward[:, :, :-1, 3]], axis=2)
        arrived = jnp.stack([from_upper_x, from_lower_x, from_upper_y, from_lower_y], axis=3)
        placed = jnp.einsum('mxyec,mxyejk->mxycjk', placing, arrived, precision=lax.Precision.HIGHEST)
        total = upstream + (inner + placed).reshape(MB, TILES_X, TILES_Y, NT, D)
        upstream = rounded(total)
        grads_in[section] = upstream
    return (jnp.stack(grads_weight), jnp.stack(grads_in).astype(jnp.bfloat16))
```

```python
import math

import jax
import jax.numpy as jnp
from jax import lax
from jax.sharding import PartitionSpec as P

AXES = ("pipe", "tx", "ty")


def silu_slope(value):
    sigma = jax.nn.sigmoid(value)
    return sigma * (1.0 + value * (1.0 - sigma))


def swap_phases(count):
    phases = []
    for first in (0, 1):
        pairs = [(low, low + 1) for low in range(first, count - 1, 2)]
        if pairs:
            phases.append((first, pairs))
    return phases


def per_device(stored, cotangent, weight, local_edges, halo_edges, pattern, pick):
    sizes = tuple(lax.axis_size(name) for name in AXES)
    sections, rows, columns = sizes
    here, row, column = (lax.axis_index(name) for name in AXES)
    lower = sections // 2
    upper = sections - lower
    top = sections - 1

    def flat(section, x, y):
        return (section * rows + x) * columns + y

    def to_sections(value, moves):
        pairs = [
            (flat(source, x, y), flat(target, x, y))
            for source, target in moves
            for x in range(rows)
            for y in range(columns)
        ]
        return lax.ppermute(value, AXES, pairs)

    features = stored[0, :, 0, 0]
    matrix = weight[0]
    batches, nodes, width = features.shape
    blocks = local_edges.shape[3]
    block_size = local_edges.shape[5]
    block_mask = pattern[:, 0, 0].astype(jnp.bfloat16)
    local_masked = local_edges[:, 0, 0] * block_mask[:, :, :blocks, None, None]
    halo_masked = (
        halo_edges[:, 0, 0] * jnp.swapaxes(block_mask[:, :, blocks:], 1, 2)[:, :, :, None, None]
    )
    picks = pick[:, 0, 0]

    slope = silu_slope(
        jnp.einsum("mnd,de->mne", features, matrix, preferred_element_type=jnp.float32)
    ).astype(jnp.bfloat16)

    exchanges = []
    for axis, position, base, count in ((1, row, 0, rows), (2, column, 2, columns)):
        for first, couples in swap_phases(count):
            is_low = (position - first) % 2 == 0
            pairs = {}
            for lead in {0, top}:
                pairs[lead] = [
                    (
                        flat(lead, *((a, other) if axis == 1 else (other, a))),
                        flat(lead, *((b, other) if axis == 1 else (other, b))),
                    )
                    for low, high in couples
                    for a, b in ((low, high), (high, low))
                    for other in range(columns if axis == 1 else rows)
                ]
            edges = jnp.where(is_low, halo_masked[:, base + 1], halo_masked[:, base])
            target = jnp.where(is_low, picks[:, base], picks[:, base + 1])
            place = (target[:, None] == jnp.arange(blocks)[None]).astype(jnp.float32)
            exchanges.append((pairs, edges, place))

    def section_round(upstream, slope, matrix, lead):
        slope_grad = (upstream.astype(jnp.float32) * slope.astype(jnp.float32)).astype(jnp.bfloat16)
        message_grad = jnp.einsum(
            "mne,de->mnd", slope_grad, matrix, preferred_element_type=jnp.float32
        ).astype(jnp.bfloat16)
        grad_blocks = message_grad.reshape(batches, blocks, block_size, width)
        total = upstream.astype(jnp.float32).reshape(batches, blocks, block_size, width)
        arrivals = []
        for pairs, edges, place in exchanges:
            outward = jnp.einsum(
                "mbij,mbik->mjk", edges, grad_blocks, preferred_element_type=jnp.float32
            ).astype(jnp.bfloat16)
            arrivals.append((lax.ppermute(outward, AXES, pairs[lead]), place))
        total = total + jnp.einsum(
            "mbcij,mbik->mcjk", local_masked, grad_blocks, preferred_element_type=jnp.float32
        )
        for arrived, place in arrivals:
            total = total + place[:, :, None, None] * arrived.astype(jnp.float32)[:, None]
        return slope_grad, total.astype(jnp.bfloat16).reshape(batches, nodes, width)

    fetched = [(slope, matrix)]
    for step in range(1, upper):
        moves = [(top - step, top)] + ([(step, 0)] if step < lower else [])
        fetched.append((to_sections(slope, moves), to_sections(matrix, moves)))

    slope_grads, results = {}, {}
    upstream = cotangent[:, 0, 0]
    for section in reversed(range(sections)):
        lead = top if section >= lower else 0
        steps = top - section if section >= lower else section
        if section == lower - 1:
            upstream = to_sections(upstream, [(top, 0)])
        slope_grads[section], upstream = section_round(upstream, *fetched[steps], lead)
        results[section] = upstream

    def home(values):
        mine = values[top] if sections == 1 else jnp.where(here == top, values[top], values[0])
        for step in range(1, upper):
            moves = [(top, top - step)]
            sent = values[top - step]
            if step < lower:
                moves.append((0, step))
                sent = jnp.where(here == top, sent, values[step])
            got = to_sections(sent, moves)
            takes = here == top - step
            if step < lower:
                takes = takes | (here == step)
            mine = jnp.where(takes, got, mine)
        return mine

    own_grad = home(slope_grads)
    product = jnp.einsum("mnd,mne->de", features, own_grad, preferred_element_type=jnp.float32)
    tiles = rows * columns
    pieces = product.astype(jnp.bfloat16).reshape(tiles, width // tiles, width)
    pieces = lax.all_to_all(pieces, ("tx", "ty"), 0, 0, tiled=True)
    scale = 1.0 / math.sqrt(batches * nodes * tiles)
    summed = jnp.sum(pieces.astype(jnp.float32), axis=0) * scale
    return (summed[None], home(results)[None, :, None, None])


def solution(mesh):
    in_specs = (
        P("pipe", None, "tx", "ty", None, None),
        P(None, "tx", "ty", None, None),
        P("pipe", None, None),
        P(None, "tx", "ty", None, None, None, None),
        P(None, "tx", "ty", None, None, None, None),
        P(None, "tx", "ty", None, None),
        P(None, "tx", "ty", None),
    )
    out_specs = (P("pipe", ("tx", "ty"), None), P("pipe", None, "tx", "ty", None, None))
    return jax.shard_map(
        per_device, mesh=mesh, in_specs=in_specs, out_specs=out_specs, check_vma=False
    )
```

```python
import functools
import math

import jax
import jax.numpy as jnp
from jax import lax
from jax.experimental import pallas as pl
from jax.experimental.pallas import tpu as pltpu
from jax.sharding import PartitionSpec as P

AXES = ("pipe", "tx", "ty")
F32, BF16 = jnp.float32, jnp.bfloat16
IN_VMEM = pl.BlockSpec(memory_space=pltpu.VMEM)
IN_SMEM = pl.BlockSpec(memory_space=pltpu.SMEM)


def silu_slope(value):
    sigma = jax.nn.sigmoid(value)
    return sigma * (1.0 + value * (1.0 - sigma))


def swap_phases(count):
    phases = []
    for first in (0, 1):
        pairs = [(low, low + 1) for low in range(first, count - 1, 2)]
        if pairs:
            phases.append((first, pairs))
    return phases


def side(phase):
    axis, base, first = phase
    return base, lax.rem(lax.axis_index(axis) + first, 2) == 0


def rows_dot(left, right):
    return lax.dot_general(left, right, (((1,), (0,)), ((), ())), preferred_element_type=F32)


def back_dot(left, right):
    return lax.dot_general(left, right, (((1,), (1,)), ((), ())), preferred_element_type=F32)


def send_blocks(grads, matrix, mixing_ref, message_ref, out_refs):
    batches, outgoing, nodes = mixing_ref.shape
    block = out_refs[0].shape[1]
    messages = back_dot(grads, matrix).astype(BF16)
    message_ref[...] = messages
    first = outgoing - block * len(out_refs)
    for batch in range(batches):
        mixed = rows_dot(
            mixing_ref[batch, first:, :], messages[batch * nodes : (batch + 1) * nodes]
        ).astype(BF16)
        for index, out_ref in enumerate(out_refs):
            out_ref[batch] = mixed[index * block : (index + 1) * block]


def first_kernel(
    phases, pattern_ref, features_ref, matrix_ref, given_ref, local_ref, halo_ref,
    layer_ref, mixing_ref, grad_ref, message_ref, *out_refs
):
    batches, blocks, _, block, _ = local_ref.shape
    pre_activation = rows_dot(features_ref[...], matrix_ref[...])
    slope = silu_slope(pre_activation).astype(BF16)
    layer_ref[0] = slope
    layer_ref[1] = matrix_ref[...]
    grads = (given_ref[...].astype(F32) * slope.astype(F32)).astype(BF16)
    grad_ref[...] = grads
    sides = [side(phase) for phase in phases]
    for batch in range(batches):
        for source in range(blocks):
            columns = slice(source * block, (source + 1) * block)
            for target in range(blocks):
                present = pattern_ref[batch, source, target].astype(F32)
                edges = local_ref[batch, source, target].astype(F32) * present
                mixing_ref[batch, target * block : (target + 1) * block, columns] = edges.T.astype(BF16)
            for index, (base, is_low) in enumerate(sides):
                slot = jnp.where(is_low, base + 1, base)
                present = pattern_ref[batch, source, blocks + slot].astype(F32)
                edges = halo_ref[batch, slot, source].astype(F32) * present
                start = (blocks + index) * block
                mixing_ref[batch, start : start + block, columns] = edges.T.astype(BF16)
    send_blocks(grads, matrix_ref[...], mixing_ref, message_ref, out_refs)


def inner_kernel(upstream_ref, message_ref, mixing_ref, total_ref):
    batches, _, nodes = mixing_ref.shape
    for batch in range(batches):
        rows = slice(batch * nodes, (batch + 1) * nodes)
        total_ref[rows] = upstream_ref[rows].astype(F32) + rows_dot(
            mixing_ref[batch, :nodes, :], message_ref[rows]
        )


def gathered(phases, pick_ref, total_ref, arrived_refs, batch, target):
    block = arrived_refs[0].shape[1]
    start = (batch * (total_ref.shape[0] // arrived_refs[0].shape[0])) + target * block
    value = total_ref[start : start + block]
    for phase, arrived_ref in zip(phases, arrived_refs):
        base, is_low = side(phase)
        slot = jnp.where(is_low, base, base + 1)
        here = (pick_ref[batch, slot] == target).astype(F32)
        value = value + arrived_ref[batch].astype(F32) * here
    return start, block, value.astype(BF16)


def close_blocks(phases, pick_ref, total_ref, arrived_refs, result_ref):
    batches, block, _ = arrived_refs[0].shape
    for batch in range(batches):
        for target in range(total_ref.shape[0] // batches // block):
            start, size, value = gathered(phases, pick_ref, total_ref, arrived_refs, batch, target)
            result_ref[start : start + size] = value


def close_kernel(phases, pick_ref, total_ref, *refs):
    close_blocks(phases, pick_ref, total_ref, refs[:-1], refs[-1])


def last_kernel(phases, top, pick_ref, total_ref, *refs):
    arrived_refs = refs[: len(phases)]
    top_ref, got_ref, result_ref = refs[len(phases) :]
    here = lax.axis_index("pipe")

    @pl.when(here == 0)
    def _():
        close_blocks(phases, pick_ref, total_ref, arrived_refs, result_ref)

    @pl.when(here == top)
    def _():
        result_ref[...] = top_ref[...]

    @pl.when((here != 0) & (here != top))
    def _():
        result_ref[...] = got_ref[...]


def step_kernel(layer_ref, mixing_ref, upstream_ref, grad_ref, message_ref, *out_refs):
    grads = (upstream_ref[...].astype(F32) * layer_ref[0].astype(F32)).astype(BF16)
    grad_ref[...] = grads
    send_blocks(grads, layer_ref[1], mixing_ref, message_ref, out_refs)


def close_step_kernel(phases, pick_ref, total_ref, *refs):
    count = len(phases)
    layer_ref, mixing_ref, result_ref, grad_ref, message_ref, *out_refs = refs[count:]
    close_blocks(phases, pick_ref, total_ref, refs[:count], result_ref)
    step_kernel(layer_ref, mixing_ref, result_ref, grad_ref, message_ref, *out_refs)


def weight_product(top, features_ref, grad_ref, top_ref, got_ref, product_ref):
    here = lax.axis_index("pipe")

    def product(ref):
        value = lax.dot_general(
            features_ref[...], ref[...], (((0,), (0,)), ((), ())), preferred_element_type=F32
        )
        product_ref[...] = value.astype(BF16)

    @pl.when(here == 0)
    def _():
        product(grad_ref)

    @pl.when(here == top)
    def _():
        product(top_ref)

    @pl.when((here != 0) & (here != top))
    def _():
        product(got_ref)


def bottom_kernel(phases, top, pick_ref, total_ref, *refs):
    count = len(phases)
    features_ref, top_ref, got_ref = refs[count : count + 3]
    result_ref, grad_ref, product_ref = refs[count + 5 : count + 8]
    close_step_kernel(
        phases, pick_ref, total_ref, *refs[:count], *refs[count + 3 : count + 7], *refs[count + 8 :]
    )
    weight_product(top, features_ref, grad_ref, top_ref, got_ref, product_ref)


def reduce_kernel(scale, pieces_ref, sum_ref):
    value = pieces_ref[0].astype(F32)
    for index in range(1, pieces_ref.shape[0]):
        value = value + pieces_ref[index].astype(F32)
    sum_ref[...] = value * scale


def after(value, token):
    return lax.optimization_barrier((value, token))


def call(body, inputs, outputs, flops, scalars=0, kind=pltpu.VMEM):
    size = sum(math.prod(shape) * jnp.dtype(dtype).itemsize for shape, dtype in outputs)
    size += sum(value.size * value.dtype.itemsize for value in inputs)
    return pl.pallas_call(
        body,
        out_shape=[kind(shape, dtype) for shape, dtype in outputs],
        in_specs=[IN_SMEM] * scalars + [IN_VMEM] * (len(inputs) - scalars),
        out_specs=[IN_VMEM] * len(outputs),
        compiler_params=pltpu.CompilerParams(vmem_limit_bytes=24 * 1024 * 1024),
        cost_estimate=pl.CostEstimate(flops=flops, bytes_accessed=size, transcendentals=0),
    )(*inputs)


def per_device(stored, cotangent, weight, local_edges, halo_edges, pattern, pick):
    sections, rows, columns = (lax.axis_size(name) for name in AXES)
    here = lax.axis_index("pipe")
    lower = sections // 2
    upper = sections - lower
    top = sections - 1

    def flat(section, x, y):
        return (section * rows + x) * columns + y

    def to_sections(value, moves):
        pairs = [
            (flat(source, x, y), flat(target, x, y))
            for source, target in moves
            for x in range(rows)
            for y in range(columns)
        ]
        return lax.ppermute(value, AXES, pairs)

    batches, nodes, width = stored.shape[1], stored.shape[4], stored.shape[5]
    blocks, block = local_edges.shape[3], local_edges.shape[5]
    total_rows = batches * nodes
    features = stored.reshape(total_rows, width)
    matrix = weight[0]
    picks = pick[:, 0, 0]

    phases, routes = [], []
    for axis, base, count in (("tx", 0, rows), ("ty", 2, columns)):
        for first, couples in swap_phases(count):
            phases.append((axis, base, first))
            route = {}
            for lead in {0, top}:
                route[lead] = [
                    (
                        flat(lead, *((a, other) if axis == "tx" else (other, a))),
                        flat(lead, *((b, other) if axis == "tx" else (other, b))),
                    )
                    for low, high in couples
                    for a, b in ((low, high), (high, low))
                    for other in range(columns if axis == "tx" else rows)
                ]
            routes.append(route)
    phases = tuple(phases)
    sent = [((batches, block, width), BF16)] * len(phases)
    whole = ((total_rows, width), BF16)
    mix_rows = (blocks + len(phases)) * block
    cost = 2 * total_rows * width * (width + len(phases) * block)

    def exchange(outs, lead):
        return [lax.ppermute(out, AXES, route[lead]) for out, route in zip(outs, routes)]

    def inner(upstream, message, mixing):
        return call(
            inner_kernel, [upstream, message, mixing], [((total_rows, width), F32)],
            2 * total_rows * width * nodes,
        )[0]

    given = cotangent.reshape(total_rows, width)
    layer, mixing, grad, message, *outs = call(
        functools.partial(first_kernel, phases),
        [pattern[:, 0, 0], features, matrix, given, local_edges[:, 0, 0], halo_edges[:, 0, 0]],
        [((2, total_rows, width), BF16), ((batches, mix_rows, nodes), BF16), whole, whole] + sent,
        cost + 2 * total_rows * width * width,
        1,
    )
    arrived = exchange(outs, top)
    total = inner(given, message, mixing)

    layer_sent, arrived[0] = after(layer, arrived[0])
    layers = [layer]
    for step in range(1, upper):
        moves = [(top - step, top)] + ([(step, 0)] if step < lower else [])
        layers.append(to_sections(layer_sent, moves))

    def fetch_home(values, arrived):
        got = None
        for step in range(1, upper):
            moves = [(top, top - step)]
            value = values[top - step]
            if step < lower:
                moves.append((0, step))
                value = jnp.where(here == top, value, values[step])
            value, arrived[0] = after(value, arrived[0])
            new = to_sections(value, moves)
            takes = here == top - step
            if step < lower:
                takes = takes | (here == step)
            got = new if step == 1 else jnp.where(takes, new, got)
        return got

    grads, results = {top: grad}, {}
    for section in reversed(range(top)):
        lead = top if section >= lower else 0
        steps = top - section if section >= lower else section
        layer_here = layers[steps]
        if section == lower - 1:
            upstream = call(
                functools.partial(close_kernel, phases), [picks, total, *arrived], [whole], 0, 1
            )[0]
            results[section + 1] = upstream
            upstream = to_sections(upstream, [(top, 0)])
            grad, message, *outs = call(
                step_kernel, [layer_here, mixing, upstream], [whole, whole] + sent, cost
            )
        elif section > 0:
            upstream, grad, message, *outs = call(
                functools.partial(close_step_kernel, phases),
                [picks, total, *arrived, layer_here, mixing],
                [whole, whole, whole] + sent, cost, 1,
            )
            results[section + 1] = upstream
        else:
            got = fetch_home(grads, arrived)
            upstream, grad, product, message, *outs = call(
                functools.partial(bottom_kernel, phases, top),
                [picks, total, *arrived, features, grads[top], got, layer_here, mixing],
                [whole, whole, ((width, width), BF16), whole] + sent,
                cost + 2 * total_rows * width * width, 1,
            )
            results[1] = upstream
        grads[section] = grad
        arrived = exchange(outs, lead)
        total = inner(upstream, message, mixing)

    tiles = rows * columns
    pieces = lax.all_to_all(
        product.reshape(tiles, width // tiles, width), ("tx", "ty"), 0, 0, tiled=True
    )
    got = fetch_home(results, arrived)
    result = call(
        functools.partial(last_kernel, phases, top),
        [picks, total, *arrived, results[top], got], [whole], 0, 1, jax.ShapeDtypeStruct,
    )[0]
    scale = 1.0 / math.sqrt(total_rows * tiles)
    summed = call(
        functools.partial(reduce_kernel, scale), [pieces], [((width // tiles, width), F32)], 0, 0,
        jax.ShapeDtypeStruct,
    )[0]
    return (summed[None], result.reshape(1, batches, 1, 1, nodes, width))


def solution(mesh):
    in_specs = (
        P("pipe", None, "tx", "ty", None, None),
        P(None, "tx", "ty", None, None),
        P("pipe", None, None),
        P(None, "tx", "ty", None, None, None, None),
        P(None, "tx", "ty", None, None, None, None),
        P(None, "tx", "ty", None, None),
        P(None, "tx", "ty", None),
    )
    out_specs = (P("pipe", ("tx", "ty"), None), P("pipe", None, "tx", "ty", None, None))
    return jax.shard_map(
        per_device, mesh=mesh, in_specs=in_specs, out_specs=out_specs, check_vma=False
    )
```

```python
import functools
import math

import jax
import jax.numpy as jnp
from jax import lax
from jax.experimental import pallas as pl
from jax.experimental.pallas import tpu as pltpu
from jax.sharding import PartitionSpec as P

AXES = ("pipe", "tx", "ty")
F32, BF16 = jnp.float32, jnp.bfloat16
IN_VMEM = pl.BlockSpec(memory_space=pltpu.VMEM)


def silu_slope(value):
    sigma = jax.nn.sigmoid(value)
    return sigma * (1.0 + value * (1.0 - sigma))


def swap_phases(count):
    phases = []
    for first in (0, 1):
        pairs = [(low, low + 1) for low in range(first, count - 1, 2)]
        if pairs:
            phases.append((first, pairs))
    return phases


def side(phase):
    axis, base, first = phase
    return base, lax.rem(lax.axis_index(axis) + first, 2) == 0


def rows_dot(left, right):
    return lax.dot_general(left, right, (((1,), (0,)), ((), ())), preferred_element_type=F32)


def back_dot(left, right):
    return lax.dot_general(left, right, (((1,), (1,)), ((), ())), preferred_element_type=F32)


def send_blocks(grads, matrix, mixing_ref, message_ref, out_refs):
    batches, outgoing, nodes = mixing_ref.shape
    block = out_refs[0].shape[1]
    messages = back_dot(grads, matrix).astype(BF16)
    message_ref[...] = messages
    first = outgoing - block * len(out_refs)
    for batch in range(batches):
        mixed = rows_dot(
            mixing_ref[batch, first:, :], messages[batch * nodes : (batch + 1) * nodes]
        ).astype(BF16)
        for index, out_ref in enumerate(out_refs):
            out_ref[batch] = mixed[index * block : (index + 1) * block]


def first_kernel(phases, *refs):
    sources, refs = refs[:7], refs[7:]
    layer_ref, mixing_ref, mask_ref, grad_ref, message_ref = refs[:5]
    out_refs = refs[5 : 5 + len(phases)]
    held, sems = refs[5 + len(phases) : -1], refs[-1]
    copies = [
        pltpu.make_async_copy(source, target, sems.at[index])
        for index, (source, target) in enumerate(zip(sources, held))
    ]
    for copy in copies:
        copy.start()
    features_ref, matrix_ref, given_ref, pattern_ref, pick_ref, local_ref, halo_ref = held
    batches, blocks, _, block, _ = local_ref.shape
    sides = [side(phase) for phase in phases]
    copies[0].wait()
    copies[1].wait()
    pre_activation = rows_dot(features_ref[...], matrix_ref[...])
    slope = silu_slope(pre_activation).astype(BF16)
    layer_ref[0] = slope
    layer_ref[1] = matrix_ref[...]
    copies[2].wait()
    grads = (given_ref[...].astype(F32) * slope.astype(F32)).astype(BF16)
    grad_ref[...] = grads
    for copy in copies[3:]:
        copy.wait()
    for batch in range(batches):
        for source in range(blocks):
            columns = slice(source * block, (source + 1) * block)
            for target in range(blocks):
                present = pattern_ref[batch, source, target].astype(F32)
                edges = local_ref[batch, source, target].astype(F32) * present
                mixing_ref[batch, target * block : (target + 1) * block, columns] = edges.T.astype(BF16)
            for index, (base, is_low) in enumerate(sides):
                slot = jnp.where(is_low, base + 1, base)
                present = pattern_ref[batch, source, blocks + slot].astype(F32)
                edges = halo_ref[batch, slot, source].astype(F32) * present
                start = (blocks + index) * block
                mixing_ref[batch, start : start + block, columns] = edges.T.astype(BF16)
        for index, (base, is_low) in enumerate(sides):
            chosen = pick_ref[batch, jnp.where(is_low, base, base + 1)]
            for target in range(blocks):
                here = (chosen == target).astype(F32)
                entry = (batch * blocks + target) * len(sides) + index
                mask_ref[entry] = jnp.full(mask_ref.shape[1:], here, F32)
    send_blocks(grads, matrix_ref[...], mixing_ref, message_ref, out_refs)


def inner_kernel(upstream_ref, message_ref, mixing_ref, total_ref):
    batches, _, nodes = mixing_ref.shape
    for batch in range(batches):
        rows = slice(batch * nodes, (batch + 1) * nodes)
        total_ref[rows] = upstream_ref[rows].astype(F32) + rows_dot(
            mixing_ref[batch, :nodes, :], message_ref[rows]
        )


def turn_kernel(features_ref, turned_ref):
    turned_ref[...] = features_ref[...].T


def choose_kernel(top, top_ref, other_ref, chosen_ref):
    at_top = lax.axis_index("pipe") == top

    @pl.when(at_top)
    def _():
        chosen_ref[...] = top_ref[...]

    @pl.when(jnp.logical_not(at_top))
    def _():
        chosen_ref[...] = other_ref[...]


def close_blocks(mask_ref, total_ref, arrived_refs, result_ref):
    batches, block, _ = arrived_refs[0].shape
    count = len(arrived_refs)
    for batch in range(batches):
        arrived = [ref[batch].astype(F32) for ref in arrived_refs]
        for target in range(total_ref.shape[0] // batches // block):
            order = batch * (total_ref.shape[0] // batches // block) + target
            rows = slice(order * block, (order + 1) * block)
            value = total_ref[rows]
            for index in range(count):
                value = value + arrived[index] * mask_ref[order * count + index]
            result_ref[rows] = value.astype(BF16)


def close_kernel(mask_ref, total_ref, *refs):
    close_blocks(mask_ref, total_ref, refs[:-1], refs[-1])


def last_kernel(top, mask_ref, total_ref, *refs):
    arrived_refs = refs[:-3]
    top_ref, got_ref, result_ref = refs[-3:]
    here = lax.axis_index("pipe")

    @pl.when(here == 0)
    def _():
        close_blocks(mask_ref, total_ref, arrived_refs, result_ref)

    @pl.when(here == top)
    def _():
        result_ref[...] = top_ref[...]

    @pl.when((here != 0) & (here != top))
    def _():
        result_ref[...] = got_ref[...]


def step_kernel(layer_ref, mixing_ref, upstream_ref, grad_ref, message_ref, *out_refs):
    grads = (upstream_ref[...].astype(F32) * layer_ref[0].astype(F32)).astype(BF16)
    grad_ref[...] = grads
    send_blocks(grads, layer_ref[1], mixing_ref, message_ref, out_refs)


def close_step_kernel(count, mask_ref, total_ref, *refs):
    layer_ref, mixing_ref, result_ref, grad_ref, message_ref, *out_refs = refs[count:]
    close_blocks(mask_ref, total_ref, refs[:count], result_ref)
    step_kernel(layer_ref, mixing_ref, result_ref, grad_ref, message_ref, *out_refs)


def weight_product(top, turned_ref, grad_ref, top_ref, got_ref, product_ref):
    here = lax.axis_index("pipe")

    def product(ref):
        product_ref[...] = rows_dot(turned_ref[...], ref[...]).astype(BF16)

    @pl.when(here == 0)
    def _():
        product(grad_ref)

    @pl.when(here == top)
    def _():
        product(top_ref)

    @pl.when((here != 0) & (here != top))
    def _():
        product(got_ref)


def bottom_kernel(count, top, mask_ref, total_ref, *refs):
    turned_ref, top_ref, got_ref, layer_ref, mixing_ref = refs[count : count + 5]
    result_ref, product_ref, next_ref = refs[count + 5 : count + 8]
    out_refs = refs[count + 8 : -2]
    grad_ref, message_ref = refs[-2:]
    close_step_kernel(
        count, mask_ref, total_ref, *refs[:count], layer_ref, mixing_ref,
        result_ref, grad_ref, message_ref, *out_refs
    )
    weight_product(top, turned_ref, grad_ref, top_ref, got_ref, product_ref)
    inner_kernel(result_ref, message_ref, mixing_ref, next_ref)


def reduce_kernel(scale, pieces_ref, sum_ref):
    value = pieces_ref[0].astype(F32)
    for index in range(1, pieces_ref.shape[0]):
        value = value + pieces_ref[index].astype(F32)
    sum_ref[...] = value * scale


def call(body, inputs, outputs, flops, kind=pltpu.VMEM, source=IN_VMEM, scratch=()):
    size = sum(math.prod(shape) * jnp.dtype(dtype).itemsize for shape, dtype in outputs)
    size += sum(value.size * value.dtype.itemsize for value in inputs)
    return pl.pallas_call(
        body,
        out_shape=[kind(shape, dtype) for shape, dtype in outputs],
        in_specs=[source] * len(inputs),
        out_specs=[IN_VMEM] * len(outputs),
        scratch_shapes=scratch,
        compiler_params=pltpu.CompilerParams(vmem_limit_bytes=16 * 1024 * 1024),
        cost_estimate=pl.CostEstimate(flops=flops, bytes_accessed=size, transcendentals=0),
    )(*inputs)


def per_device(stored, cotangent, weight, local_edges, halo_edges, pattern, pick):
    sections, rows, columns = (lax.axis_size(name) for name in AXES)
    here = lax.axis_index("pipe")
    lower = sections // 2
    upper = sections - lower
    top = sections - 1

    def flat(section, x, y):
        return (section * rows + x) * columns + y

    def to_sections(value, moves):
        pairs = [
            (flat(source, x, y), flat(target, x, y))
            for source, target in moves
            for x in range(rows)
            for y in range(columns)
        ]
        return lax.ppermute(value, AXES, pairs)

    batches, nodes, width = stored.shape[1], stored.shape[4], stored.shape[5]
    blocks, block = local_edges.shape[3], local_edges.shape[5]
    total_rows = batches * nodes
    features = stored.reshape(total_rows, width)
    matrix = weight[0]
    picks = pick[:, 0, 0]

    phases, routes = [], []
    for axis, base, count in (("tx", 0, rows), ("ty", 2, columns)):
        for first, couples in swap_phases(count):
            phases.append((axis, base, first))
            route = {}
            for lead in {0, top}:
                route[lead] = [
                    (
                        flat(lead, *((a, other) if axis == "tx" else (other, a))),
                        flat(lead, *((b, other) if axis == "tx" else (other, b))),
                    )
                    for low, high in couples
                    for a, b in ((low, high), (high, low))
                    for other in range(columns if axis == "tx" else rows)
                ]
            routes.append(route)
    phases = tuple(phases)
    sent = [((batches, block, width), BF16)] * len(phases)
    whole = ((total_rows, width), BF16)
    mix_rows = (blocks + len(phases)) * block
    cost = 2 * total_rows * width * (width + len(phases) * block)

    def exchange(outs, lead):
        return [lax.ppermute(out, AXES, route[lead]) for out, route in zip(outs, routes)]

    def inner(upstream, message, mixing):
        return call(
            inner_kernel, [upstream, message, mixing], [((total_rows, width), F32)],
            2 * total_rows * width * nodes,
        )[0]

    given = cotangent.reshape(total_rows, width)
    operands = [
        features, matrix, given, pattern[:, 0, 0], picks, local_edges[:, 0, 0], halo_edges[:, 0, 0]
    ]
    layer, mixing, mask, grad, message, *outs = call(
        functools.partial(first_kernel, phases),
        [pltpu.with_memory_space_constraint(value, pltpu.HBM) for value in operands],
        [
            ((2, total_rows, width), BF16), ((batches, mix_rows, nodes), BF16),
            ((batches * blocks * len(phases), 1, width), F32), whole, whole,
        ] + sent,
        cost + 2 * total_rows * width * width,
        source=pl.BlockSpec(memory_space=pltpu.HBM),
        scratch=[
            (pltpu.VMEM if value.dtype == BF16 else pltpu.SMEM)(value.shape, value.dtype)
            for value in operands
        ] + [pltpu.SemaphoreType.DMA((len(operands),))],
    )
    arrived = exchange(outs, top)
    total = inner(given, message, mixing)
    turned = call(turn_kernel, [features], [((width, total_rows), BF16)], 0)[0]

    layers = [layer]
    for step in range(1, upper):
        moves = [(top - step, top)] + ([(step, 0)] if step < lower else [])
        layers.append(to_sections(layer, moves))

    def fetch_home(values):
        got = None
        for step in range(1, upper):
            moves = [(top, top - step)]
            value = values[top - step]
            if step < lower:
                moves.append((0, step))
                value = call(
                    functools.partial(choose_kernel, top), [value, values[step]], [whole], 0
                )[0]
            new = to_sections(value, moves)
            takes = here == top - step
            if step < lower:
                takes = takes | (here == step)
            got = new if step == 1 else jnp.where(takes, new, got)
        return got

    count = len(phases)
    grads, results = {top: grad}, {}
    for section in reversed(range(top)):
        lead = top if section >= lower else 0
        steps = top - section if section >= lower else section
        layer_here = layers[steps]
        if section == lower - 1:
            upstream = call(close_kernel, [mask, total, *arrived], [whole], 0)[0]
            results[section + 1] = upstream
            upstream = to_sections(upstream, [(top, 0)])
            grad, message, *outs = call(
                step_kernel, [layer_here, mixing, upstream], [whole, whole] + sent, cost
            )
        elif section > 0:
            upstream, grad, message, *outs = call(
                functools.partial(close_step_kernel, count),
                [mask, total, *arrived, layer_here, mixing],
                [whole, whole, whole] + sent, cost,
            )
            results[section + 1] = upstream
        else:
            upstream, product, total, *outs = call(
                functools.partial(bottom_kernel, count, top),
                [mask, total, *arrived, turned, grads[top], fetch_home(grads), layer_here, mixing],
                [whole, ((width, width), BF16), ((total_rows, width), F32)] + sent,
                cost + 2 * total_rows * width * (width + nodes),
                scratch=[pltpu.VMEM(*whole), pltpu.VMEM(*whole)],
            )
            results[1] = upstream
        arrived = exchange(outs, lead)
        if section > 0:
            grads[section] = grad
            total = inner(upstream, message, mixing)

    tiles = rows * columns
    pieces = lax.all_to_all(
        product.reshape(tiles, width // tiles, width), ("tx", "ty"), 0, 0, tiled=True
    )
    result = call(
        functools.partial(last_kernel, top),
        [mask, total, *arrived, results[top], fetch_home(results)], [whole], 0,
        jax.ShapeDtypeStruct,
    )[0]
    scale = 1.0 / math.sqrt(total_rows * tiles)
    summed = call(
        functools.partial(reduce_kernel, scale), [pieces], [((width // tiles, width), F32)], 0,
        jax.ShapeDtypeStruct,
    )[0]
    return (summed[None], result.reshape(1, batches, 1, 1, nodes, width))


def solution(mesh):
    in_specs = (
        P("pipe", None, "tx", "ty", None, None),
        P(None, "tx", "ty", None, None),
        P("pipe", None, None),
        P(None, "tx", "ty", None, None, None, None),
        P(None, "tx", "ty", None, None, None, None),
        P(None, "tx", "ty", None, None),
        P(None, "tx", "ty", None),
    )
    out_specs = (P("pipe", ("tx", "ty"), None), P("pipe", None, "tx", "ty", None, None))
    return jax.shard_map(
        per_device, mesh=mesh, in_specs=in_specs, out_specs=out_specs, check_vma=False
    )
```

```python
import functools
import math

import jax
import jax.numpy as jnp
from jax import lax
from jax.experimental import pallas as pl
from jax.experimental.pallas import tpu as pltpu
from jax.sharding import PartitionSpec as P

AXES = ("pipe", "tx", "ty")
F32, BF16 = jnp.float32, jnp.bfloat16
IN_VMEM = pl.BlockSpec(memory_space=pltpu.VMEM)


def silu_slope(value):
    sigma = jax.nn.sigmoid(value)
    return sigma * (1.0 + value * (1.0 - sigma))


def swap_phases(count):
    phases = []
    for first in (0, 1):
        pairs = [(low, low + 1) for low in range(first, count - 1, 2)]
        if pairs:
            phases.append((first, pairs))
    return phases


def side(phase):
    axis, base, first = phase
    return base, lax.rem(lax.axis_index(axis) + first, 2) == 0


def rows_dot(left, right):
    return lax.dot_general(left, right, (((1,), (0,)), ((), ())), preferred_element_type=F32)


def back_dot(left, right):
    return lax.dot_general(left, right, (((1,), (1,)), ((), ())), preferred_element_type=F32)


def send_blocks(grads, matrix, mixing_ref, message_ref, out_refs):
    batches, outgoing, nodes = mixing_ref.shape
    block = out_refs[0].shape[1]
    messages = back_dot(grads, matrix).astype(BF16)
    message_ref[...] = messages
    first = outgoing - block * len(out_refs)
    for batch in range(batches):
        mixed = rows_dot(
            mixing_ref[batch, first:, :], messages[batch * nodes : (batch + 1) * nodes]
        ).astype(BF16)
        for index, out_ref in enumerate(out_refs):
            out_ref[batch] = mixed[index * block : (index + 1) * block]


def first_kernel(phases, *refs):
    sources, refs = refs[:7], refs[7:]
    layer_ref, mixing_ref, mask_ref, grad_ref, message_ref = refs[:5]
    out_refs = refs[5 : 5 + len(phases)]
    held, sems = refs[5 + len(phases) : -1], refs[-1]
    copies = [
        pltpu.make_async_copy(source, target, sems.at[index])
        for index, (source, target) in enumerate(zip(sources, held))
    ]
    for copy in copies:
        copy.start()
    features_ref, matrix_ref, given_ref, pattern_ref, pick_ref, local_ref, halo_ref = held
    batches, blocks, _, block, _ = local_ref.shape
    sides = [side(phase) for phase in phases]
    copies[0].wait()
    copies[1].wait()
    pre_activation = rows_dot(features_ref[...], matrix_ref[...])
    slope = silu_slope(pre_activation).astype(BF16)
    layer_ref[0] = slope
    layer_ref[1] = matrix_ref[...]
    copies[2].wait()
    grads = (given_ref[...].astype(F32) * slope.astype(F32)).astype(BF16)
    grad_ref[...] = grads
    for copy in copies[3:]:
        copy.wait()
    for batch in range(batches):
        for source in range(blocks):
            columns = slice(source * block, (source + 1) * block)
            for target in range(blocks):
                present = pattern_ref[batch, source, target].astype(F32)
                edges = local_ref[batch, source, target].astype(F32) * present
                mixing_ref[batch, target * block : (target + 1) * block, columns] = edges.T.astype(BF16)
            for index, (base, is_low) in enumerate(sides):
                slot = jnp.where(is_low, base + 1, base)
                present = pattern_ref[batch, source, blocks + slot].astype(F32)
                edges = halo_ref[batch, slot, source].astype(F32) * present
                start = (blocks + index) * block
                mixing_ref[batch, start : start + block, columns] = edges.T.astype(BF16)
        for index, (base, is_low) in enumerate(sides):
            chosen = pick_ref[batch, jnp.where(is_low, base, base + 1)]
            for target in range(blocks):
                here = (chosen == target).astype(F32)
                entry = (batch * blocks + target) * len(sides) + index
                mask_ref[entry] = jnp.full(mask_ref.shape[1:], here, F32)
    send_blocks(grads, matrix_ref[...], mixing_ref, message_ref, out_refs)


def inner_kernel(upstream_ref, message_ref, mixing_ref, total_ref):
    batches, _, nodes = mixing_ref.shape
    for batch in range(batches):
        rows = slice(batch * nodes, (batch + 1) * nodes)
        total_ref[rows] = upstream_ref[rows].astype(F32) + rows_dot(
            mixing_ref[batch, :nodes, :], message_ref[rows]
        )


def turn_kernel(features_ref, turned_ref):
    turned_ref[...] = features_ref[...].T


def choose_kernel(top, top_ref, other_ref, chosen_ref):
    at_top = lax.axis_index("pipe") == top

    @pl.when(at_top)
    def _():
        chosen_ref[...] = top_ref[...]

    @pl.when(jnp.logical_not(at_top))
    def _():
        chosen_ref[...] = other_ref[...]


def close_blocks(mask_ref, total_ref, arrived_refs, result_ref):
    batches, block, _ = arrived_refs[0].shape
    count = len(arrived_refs)
    for batch in range(batches):
        arrived = [ref[batch].astype(F32) for ref in arrived_refs]
        for target in range(total_ref.shape[0] // batches // block):
            order = batch * (total_ref.shape[0] // batches // block) + target
            rows = slice(order * block, (order + 1) * block)
            value = total_ref[rows]
            for index in range(count):
                value = value + arrived[index] * mask_ref[order * count + index]
            result_ref[rows] = value.astype(BF16)


def close_kernel(mask_ref, total_ref, *refs):
    close_blocks(mask_ref, total_ref, refs[:-1], refs[-1])


def last_kernel(top, count, scale, mask_ref, total_ref, *refs):
    arrived_refs = refs[:count]
    top_ref, got_ref = refs[count : count + 2]
    result_ref = refs[-1]
    here = lax.axis_index("pipe")
    if scale is not None:
        kept_ref, piece_ref, result_ref, sum_ref = refs[count + 2 :]
        sum_ref[...] = (kept_ref[...] + piece_ref[...].astype(F32)) * scale

    @pl.when(here == 0)
    def _():
        close_blocks(mask_ref, total_ref, arrived_refs, result_ref)

    @pl.when(here == top)
    def _():
        result_ref[...] = top_ref[...]

    @pl.when((here != 0) & (here != top))
    def _():
        result_ref[...] = got_ref[...]


def step_kernel(layer_ref, mixing_ref, upstream_ref, grad_ref, message_ref, *out_refs):
    grads = (upstream_ref[...].astype(F32) * layer_ref[0].astype(F32)).astype(BF16)
    grad_ref[...] = grads
    send_blocks(grads, layer_ref[1], mixing_ref, message_ref, out_refs)


def close_step_kernel(count, mask_ref, total_ref, *refs):
    layer_ref, mixing_ref, result_ref, grad_ref, message_ref, *out_refs = refs[count:]
    close_blocks(mask_ref, total_ref, refs[:count], result_ref)
    step_kernel(layer_ref, mixing_ref, result_ref, grad_ref, message_ref, *out_refs)


def weight_product(top, turned_ref, grad_ref, top_ref, got_ref, product_ref):
    here = lax.axis_index("pipe")

    def product(ref):
        product_ref[...] = rows_dot(turned_ref[...], ref[...])

    @pl.when(here == 0)
    def _():
        product(grad_ref)

    @pl.when(here == top)
    def _():
        product(top_ref)

    @pl.when((here != 0) & (here != top))
    def _():
        product(got_ref)


def split_halves(step, product_ref, sent_ref, kept_ref):
    axis, distance, groups = step
    size = kept_ref.shape[0] // groups
    place = lax.rem(lax.axis_index(axis) // distance, 2)
    for group in range(groups):
        start = 2 * group * size
        rows = slice(group * size, (group + 1) * size)
        kept = pl.ds(pl.multiple_of(start + place * size, size), size)
        sent = pl.ds(pl.multiple_of(start + (1 - place) * size, size), size)
        kept_ref[rows] = product_ref[kept]
        sent_ref[rows] = product_ref[sent].astype(BF16)


def halve_kernel(step, kept_ref, got_ref, sent_ref, next_ref, sum_ref):
    sum_ref[...] = kept_ref[...] + got_ref[...].astype(F32)
    split_halves(step, sum_ref, sent_ref, next_ref)


def bottom_kernel(count, top, step, mask_ref, total_ref, *refs):
    turned_ref, top_ref, got_ref, layer_ref, mixing_ref = refs[count : count + 5]
    result_ref, next_ref = refs[count + 5 : count + 7]
    out_refs = refs[count + 7 : 2 * count + 7]
    grad_ref, message_ref = refs[-2:]
    close_step_kernel(
        count, mask_ref, total_ref, *refs[:count], layer_ref, mixing_ref,
        result_ref, grad_ref, message_ref, *out_refs
    )
    if step is None:
        weight_product(top, turned_ref, grad_ref, top_ref, got_ref, refs[2 * count + 7])
    else:
        sent_ref, kept_ref, product_ref = refs[2 * count + 7 : -2]
        weight_product(top, turned_ref, grad_ref, top_ref, got_ref, product_ref)
        split_halves(step, product_ref, sent_ref, kept_ref)
    inner_kernel(result_ref, message_ref, mixing_ref, next_ref)


def call(body, inputs, outputs, flops, kind=pltpu.VMEM, source=IN_VMEM, scratch=()):
    size = sum(math.prod(shape) * jnp.dtype(dtype).itemsize for shape, dtype in outputs)
    size += sum(value.size * value.dtype.itemsize for value in inputs)
    return pl.pallas_call(
        body,
        out_shape=[kind(shape, dtype) for shape, dtype in outputs],
        in_specs=[source] * len(inputs),
        out_specs=[IN_VMEM] * len(outputs),
        scratch_shapes=scratch,
        compiler_params=pltpu.CompilerParams(vmem_limit_bytes=16 * 1024 * 1024),
        cost_estimate=pl.CostEstimate(flops=flops, bytes_accessed=size, transcendentals=0),
    )(*inputs)


def per_device(stored, cotangent, weight, local_edges, halo_edges, pattern, pick):
    sections, rows, columns = (lax.axis_size(name) for name in AXES)
    here = lax.axis_index("pipe")
    lower = sections // 2
    upper = sections - lower
    top = sections - 1

    def flat(section, x, y):
        return (section * rows + x) * columns + y

    def to_sections(value, moves):
        pairs = [
            (flat(source, x, y), flat(target, x, y))
            for source, target in moves
            for x in range(rows)
            for y in range(columns)
        ]
        return lax.ppermute(value, AXES, pairs)

    batches, nodes, width = stored.shape[1], stored.shape[4], stored.shape[5]
    blocks, block = local_edges.shape[3], local_edges.shape[5]
    total_rows = batches * nodes
    features = stored.reshape(total_rows, width)
    matrix = weight[0]
    picks = pick[:, 0, 0]

    phases, routes = [], []
    for axis, base, count in (("tx", 0, rows), ("ty", 2, columns)):
        for first, couples in swap_phases(count):
            phases.append((axis, base, first))
            route = {}
            for lead in {0, top}:
                route[lead] = [
                    (
                        flat(lead, *((a, other) if axis == "tx" else (other, a))),
                        flat(lead, *((b, other) if axis == "tx" else (other, b))),
                    )
                    for low, high in couples
                    for a, b in ((low, high), (high, low))
                    for other in range(columns if axis == "tx" else rows)
                ]
            routes.append(route)
    phases = tuple(phases)
    splits, left = [], rows * columns
    if left & (left - 1) == 0 and width // left % 16 == 0:
        for axis, count, other in (("ty", columns, rows), ("tx", rows, 1)):
            distance = count // 2
            while distance > 0:
                pairs = [
                    (flat(p, x, y), flat(p, x, y ^ distance) if axis == "ty" else flat(p, x ^ distance, y))
                    for p in range(sections)
                    for x in range(rows)
                    for y in range(columns)
                ]
                splits.append(((axis, distance, other), pairs))
                distance //= 2
    sent = [((batches, block, width), BF16)] * len(phases)
    whole = ((total_rows, width), BF16)
    mix_rows = (blocks + len(phases)) * block
    cost = 2 * total_rows * width * (width + len(phases) * block)

    def exchange(outs, lead):
        return [lax.ppermute(out, AXES, route[lead]) for out, route in zip(outs, routes)]

    def inner(upstream, message, mixing):
        return call(
            inner_kernel, [upstream, message, mixing], [((total_rows, width), F32)],
            2 * total_rows * width * nodes,
        )[0]

    given = cotangent.reshape(total_rows, width)
    operands = [
        features, matrix, given, pattern[:, 0, 0], picks, local_edges[:, 0, 0], halo_edges[:, 0, 0]
    ]
    layer, mixing, mask, grad, message, *outs = call(
        functools.partial(first_kernel, phases),
        [pltpu.with_memory_space_constraint(value, pltpu.HBM) for value in operands],
        [
            ((2, total_rows, width), BF16), ((batches, mix_rows, nodes), BF16),
            ((batches * blocks * len(phases), 1, width), F32), whole, whole,
        ] + sent,
        cost + 2 * total_rows * width * width,
        source=pl.BlockSpec(memory_space=pltpu.HBM),
        scratch=[
            (pltpu.VMEM if value.dtype == BF16 else pltpu.SMEM)(value.shape, value.dtype)
            for value in operands
        ] + [pltpu.SemaphoreType.DMA((len(operands),))],
    )
    arrived = exchange(outs, top)
    total = inner(given, message, mixing)
    turned = call(turn_kernel, [features], [((width, total_rows), BF16)], 0)[0]

    layers = [layer]
    for step in range(1, upper):
        moves = [(top - step, top)] + ([(step, 0)] if step < lower else [])
        layers.append(to_sections(layer, moves))

    def fetch_home(values):
        got = None
        for step in range(1, upper):
            moves = [(top, top - step)]
            value = values[top - step]
            if step < lower:
                moves.append((0, step))
                value = call(
                    functools.partial(choose_kernel, top), [value, values[step]], [whole], 0
                )[0]
            new = to_sections(value, moves)
            takes = here == top - step
            if step < lower:
                takes = takes | (here == step)
            got = new if step == 1 else jnp.where(takes, new, got)
        return got

    count = len(phases)
    grads, results = {top: grad}, {}
    for section in reversed(range(top)):
        lead = top if section >= lower else 0
        steps = top - section if section >= lower else section
        layer_here = layers[steps]
        if section == lower - 1:
            upstream = call(close_kernel, [mask, total, *arrived], [whole], 0)[0]
            results[section + 1] = upstream
            upstream = to_sections(upstream, [(top, 0)])
            grad, message, *outs = call(
                step_kernel, [layer_here, mixing, upstream], [whole, whole] + sent, cost
            )
        elif section > 0:
            upstream, grad, message, *outs = call(
                functools.partial(close_step_kernel, count),
                [mask, total, *arrived, layer_here, mixing],
                [whole, whole, whole] + sent, cost,
            )
            results[section + 1] = upstream
        else:
            product = ((width, width), F32)
            halves = [((width // 2, width), BF16), ((width // 2, width), F32)] if splits else [product]
            upstream, total, *outs = call(
                functools.partial(bottom_kernel, count, top, splits[0][0] if splits else None),
                [mask, total, *arrived, turned, grads[top], fetch_home(grads), layer_here, mixing],
                [whole, ((total_rows, width), F32)] + sent + halves,
                cost + 2 * total_rows * width * (width + nodes),
                scratch=[pltpu.VMEM(*product)] * len(splits[:1]) + [pltpu.VMEM(*whole)] * 2,
            )
            outs, pieces = outs[:count], outs[count:]
            results[1] = upstream
        arrived = exchange(outs, lead)
        if section > 0:
            grads[section] = grad
            total = inner(upstream, message, mixing)

    scale = 1.0 / math.sqrt(total_rows * rows * columns)
    if splits:
        parcel, kept = pieces
        for (_, pairs), following in zip(splits, splits[1:]):
            got = lax.ppermute(parcel, AXES, pairs)
            half = (kept.shape[0] // 2, width)
            parcel, kept = call(
                functools.partial(halve_kernel, following[0]), [kept, got],
                [(half, BF16), (half, F32)], 0, scratch=[pltpu.VMEM(kept.shape, F32)],
            )
        got = lax.ppermute(parcel, AXES, splits[-1][1])
        result, summed = call(
            functools.partial(last_kernel, top, count, scale),
            [mask, total, *arrived, results[top], fetch_home(results), kept, got],
            [whole, (kept.shape, F32)], 0, jax.ShapeDtypeStruct,
        )
    else:
        summed = scale * lax.psum_scatter(pieces[0], ("tx", "ty"), scatter_dimension=0, tiled=True)
        result = call(
            functools.partial(last_kernel, top, count, None),
            [mask, total, *arrived, results[top], fetch_home(results)], [whole], 0,
            jax.ShapeDtypeStruct,
        )[0]
    return (summed[None], result.reshape(1, batches, 1, 1, nodes, width))


def solution(mesh):
    in_specs = (
        P("pipe", None, "tx", "ty", None, None),
        P(None, "tx", "ty", None, None),
        P("pipe", None, None),
        P(None, "tx", "ty", None, None, None, None),
        P(None, "tx", "ty", None, None, None, None),
        P(None, "tx", "ty", None, None),
        P(None, "tx", "ty", None),
    )
    out_specs = (P("pipe", ("tx", "ty"), None), P("pipe", None, "tx", "ty", None, None))
    return jax.shard_map(
        per_device, mesh=mesh, in_specs=in_specs, out_specs=out_specs, check_vma=False
    )
```

```python
import functools
import math

import jax
import jax.numpy as jnp
from jax import lax
from jax.experimental import pallas as pl
from jax.experimental.pallas import tpu as pltpu
from jax.sharding import PartitionSpec as P

AXES = ("pipe", "tx", "ty")
F32, BF16 = jnp.float32, jnp.bfloat16
IN_VMEM = pl.BlockSpec(memory_space=pltpu.VMEM)


def silu_slope(value):
    sigma = jax.nn.sigmoid(value)
    return sigma * (1.0 + value * (1.0 - sigma))


def swap_phases(count):
    phases = []
    for first in (0, 1):
        pairs = [(low, low + 1) for low in range(first, count - 1, 2)]
        if pairs:
            phases.append((first, pairs))
    return phases


def completed(pairs, devices):
    pairs = list(pairs)
    silent = set(range(devices)) - {source for source, _ in pairs}
    unfed = set(range(devices)) - {target for _, target in pairs}
    back = [(target, source) for source, target in pairs if target in silent and source in unfed]
    pairs += back
    silent -= {source for source, _ in back}
    unfed -= {target for _, target in back}
    return pairs + [(device, device) for device in sorted(silent & unfed)]


def side(phase):
    axis, base, first, count = phase
    place = lax.axis_index(axis)
    is_low = lax.rem(place + first, 2) == 0
    return base, is_low, jnp.where(is_low, place < count - 1, place > 0)


def rows_dot(left, right):
    return lax.dot_general(left, right, (((1,), (0,)), ((), ())), preferred_element_type=F32)


def back_dot(left, right):
    return lax.dot_general(left, right, (((1,), (1,)), ((), ())), preferred_element_type=F32)


def send_blocks(grads, matrix, mixing_ref, message_ref, out_refs):
    batches, outgoing, nodes = mixing_ref.shape
    block = out_refs[0].shape[1]
    messages = back_dot(grads, matrix).astype(BF16)
    message_ref[...] = messages
    first = outgoing - block * len(out_refs)
    for batch in range(batches):
        mixed = rows_dot(
            mixing_ref[batch, first:, :], messages[batch * nodes : (batch + 1) * nodes]
        ).astype(BF16)
        for index, out_ref in enumerate(out_refs):
            out_ref[batch] = mixed[index * block : (index + 1) * block]


def first_kernel(phases, *refs):
    sources, refs = refs[:7], refs[7:]
    layer_ref, mixing_ref, mask_ref, grad_ref, message_ref = refs[:5]
    out_refs = refs[5 : 5 + len(phases)]
    held, sems = refs[5 + len(phases) : -1], refs[-1]
    copies = [
        pltpu.make_async_copy(source, target, sems.at[index])
        for index, (source, target) in enumerate(zip(sources, held))
    ]
    for copy in copies:
        copy.start()
    features_ref, matrix_ref, given_ref, pattern_ref, pick_ref, local_ref, halo_ref = held
    batches, blocks, _, block, _ = local_ref.shape
    sides = [side(phase) for phase in phases]
    copies[0].wait()
    copies[1].wait()
    pre_activation = rows_dot(features_ref[...], matrix_ref[...])
    slope = silu_slope(pre_activation).astype(BF16)
    layer_ref[0] = slope
    layer_ref[1] = matrix_ref[...]
    copies[2].wait()
    grads = (given_ref[...].astype(F32) * slope.astype(F32)).astype(BF16)
    grad_ref[...] = grads
    for copy in copies[3:]:
        copy.wait()
    for batch in range(batches):
        for source in range(blocks):
            columns = slice(source * block, (source + 1) * block)
            for target in range(blocks):
                present = pattern_ref[batch, source, target].astype(F32)
                edges = local_ref[batch, source, target].astype(F32) * present
                mixing_ref[batch, target * block : (target + 1) * block, columns] = edges.T.astype(BF16)
            for index, (base, is_low, _) in enumerate(sides):
                slot = jnp.where(is_low, base + 1, base)
                present = pattern_ref[batch, source, blocks + slot].astype(F32)
                edges = halo_ref[batch, slot, source].astype(F32) * present
                start = (blocks + index) * block
                mixing_ref[batch, start : start + block, columns] = edges.T.astype(BF16)
        for index, (base, is_low, paired) in enumerate(sides):
            chosen = pick_ref[batch, jnp.where(is_low, base, base + 1)]
            for target in range(blocks):
                here = ((chosen == target) & paired).astype(F32)
                entry = (batch * blocks + target) * len(sides) + index
                mask_ref[entry] = jnp.full(mask_ref.shape[1:], here, F32)
    send_blocks(grads, matrix_ref[...], mixing_ref, message_ref, out_refs)


def inner_kernel(upstream_ref, message_ref, mixing_ref, total_ref):
    batches, _, nodes = mixing_ref.shape
    for batch in range(batches):
        rows = slice(batch * nodes, (batch + 1) * nodes)
        total_ref[rows] = upstream_ref[rows].astype(F32) + rows_dot(
            mixing_ref[batch, :nodes, :], message_ref[rows]
        )


def turn_kernel(features_ref, turned_ref):
    turned_ref[...] = features_ref[...].T


def choose_kernel(top, top_ref, other_ref, chosen_ref):
    at_top = lax.axis_index("pipe") == top

    @pl.when(at_top)
    def _():
        chosen_ref[...] = top_ref[...]

    @pl.when(jnp.logical_not(at_top))
    def _():
        chosen_ref[...] = other_ref[...]


def close_blocks(mask_ref, total_ref, arrived_refs, result_ref):
    batches, block, _ = arrived_refs[0].shape
    count = len(arrived_refs)
    for batch in range(batches):
        arrived = [ref[batch].astype(F32) for ref in arrived_refs]
        for target in range(total_ref.shape[0] // batches // block):
            order = batch * (total_ref.shape[0] // batches // block) + target
            rows = slice(order * block, (order + 1) * block)
            value = total_ref[rows]
            for index in range(count):
                value = value + arrived[index] * mask_ref[order * count + index]
            result_ref[rows] = value.astype(BF16)


def close_kernel(mask_ref, total_ref, *refs):
    close_blocks(mask_ref, total_ref, refs[:-1], refs[-1])


def last_kernel(top, count, scale, mask_ref, total_ref, *refs):
    arrived_refs = refs[:count]
    top_ref, got_ref = refs[count : count + 2]
    result_ref = refs[-1]
    here = lax.axis_index("pipe")
    if scale is not None:
        kept_ref, piece_ref, result_ref, sum_ref = refs[count + 2 :]
        sum_ref[...] = (kept_ref[...] + piece_ref[...].astype(F32)) * scale

    @pl.when(here == 0)
    def _():
        close_blocks(mask_ref, total_ref, arrived_refs, result_ref)

    @pl.when(here == top)
    def _():
        result_ref[...] = top_ref[...]

    @pl.when((here != 0) & (here != top))
    def _():
        result_ref[...] = got_ref[...]


def step_kernel(layer_ref, mixing_ref, upstream_ref, grad_ref, message_ref, *out_refs):
    grads = (upstream_ref[...].astype(F32) * layer_ref[0].astype(F32)).astype(BF16)
    grad_ref[...] = grads
    send_blocks(grads, layer_ref[1], mixing_ref, message_ref, out_refs)


def close_step_kernel(count, mask_ref, total_ref, *refs):
    layer_ref, mixing_ref, result_ref, grad_ref, message_ref, *out_refs = refs[count:]
    close_blocks(mask_ref, total_ref, refs[:count], result_ref)
    step_kernel(layer_ref, mixing_ref, result_ref, grad_ref, message_ref, *out_refs)


def weight_product(top, turned_ref, grad_ref, top_ref, got_ref, product_ref):
    here = lax.axis_index("pipe")

    def product(ref):
        product_ref[...] = rows_dot(turned_ref[...], ref[...])

    @pl.when(here == 0)
    def _():
        product(grad_ref)

    @pl.when(here == top)
    def _():
        product(top_ref)

    @pl.when((here != 0) & (here != top))
    def _():
        product(got_ref)


def split_halves(step, product_ref, sent_ref, kept_ref):
    axis, distance, groups = step
    size = kept_ref.shape[0] // groups
    place = lax.rem(lax.axis_index(axis) // distance, 2)
    for group in range(groups):
        start = 2 * group * size
        rows = slice(group * size, (group + 1) * size)
        kept = pl.ds(pl.multiple_of(start + place * size, size), size)
        sent = pl.ds(pl.multiple_of(start + (1 - place) * size, size), size)
        kept_ref[rows] = product_ref[kept]
        sent_ref[rows] = product_ref[sent].astype(BF16)


def halve_kernel(step, kept_ref, got_ref, sent_ref, next_ref, sum_ref):
    sum_ref[...] = kept_ref[...] + got_ref[...].astype(F32)
    split_halves(step, sum_ref, sent_ref, next_ref)


def bottom_kernel(count, top, step, mask_ref, total_ref, *refs):
    turned_ref, top_ref, got_ref, layer_ref, mixing_ref = refs[count : count + 5]
    result_ref, next_ref = refs[count + 5 : count + 7]
    out_refs = refs[count + 7 : 2 * count + 7]
    grad_ref, message_ref = refs[-2:]
    close_step_kernel(
        count, mask_ref, total_ref, *refs[:count], layer_ref, mixing_ref,
        result_ref, grad_ref, message_ref, *out_refs
    )
    if step is None:
        weight_product(top, turned_ref, grad_ref, top_ref, got_ref, refs[2 * count + 7])
    else:
        sent_ref, kept_ref, product_ref = refs[2 * count + 7 : -2]
        weight_product(top, turned_ref, grad_ref, top_ref, got_ref, product_ref)
        split_halves(step, product_ref, sent_ref, kept_ref)
    inner_kernel(result_ref, message_ref, mixing_ref, next_ref)


def call(body, inputs, outputs, flops, kind=pltpu.VMEM, source=IN_VMEM, scratch=()):
    size = sum(math.prod(shape) * jnp.dtype(dtype).itemsize for shape, dtype in outputs)
    size += sum(value.size * value.dtype.itemsize for value in inputs)
    return pl.pallas_call(
        body,
        out_shape=[kind(shape, dtype) for shape, dtype in outputs],
        in_specs=[source] * len(inputs),
        out_specs=[IN_VMEM] * len(outputs),
        scratch_shapes=scratch,
        compiler_params=pltpu.CompilerParams(vmem_limit_bytes=16 * 1024 * 1024),
        cost_estimate=pl.CostEstimate(flops=flops, bytes_accessed=size, transcendentals=0),
    )(*inputs)


def per_device(stored, cotangent, weight, local_edges, halo_edges, pattern, pick):
    sections, rows, columns = (lax.axis_size(name) for name in AXES)
    here = lax.axis_index("pipe")
    devices = sections * rows * columns
    lower = sections // 2
    upper = sections - lower
    top = sections - 1

    def flat(section, x, y):
        return (section * rows + x) * columns + y

    def to_sections(value, moves):
        pairs = [
            (flat(source, x, y), flat(target, x, y))
            for source, target in moves
            for x in range(rows)
            for y in range(columns)
        ]
        return lax.ppermute(value, AXES, completed(pairs, devices))

    batches, nodes, width = stored.shape[1], stored.shape[4], stored.shape[5]
    blocks, block = local_edges.shape[3], local_edges.shape[5]
    total_rows = batches * nodes
    features = stored.reshape(total_rows, width)
    matrix = weight[0]
    picks = pick[:, 0, 0]

    phases, routes = [], []
    for axis, base, count in (("tx", 0, rows), ("ty", 2, columns)):
        for first, couples in swap_phases(count):
            phases.append((axis, base, first, count))
            route = {}
            for lead in {0, top}:
                route[lead] = completed([
                    (
                        flat(lead, *((a, other) if axis == "tx" else (other, a))),
                        flat(lead, *((b, other) if axis == "tx" else (other, b))),
                    )
                    for low, high in couples
                    for a, b in ((low, high), (high, low))
                    for other in range(columns if axis == "tx" else rows)
                ], devices)
            routes.append(route)
    phases = tuple(phases)
    splits, left = [], rows * columns
    if left & (left - 1) == 0 and width // left % 16 == 0:
        for axis, count, other in (("ty", columns, rows), ("tx", rows, 1)):
            distance = count // 2
            while distance > 0:
                pairs = [
                    (flat(p, x, y), flat(p, x, y ^ distance) if axis == "ty" else flat(p, x ^ distance, y))
                    for p in range(sections)
                    for x in range(rows)
                    for y in range(columns)
                ]
                splits.append(((axis, distance, other), pairs))
                distance //= 2
    sent = [((batches, block, width), BF16)] * len(phases)
    whole = ((total_rows, width), BF16)
    mix_rows = (blocks + len(phases)) * block
    cost = 2 * total_rows * width * (width + len(phases) * block)

    def exchange(outs, lead):
        return [lax.ppermute(out, AXES, route[lead]) for out, route in zip(outs, routes)]

    def inner(upstream, message, mixing):
        return call(
            inner_kernel, [upstream, message, mixing], [((total_rows, width), F32)],
            2 * total_rows * width * nodes,
        )[0]

    given = cotangent.reshape(total_rows, width)
    operands = [
        features, matrix, given, pattern[:, 0, 0], picks, local_edges[:, 0, 0], halo_edges[:, 0, 0]
    ]
    layer, mixing, mask, grad, message, *outs = call(
        functools.partial(first_kernel, phases),
        [pltpu.with_memory_space_constraint(value, pltpu.HBM) for value in operands],
        [
            ((2, total_rows, width), BF16), ((batches, mix_rows, nodes), BF16),
            ((batches * blocks * len(phases), 1, width), F32), whole, whole,
        ] + sent,
        cost + 2 * total_rows * width * width,
        source=pl.BlockSpec(memory_space=pltpu.HBM),
        scratch=[
            (pltpu.VMEM if value.dtype == BF16 else pltpu.SMEM)(value.shape, value.dtype)
            for value in operands
        ] + [pltpu.SemaphoreType.DMA((len(operands),))],
    )
    arrived = exchange(outs, top)
    total = inner(given, message, mixing)
    turned = call(turn_kernel, [features], [((width, total_rows), BF16)], 0)[0]

    layers = [layer]
    for step in range(1, upper):
        moves = [(top - step, top)] + ([(step, 0)] if step < lower else [])
        layers.append(to_sections(layer, moves))

    def fetch_home(values):
        got = None
        for step in range(1, upper):
            moves = [(top, top - step)]
            value = values[top - step]
            if step < lower:
                moves.append((0, step))
                value = call(
                    functools.partial(choose_kernel, top), [value, values[step]], [whole], 0
                )[0]
            new = to_sections(value, moves)
            takes = here == top - step
            if step < lower:
                takes = takes | (here == step)
            got = new if step == 1 else jnp.where(takes, new, got)
        return got

    count = len(phases)
    grads, results = {top: grad}, {}
    for section in reversed(range(top)):
        lead = top if section >= lower else 0
        steps = top - section if section >= lower else section
        layer_here = layers[steps]
        if section == lower - 1:
            upstream = call(close_kernel, [mask, total, *arrived], [whole], 0)[0]
            results[section + 1] = upstream
            upstream = to_sections(upstream, [(top, 0)])
            grad, message, *outs = call(
                step_kernel, [layer_here, mixing, upstream], [whole, whole] + sent, cost
            )
        elif section > 0:
            upstream, grad, message, *outs = call(
                functools.partial(close_step_kernel, count),
                [mask, total, *arrived, layer_here, mixing],
                [whole, whole, whole] + sent, cost,
            )
            results[section + 1] = upstream
        else:
            product = ((width, width), F32)
            halves = [((width // 2, width), BF16), ((width // 2, width), F32)] if splits else [product]
            upstream, total, *outs = call(
                functools.partial(bottom_kernel, count, top, splits[0][0] if splits else None),
                [mask, total, *arrived, turned, grads[top], fetch_home(grads), layer_here, mixing],
                [whole, ((total_rows, width), F32)] + sent + halves,
                cost + 2 * total_rows * width * (width + nodes),
                scratch=[pltpu.VMEM(*product)] * len(splits[:1]) + [pltpu.VMEM(*whole)] * 2,
            )
            outs, pieces = outs[:count], outs[count:]
            results[1] = upstream
        arrived = exchange(outs, lead)
        if section > 0:
            grads[section] = grad
            total = inner(upstream, message, mixing)

    scale = 1.0 / math.sqrt(total_rows * rows * columns)
    if splits:
        parcel, kept = pieces
        for (_, pairs), following in zip(splits, splits[1:]):
            got = lax.ppermute(parcel, AXES, pairs)
            half = (kept.shape[0] // 2, width)
            parcel, kept = call(
                functools.partial(halve_kernel, following[0]), [kept, got],
                [(half, BF16), (half, F32)], 0, scratch=[pltpu.VMEM(kept.shape, F32)],
            )
        got = lax.ppermute(parcel, AXES, splits[-1][1])
        result, summed = call(
            functools.partial(last_kernel, top, count, scale),
            [mask, total, *arrived, results[top], fetch_home(results), kept, got],
            [whole, (kept.shape, F32)], 0, jax.ShapeDtypeStruct,
        )
    else:
        summed = scale * lax.psum_scatter(pieces[0], ("tx", "ty"), scatter_dimension=0, tiled=True)
        result = call(
            functools.partial(last_kernel, top, count, None),
            [mask, total, *arrived, results[top], fetch_home(results)], [whole], 0,
            jax.ShapeDtypeStruct,
        )[0]
    return (summed[None], result.reshape(1, batches, 1, 1, nodes, width))


def solution(mesh):
    in_specs = (
        P("pipe", None, "tx", "ty", None, None),
        P(None, "tx", "ty", None, None),
        P("pipe", None, None),
        P(None, "tx", "ty", None, None, None, None),
        P(None, "tx", "ty", None, None, None, None),
        P(None, "tx", "ty", None, None),
        P(None, "tx", "ty", None),
    )
    out_specs = (P("pipe", ("tx", "ty"), None), P("pipe", None, "tx", "ty", None, None))
    return jax.shard_map(
        per_device, mesh=mesh, in_specs=in_specs, out_specs=out_specs, check_vma=False
    )
```

```python
import functools
import math

import jax
import jax.numpy as jnp
from jax import lax
from jax.experimental import pallas as pl
from jax.experimental.pallas import tpu as pltpu
from jax.sharding import PartitionSpec as P

AXES = ("pipe", "tx", "ty")
F32, BF16 = jnp.float32, jnp.bfloat16
IN_VMEM = pl.BlockSpec(memory_space=pltpu.VMEM)


def silu_slope(value):
    sigma = jax.nn.sigmoid(value)
    return sigma * (1.0 + value * (1.0 - sigma))


def swap_phases(count):
    phases = []
    for first in (0, 1):
        pairs = [(low, low + 1) for low in range(first, count - 1, 2)]
        if pairs:
            phases.append((first, pairs))
    return phases


def side(phase):
    axis, base, first, count = phase
    place = lax.axis_index(axis)
    is_low = lax.rem(place + first, 2) == 0
    return base, is_low, jnp.where(is_low, place < count - 1, place > 0)


def rows_dot(left, right):
    return lax.dot_general(left, right, (((1,), (0,)), ((), ())), preferred_element_type=F32)


def back_dot(left, right):
    return lax.dot_general(left, right, (((1,), (1,)), ((), ())), preferred_element_type=F32)


def send_blocks(grads, matrix, mixing_ref, message_ref, out_refs):
    batches, outgoing, nodes = mixing_ref.shape
    block = out_refs[0].shape[1]
    messages = back_dot(grads, matrix).astype(BF16)
    message_ref[...] = messages
    first = outgoing - block * len(out_refs)
    for batch in range(batches):
        mixed = rows_dot(
            mixing_ref[batch, first:, :], messages[batch * nodes : (batch + 1) * nodes]
        ).astype(BF16)
        for index, out_ref in enumerate(out_refs):
            out_ref[batch] = mixed[index * block : (index + 1) * block]


def first_kernel(phases, *refs):
    sources, refs = refs[:7], refs[7:]
    layer_ref, mixing_ref, mask_ref, grad_ref, message_ref = refs[:5]
    out_refs = refs[5 : 5 + len(phases)]
    held, sems = refs[5 + len(phases) : -1], refs[-1]
    copies = [
        pltpu.make_async_copy(source, target, sems.at[index])
        for index, (source, target) in enumerate(zip(sources, held))
    ]
    for copy in copies:
        copy.start()
    features_ref, matrix_ref, given_ref, pattern_ref, pick_ref, local_ref, halo_ref = held
    batches, blocks, _, block, _ = local_ref.shape
    sides = [side(phase) for phase in phases]
    copies[0].wait()
    copies[1].wait()
    pre_activation = rows_dot(features_ref[...], matrix_ref[...])
    slope = silu_slope(pre_activation).astype(BF16)
    layer_ref[0] = slope
    layer_ref[1] = matrix_ref[...]
    copies[2].wait()
    grads = (given_ref[...].astype(F32) * slope.astype(F32)).astype(BF16)
    grad_ref[...] = grads
    for copy in copies[3:]:
        copy.wait()
    for batch in range(batches):
        for source in range(blocks):
            columns = slice(source * block, (source + 1) * block)
            for target in range(blocks):
                present = pattern_ref[batch, source, target].astype(F32)
                edges = local_ref[batch, source, target].astype(F32) * present
                mixing_ref[batch, target * block : (target + 1) * block, columns] = edges.T.astype(BF16)
            for index, (base, is_low, _) in enumerate(sides):
                slot = jnp.where(is_low, base + 1, base)
                present = pattern_ref[batch, source, blocks + slot].astype(F32)
                edges = halo_ref[batch, slot, source].astype(F32) * present
                start = (blocks + index) * block
                mixing_ref[batch, start : start + block, columns] = edges.T.astype(BF16)
        for index, (base, is_low, paired) in enumerate(sides):
            chosen = pick_ref[batch, jnp.where(is_low, base, base + 1)]
            for target in range(blocks):
                here = ((chosen == target) & paired).astype(F32)
                entry = (batch * blocks + target) * len(sides) + index
                mask_ref[entry] = jnp.full(mask_ref.shape[1:], here, F32)
    send_blocks(grads, matrix_ref[...], mixing_ref, message_ref, out_refs)


def inner_kernel(upstream_ref, message_ref, mixing_ref, total_ref):
    batches, _, nodes = mixing_ref.shape
    for batch in range(batches):
        rows = slice(batch * nodes, (batch + 1) * nodes)
        total_ref[rows] = upstream_ref[rows].astype(F32) + rows_dot(
            mixing_ref[batch, :nodes, :], message_ref[rows]
        )


def turn_kernel(features_ref, turned_ref):
    turned_ref[...] = features_ref[...].T


def choose_kernel(top, top_ref, other_ref, chosen_ref):
    at_top = lax.axis_index("pipe") == top

    @pl.when(at_top)
    def _():
        chosen_ref[...] = top_ref[...]

    @pl.when(jnp.logical_not(at_top))
    def _():
        chosen_ref[...] = other_ref[...]


def close_blocks(mask_ref, total_ref, arrived_refs, result_ref):
    batches, block, _ = arrived_refs[0].shape
    count = len(arrived_refs)
    for batch in range(batches):
        arrived = [ref[batch].astype(F32) for ref in arrived_refs]
        for target in range(total_ref.shape[0] // batches // block):
            order = batch * (total_ref.shape[0] // batches // block) + target
            rows = slice(order * block, (order + 1) * block)
            value = total_ref[rows]
            for index in range(count):
                value = value + arrived[index] * mask_ref[order * count + index]
            result_ref[rows] = value.astype(BF16)


def close_kernel(mask_ref, total_ref, *refs):
    close_blocks(mask_ref, total_ref, refs[:-1], refs[-1])


def last_kernel(top, count, scale, mask_ref, total_ref, *refs):
    arrived_refs = refs[:count]
    top_ref, got_ref = refs[count : count + 2]
    result_ref = refs[-1]
    here = lax.axis_index("pipe")
    if scale is not None:
        kept_ref, piece_ref, result_ref, sum_ref = refs[count + 2 :]
        sum_ref[...] = (kept_ref[...] + piece_ref[...].astype(F32)) * scale

    @pl.when(here == 0)
    def _():
        close_blocks(mask_ref, total_ref, arrived_refs, result_ref)

    @pl.when(here == top)
    def _():
        result_ref[...] = top_ref[...]

    @pl.when((here != 0) & (here != top))
    def _():
        result_ref[...] = got_ref[...]


def step_kernel(layer_ref, mixing_ref, upstream_ref, grad_ref, message_ref, *out_refs):
    grads = (upstream_ref[...].astype(F32) * layer_ref[0].astype(F32)).astype(BF16)
    grad_ref[...] = grads
    send_blocks(grads, layer_ref[1], mixing_ref, message_ref, out_refs)


def close_step_kernel(count, mask_ref, total_ref, *refs):
    layer_ref, mixing_ref, result_ref, grad_ref, message_ref, *out_refs = refs[count:]
    close_blocks(mask_ref, total_ref, refs[:count], result_ref)
    step_kernel(layer_ref, mixing_ref, result_ref, grad_ref, message_ref, *out_refs)


def weight_product(top, turned_ref, grad_ref, top_ref, got_ref, product_ref):
    here = lax.axis_index("pipe")

    def product(ref):
        product_ref[...] = rows_dot(turned_ref[...], ref[...])

    @pl.when(here == 0)
    def _():
        product(grad_ref)

    @pl.when(here == top)
    def _():
        product(top_ref)

    @pl.when((here != 0) & (here != top))
    def _():
        product(got_ref)


def split_halves(step, product_ref, sent_ref, kept_ref):
    axis, distance, groups = step
    size = kept_ref.shape[0] // groups
    place = lax.rem(lax.axis_index(axis) // distance, 2)
    for group in range(groups):
        start = 2 * group * size
        rows = slice(group * size, (group + 1) * size)
        kept = pl.ds(pl.multiple_of(start + place * size, size), size)
        sent = pl.ds(pl.multiple_of(start + (1 - place) * size, size), size)
        kept_ref[rows] = product_ref[kept]
        sent_ref[rows] = product_ref[sent].astype(BF16)


def halve_kernel(step, kept_ref, got_ref, sent_ref, next_ref, sum_ref):
    sum_ref[...] = kept_ref[...] + got_ref[...].astype(F32)
    split_halves(step, sum_ref, sent_ref, next_ref)


def bottom_kernel(count, top, step, mask_ref, total_ref, *refs):
    turned_ref, top_ref, got_ref, layer_ref, mixing_ref = refs[count : count + 5]
    result_ref, next_ref = refs[count + 5 : count + 7]
    out_refs = refs[count + 7 : 2 * count + 7]
    grad_ref, message_ref = refs[-2:]
    close_step_kernel(
        count, mask_ref, total_ref, *refs[:count], layer_ref, mixing_ref,
        result_ref, grad_ref, message_ref, *out_refs
    )
    if step is None:
        weight_product(top, turned_ref, grad_ref, top_ref, got_ref, refs[2 * count + 7])
    else:
        sent_ref, kept_ref, product_ref = refs[2 * count + 7 : -2]
        weight_product(top, turned_ref, grad_ref, top_ref, got_ref, product_ref)
        split_halves(step, product_ref, sent_ref, kept_ref)
    inner_kernel(result_ref, message_ref, mixing_ref, next_ref)


def call(body, inputs, outputs, flops, kind=pltpu.VMEM, source=IN_VMEM, scratch=()):
    size = sum(math.prod(shape) * jnp.dtype(dtype).itemsize for shape, dtype in outputs)
    size += sum(value.size * value.dtype.itemsize for value in inputs)
    return pl.pallas_call(
        body,
        out_shape=[kind(shape, dtype) for shape, dtype in outputs],
        in_specs=[source] * len(inputs),
        out_specs=[IN_VMEM] * len(outputs),
        scratch_shapes=scratch,
        compiler_params=pltpu.CompilerParams(vmem_limit_bytes=16 * 1024 * 1024),
        cost_estimate=pl.CostEstimate(flops=flops, bytes_accessed=size, transcendentals=0),
    )(*inputs)


def per_device(stored, cotangent, weight, local_edges, halo_edges, pattern, pick):
    sections, rows, columns = (lax.axis_size(name) for name in AXES)
    here = lax.axis_index("pipe")
    lower = sections // 2
    upper = sections - lower
    top = sections - 1

    def flat(section, x, y):
        return (section * rows + x) * columns + y

    def to_sections(value, moves, back=True):
        if back:
            moves = moves + [(target, source) for source, target in moves]
        pairs = [
            (flat(source, x, y), flat(target, x, y))
            for source, target in moves
            for x in range(rows)
            for y in range(columns)
        ]
        return lax.ppermute(value, AXES, pairs)

    def tile_swaps(axis, couples, lead):
        partner = {}
        for x in range(rows):
            for y in range(columns):
                if axis == "tx":
                    spare = (x, y ^ 1) if columns % 2 == 0 else (x, y)
                    near = [((a, y), (b, y)) for low, high in couples for a, b in ((low, high), (high, low)) if a == x]
                else:
                    spare = (x ^ 1, y) if rows % 2 == 0 else (x, y)
                    near = [((x, a), (x, b)) for low, high in couples for a, b in ((low, high), (high, low)) if a == y]
                partner[x, y] = near[0][1] if near else spare
        others = [p for p in range(sections) if p != lead]
        pairs = [(flat(lead, *tile), flat(lead, *other)) for tile, other in partner.items()]
        for tile in partner:
            for source, target in zip(others, others[1:] + others[:1]):
                pairs.append((flat(source, *tile), flat(target, *tile)))
        return pairs

    batches, nodes, width = stored.shape[1], stored.shape[4], stored.shape[5]
    blocks, block = local_edges.shape[3], local_edges.shape[5]
    total_rows = batches * nodes
    features = stored.reshape(total_rows, width)
    matrix = weight[0]
    picks = pick[:, 0, 0]

    phases, routes = [], []
    for axis, base, count in (("tx", 0, rows), ("ty", 2, columns)):
        for first, couples in swap_phases(count):
            phases.append((axis, base, first, count))
            route = {lead: tile_swaps(axis, couples, lead) for lead in {0, top}}
            routes.append(route)
    phases = tuple(phases)
    splits, left = [], rows * columns
    if left & (left - 1) == 0 and width // left % 16 == 0:
        for axis, count, other in (("ty", columns, rows), ("tx", rows, 1)):
            distance = count // 2
            while distance > 0:
                pairs = [
                    (flat(p, x, y), flat(p, x, y ^ distance) if axis == "ty" else flat(p, x ^ distance, y))
                    for p in range(sections)
                    for x in range(rows)
                    for y in range(columns)
                ]
                splits.append(((axis, distance, other), pairs))
                distance //= 2
    sent = [((batches, block, width), BF16)] * len(phases)
    whole = ((total_rows, width), BF16)
    mix_rows = (blocks + len(phases)) * block
    cost = 2 * total_rows * width * (width + len(phases) * block)

    def exchange(outs, lead):
        return [lax.ppermute(out, AXES, route[lead]) for out, route in zip(outs, routes)]

    def inner(upstream, message, mixing):
        return call(
            inner_kernel, [upstream, message, mixing], [((total_rows, width), F32)],
            2 * total_rows * width * nodes,
        )[0]

    given = cotangent.reshape(total_rows, width)
    operands = [
        features, matrix, given, pattern[:, 0, 0], picks, local_edges[:, 0, 0], halo_edges[:, 0, 0]
    ]
    layer, mixing, mask, grad, message, *outs = call(
        functools.partial(first_kernel, phases),
        [pltpu.with_memory_space_constraint(value, pltpu.HBM) for value in operands],
        [
            ((2, total_rows, width), BF16), ((batches, mix_rows, nodes), BF16),
            ((batches * blocks * len(phases), 1, width), F32), whole, whole,
        ] + sent,
        cost + 2 * total_rows * width * width,
        source=pl.BlockSpec(memory_space=pltpu.HBM),
        scratch=[
            (pltpu.VMEM if value.dtype == BF16 else pltpu.SMEM)(value.shape, value.dtype)
            for value in operands
        ] + [pltpu.SemaphoreType.DMA((len(operands),))],
    )
    arrived = exchange(outs, top)
    total = inner(given, message, mixing)
    turned = call(turn_kernel, [features], [((width, total_rows), BF16)], 0)[0]

    layers = [layer]
    for step in range(1, upper):
        moves = [(top - step, top)] + ([(step, 0)] if step < lower else [])
        layers.append(to_sections(layer, moves))

    def fetch_home(values):
        got = None
        for step in range(1, upper):
            moves = [(top, top - step)]
            value = values[top - step]
            if step < lower:
                moves.append((0, step))
                value = call(
                    functools.partial(choose_kernel, top), [value, values[step]], [whole], 0
                )[0]
            new = to_sections(value, moves)
            takes = here == top - step
            if step < lower:
                takes = takes | (here == step)
            got = new if step == 1 else jnp.where(takes, new, got)
        return got

    count = len(phases)
    grads, results = {top: grad}, {}
    for section in reversed(range(top)):
        lead = top if section >= lower else 0
        steps = top - section if section >= lower else section
        layer_here = layers[steps]
        if section == lower - 1:
            upstream = call(close_kernel, [mask, total, *arrived], [whole], 0)[0]
            results[section + 1] = upstream
            upstream = to_sections(upstream, [(top, 0)], False)
            grad, message, *outs = call(
                step_kernel, [layer_here, mixing, upstream], [whole, whole] + sent, cost
            )
        elif section > 0:
            upstream, grad, message, *outs = call(
                functools.partial(close_step_kernel, count),
                [mask, total, *arrived, layer_here, mixing],
                [whole, whole, whole] + sent, cost,
            )
            results[section + 1] = upstream
        else:
            product = ((width, width), F32)
            halves = [((width // 2, width), BF16), ((width // 2, width), F32)] if splits else [product]
            upstream, total, *outs = call(
                functools.partial(bottom_kernel, count, top, splits[0][0] if splits else None),
                [mask, total, *arrived, turned, grads[top], fetch_home(grads), layer_here, mixing],
                [whole, ((total_rows, width), F32)] + sent + halves,
                cost + 2 * total_rows * width * (width + nodes),
                scratch=[pltpu.VMEM(*product)] * len(splits[:1]) + [pltpu.VMEM(*whole)] * 2,
            )
            outs, pieces = outs[:count], outs[count:]
            results[1] = upstream
        arrived = exchange(outs, lead)
        if section > 0:
            grads[section] = grad
            total = inner(upstream, message, mixing)

    scale = 1.0 / math.sqrt(total_rows * rows * columns)
    if splits:
        parcel, kept = pieces
        for (_, pairs), following in zip(splits, splits[1:]):
            got = lax.ppermute(parcel, AXES, pairs)
            half = (kept.shape[0] // 2, width)
            parcel, kept = call(
                functools.partial(halve_kernel, following[0]), [kept, got],
                [(half, BF16), (half, F32)], 0, scratch=[pltpu.VMEM(kept.shape, F32)],
            )
        got = lax.ppermute(parcel, AXES, splits[-1][1])
        result, summed = call(
            functools.partial(last_kernel, top, count, scale),
            [mask, total, *arrived, results[top], fetch_home(results), kept, got],
            [whole, (kept.shape, F32)], 0, jax.ShapeDtypeStruct,
        )
    else:
        summed = scale * lax.psum_scatter(pieces[0], ("tx", "ty"), scatter_dimension=0, tiled=True)
        result = call(
            functools.partial(last_kernel, top, count, None),
            [mask, total, *arrived, results[top], fetch_home(results)], [whole], 0,
            jax.ShapeDtypeStruct,
        )[0]
    return (summed[None], result.reshape(1, batches, 1, 1, nodes, width))


def solution(mesh):
    in_specs = (
        P("pipe", None, "tx", "ty", None, None),
        P(None, "tx", "ty", None, None),
        P("pipe", None, None),
        P(None, "tx", "ty", None, None, None, None),
        P(None, "tx", "ty", None, None, None, None),
        P(None, "tx", "ty", None, None),
        P(None, "tx", "ty", None),
    )
    out_specs = (P("pipe", ("tx", "ty"), None), P("pipe", None, "tx", "ty", None, None))
    return jax.shard_map(
        per_device, mesh=mesh, in_specs=in_specs, out_specs=out_specs, check_vma=False
    )
```

```python
import functools
import math

import jax
import jax.numpy as jnp
from jax import lax
from jax.experimental import pallas as pl
from jax.experimental.pallas import tpu as pltpu
from jax.sharding import PartitionSpec as P

AXES = ("pipe", "tx", "ty")
F32, BF16 = jnp.float32, jnp.bfloat16
IN_VMEM = pl.BlockSpec(memory_space=pltpu.VMEM)


def silu_slope(value):
    sigma = jax.nn.sigmoid(value)
    return sigma * (1.0 + value * (1.0 - sigma))


def swap_phases(count):
    phases = []
    for first in (0, 1):
        pairs = [(low, low + 1) for low in range(first, count - 1, 2)]
        if pairs:
            phases.append((first, pairs))
    return phases


def side(phase):
    axis, base, first, count = phase
    place = lax.axis_index(axis)
    is_low = lax.rem(place + first, 2) == 0
    return base, is_low, jnp.where(is_low, place < count - 1, place > 0)


def rows_dot(left, right):
    return lax.dot_general(left, right, (((1,), (0,)), ((), ())), preferred_element_type=F32)


def back_dot(left, right):
    return lax.dot_general(left, right, (((1,), (1,)), ((), ())), preferred_element_type=F32)


def send_blocks(grads, matrix, mixing_ref, message_ref, out_refs):
    batches, outgoing, nodes = mixing_ref.shape
    block = out_refs[0].shape[1]
    messages = back_dot(grads, matrix).astype(BF16)
    message_ref[...] = messages
    first = outgoing - block * len(out_refs)
    for batch in range(batches):
        mixed = rows_dot(
            mixing_ref[batch, first:, :], messages[batch * nodes : (batch + 1) * nodes]
        ).astype(BF16)
        for index, out_ref in enumerate(out_refs):
            out_ref[batch] = mixed[index * block : (index + 1) * block]


def first_kernel(phases, *refs):
    sources, refs = refs[:7], refs[7:]
    layer_ref, mixing_ref, mask_ref, grad_ref, message_ref = refs[:5]
    out_refs = refs[5 : 5 + len(phases)]
    held, sems = refs[5 + len(phases) : -1], refs[-1]
    copies = [
        pltpu.make_async_copy(source, target, sems.at[index])
        for index, (source, target) in enumerate(zip(sources, held))
    ]
    for copy in copies:
        copy.start()
    features_ref, matrix_ref, given_ref, pattern_ref, pick_ref, local_ref, halo_ref = held
    batches, blocks, _, block, _ = local_ref.shape
    sides = [side(phase) for phase in phases]
    copies[0].wait()
    copies[1].wait()
    pre_activation = rows_dot(features_ref[...], matrix_ref[...])
    slope = silu_slope(pre_activation).astype(BF16)
    layer_ref[0] = slope
    layer_ref[1] = matrix_ref[...]
    copies[2].wait()
    grads = (given_ref[...].astype(F32) * slope.astype(F32)).astype(BF16)
    grad_ref[...] = grads
    for copy in copies[3:]:
        copy.wait()
    for batch in range(batches):
        for source in range(blocks):
            columns = slice(source * block, (source + 1) * block)
            for target in range(blocks):
                present = pattern_ref[batch, source, target].astype(F32)
                edges = local_ref[batch, source, target].astype(F32) * present
                mixing_ref[batch, target * block : (target + 1) * block, columns] = edges.T.astype(BF16)
            for index, (base, is_low, _) in enumerate(sides):
                slot = jnp.where(is_low, base + 1, base)
                present = pattern_ref[batch, source, blocks + slot].astype(F32)
                edges = halo_ref[batch, slot, source].astype(F32) * present
                start = (blocks + index) * block
                mixing_ref[batch, start : start + block, columns] = edges.T.astype(BF16)
        for index, (base, is_low, paired) in enumerate(sides):
            chosen = pick_ref[batch, jnp.where(is_low, base, base + 1)]
            for target in range(blocks):
                here = ((chosen == target) & paired).astype(F32)
                entry = (batch * blocks + target) * len(sides) + index
                mask_ref[entry] = jnp.full(mask_ref.shape[1:], here, F32)
    send_blocks(grads, matrix_ref[...], mixing_ref, message_ref, out_refs)


def inner_kernel(upstream_ref, message_ref, mixing_ref, total_ref):
    batches, _, nodes = mixing_ref.shape
    for batch in range(batches):
        rows = slice(batch * nodes, (batch + 1) * nodes)
        total_ref[rows] = upstream_ref[rows].astype(F32) + rows_dot(
            mixing_ref[batch, :nodes, :], message_ref[rows]
        )


def turn_kernel(features_ref, turned_ref):
    turned_ref[...] = features_ref[...].T


def choose_kernel(top, top_ref, other_ref, chosen_ref):
    at_top = lax.axis_index("pipe") == top

    @pl.when(at_top)
    def _():
        chosen_ref[...] = top_ref[...]

    @pl.when(jnp.logical_not(at_top))
    def _():
        chosen_ref[...] = other_ref[...]


def close_blocks(mask_ref, total_ref, arrived_refs, result_ref):
    batches, block, _ = arrived_refs[0].shape
    count = len(arrived_refs)
    for batch in range(batches):
        arrived = [ref[batch].astype(F32) for ref in arrived_refs]
        for target in range(total_ref.shape[0] // batches // block):
            order = batch * (total_ref.shape[0] // batches // block) + target
            rows = slice(order * block, (order + 1) * block)
            value = total_ref[rows]
            for index in range(count):
                value = value + arrived[index] * mask_ref[order * count + index]
            result_ref[rows] = value.astype(BF16)


def close_kernel(mask_ref, total_ref, *refs):
    close_blocks(mask_ref, total_ref, refs[:-1], refs[-1])


def last_kernel(top, count, scale, mask_ref, total_ref, *refs):
    arrived_refs = refs[:count]
    top_ref, got_ref = refs[count : count + 2]
    result_ref = refs[-1]
    here = lax.axis_index("pipe")
    if scale is not None:
        kept_ref, piece_ref, result_ref, sum_ref = refs[count + 2 :]
        sum_ref[...] = (kept_ref[...] + piece_ref[...].astype(F32)) * scale

    @pl.when(here == 0)
    def _():
        close_blocks(mask_ref, total_ref, arrived_refs, result_ref)

    @pl.when(here == top)
    def _():
        result_ref[...] = top_ref[...]

    @pl.when((here != 0) & (here != top))
    def _():
        result_ref[...] = got_ref[...]


def step_kernel(layer_ref, mixing_ref, upstream_ref, grad_ref, message_ref, *out_refs):
    grads = (upstream_ref[...].astype(F32) * layer_ref[0].astype(F32)).astype(BF16)
    grad_ref[...] = grads
    send_blocks(grads, layer_ref[1], mixing_ref, message_ref, out_refs)


def close_step_kernel(count, mask_ref, total_ref, *refs):
    layer_ref, mixing_ref, result_ref, grad_ref, message_ref, *out_refs = refs[count:]
    close_blocks(mask_ref, total_ref, refs[:count], result_ref)
    step_kernel(layer_ref, mixing_ref, result_ref, grad_ref, message_ref, *out_refs)


def weight_product(top, turned_ref, grad_ref, top_ref, got_ref, product_ref):
    here = lax.axis_index("pipe")

    def product(ref):
        product_ref[...] = rows_dot(turned_ref[...], ref[...])

    @pl.when(here == 0)
    def _():
        product(grad_ref)

    @pl.when(here == top)
    def _():
        product(top_ref)

    @pl.when((here != 0) & (here != top))
    def _():
        product(got_ref)


def split_halves(step, product_ref, sent_ref, kept_ref):
    axis, distance, groups = step
    size = kept_ref.shape[0] // groups
    place = lax.rem(lax.axis_index(axis) // distance, 2)
    for group in range(groups):
        start = 2 * group * size
        rows = slice(group * size, (group + 1) * size)
        kept = pl.ds(pl.multiple_of(start + place * size, size), size)
        sent = pl.ds(pl.multiple_of(start + (1 - place) * size, size), size)
        kept_ref[rows] = product_ref[kept]
        sent_ref[rows] = product_ref[sent].astype(BF16)


def halve_kernel(step, kept_ref, got_ref, sent_ref, next_ref, sum_ref):
    sum_ref[...] = kept_ref[...] + got_ref[...].astype(F32)
    split_halves(step, sum_ref, sent_ref, next_ref)


def bottom_kernel(count, top, step, mask_ref, total_ref, *refs):
    turned_ref, top_ref, got_ref, layer_ref, mixing_ref = refs[count : count + 5]
    result_ref, next_ref = refs[count + 5 : count + 7]
    out_refs = refs[count + 7 : 2 * count + 7]
    grad_ref, message_ref = refs[-2:]
    close_step_kernel(
        count, mask_ref, total_ref, *refs[:count], layer_ref, mixing_ref,
        result_ref, grad_ref, message_ref, *out_refs
    )
    if step is None:
        weight_product(top, turned_ref, grad_ref, top_ref, got_ref, refs[2 * count + 7])
    else:
        sent_ref, kept_ref, product_ref = refs[2 * count + 7 : -2]
        weight_product(top, turned_ref, grad_ref, top_ref, got_ref, product_ref)
        split_halves(step, product_ref, sent_ref, kept_ref)
    inner_kernel(result_ref, message_ref, mixing_ref, next_ref)


def call(body, inputs, outputs, flops, kind=pltpu.VMEM, source=IN_VMEM, scratch=()):
    size = sum(math.prod(shape) * jnp.dtype(dtype).itemsize for shape, dtype in outputs)
    size += sum(value.size * value.dtype.itemsize for value in inputs)
    return pl.pallas_call(
        body,
        out_shape=[kind(shape, dtype) for shape, dtype in outputs],
        in_specs=[source] * len(inputs),
        out_specs=[IN_VMEM] * len(outputs),
        scratch_shapes=scratch,
        compiler_params=pltpu.CompilerParams(vmem_limit_bytes=16 * 1024 * 1024),
        cost_estimate=pl.CostEstimate(flops=flops, bytes_accessed=size, transcendentals=0),
    )(*inputs)


def per_device(stored, cotangent, weight, local_edges, halo_edges, pattern, pick):
    sections, rows, columns = (lax.axis_size(name) for name in AXES)
    here = lax.axis_index("pipe")
    lower = sections // 2
    upper = sections - lower
    top = sections - 1

    def flat(section, x, y):
        return (section * rows + x) * columns + y

    def to_sections(value, moves, back=True, crossed=False):
        if back:
            returns = [source for source, _ in moves]
            returns = returns[::-1] if crossed else returns
            moves = moves + [(target, source) for (_, target), source in zip(moves, returns)]
        pairs = [
            (flat(source, x, y), flat(target, x, y))
            for source, target in moves
            for x in range(rows)
            for y in range(columns)
        ]
        return lax.ppermute(value, AXES, pairs)

    def beside(axis):
        def other(x, y):
            if axis == "tx":
                return (x ^ 1, y) if rows % 2 == 0 else (x, y)
            return (x, y ^ 1) if columns % 2 == 0 else (x, y)

        return other

    def tile_swaps(axis, first, couples, lead):
        places = {}
        for low, high in couples:
            places[low], places[high] = high, low
        across = beside("ty" if axis == "tx" else "tx")

        def swapped(x, y):
            if axis == "tx":
                return (places[x], y) if x in places else across(x, y)
            return (x, places[y]) if y in places else across(x, y)

        def same(x, y):
            return (x, y)

        others = [p for p in range(sections) if p != lead]
        moves = [(lead, lead, swapped)]
        if sections == 4:
            buddy, inner, outer = lead ^ 1, 3 - (lead ^ 1), 3 - lead
            if axis == "tx":
                moves += [(buddy, inner, same), (inner, buddy, same)]
                moves += [(outer, outer, beside("tx") if first else across)]
            else:
                moves += [(inner, outer, same), (outer, inner, same), (buddy, buddy, across)]
        else:
            moves += [(p, q, same) for p, q in zip(others, others[1:] + others[:1])]
        return [
            (flat(source, x, y), flat(target, *place(x, y)))
            for source, target, place in moves
            for x in range(rows)
            for y in range(columns)
        ]

    batches, nodes, width = stored.shape[1], stored.shape[4], stored.shape[5]
    blocks, block = local_edges.shape[3], local_edges.shape[5]
    total_rows = batches * nodes
    features = stored.reshape(total_rows, width)
    matrix = weight[0]
    picks = pick[:, 0, 0]

    phases, routes = [], []
    for axis, base, count in (("tx", 0, rows), ("ty", 2, columns)):
        for first, couples in swap_phases(count):
            phases.append((axis, base, first, count))
            route = {lead: tile_swaps(axis, first, couples, lead) for lead in {0, top}}
            routes.append(route)
    phases = tuple(phases)
    splits, left = [], rows * columns
    if left & (left - 1) == 0 and width // left % 16 == 0:
        for axis, count, other in (("ty", columns, rows), ("tx", rows, 1)):
            distance = count // 2
            while distance > 0:
                pairs = [
                    (flat(p, x, y), flat(p, x, y ^ distance) if axis == "ty" else flat(p, x ^ distance, y))
                    for p in range(sections)
                    for x in range(rows)
                    for y in range(columns)
                ]
                splits.append(((axis, distance, other), pairs))
                distance //= 2
    sent = [((batches, block, width), BF16)] * len(phases)
    whole = ((total_rows, width), BF16)
    mix_rows = (blocks + len(phases)) * block
    cost = 2 * total_rows * width * (width + len(phases) * block)

    def exchange(outs, lead):
        return [lax.ppermute(out, AXES, route[lead]) for out, route in zip(outs, routes)]

    def inner(upstream, message, mixing):
        return call(
            inner_kernel, [upstream, message, mixing], [((total_rows, width), F32)],
            2 * total_rows * width * nodes,
        )[0]

    given = cotangent.reshape(total_rows, width)
    operands = [
        features, matrix, given, pattern[:, 0, 0], picks, local_edges[:, 0, 0], halo_edges[:, 0, 0]
    ]
    layer, mixing, mask, grad, message, *outs = call(
        functools.partial(first_kernel, phases),
        [pltpu.with_memory_space_constraint(value, pltpu.HBM) for value in operands],
        [
            ((2, total_rows, width), BF16), ((batches, mix_rows, nodes), BF16),
            ((batches * blocks * len(phases), 1, width), F32), whole, whole,
        ] + sent,
        cost + 2 * total_rows * width * width,
        source=pl.BlockSpec(memory_space=pltpu.HBM),
        scratch=[
            (pltpu.VMEM if value.dtype == BF16 else pltpu.SMEM)(value.shape, value.dtype)
            for value in operands
        ] + [pltpu.SemaphoreType.DMA((len(operands),))],
    )
    arrived = exchange(outs, top)
    total = inner(given, message, mixing)
    turned = call(turn_kernel, [features], [((width, total_rows), BF16)], 0)[0]

    layers = [layer]
    for step in range(1, upper):
        moves = [(top - step, top)] + ([(step, 0)] if step < lower else [])
        layers.append(to_sections(layer, moves))

    def fetch_home(values, crossed=False):
        got = None
        for step in range(1, upper):
            moves = [(top, top - step)]
            value = values[top - step]
            if step < lower:
                moves.append((0, step))
                value = call(
                    functools.partial(choose_kernel, top), [value, values[step]], [whole], 0
                )[0]
            new = to_sections(value, moves, crossed=crossed)
            takes = here == top - step
            if step < lower:
                takes = takes | (here == step)
            got = new if step == 1 else jnp.where(takes, new, got)
        return got

    count = len(phases)
    grads, results = {top: grad}, {}
    for section in reversed(range(top)):
        lead = top if section >= lower else 0
        steps = top - section if section >= lower else section
        layer_here = layers[steps]
        if section == lower - 1:
            upstream = call(close_kernel, [mask, total, *arrived], [whole], 0)[0]
            results[section + 1] = upstream
            upstream = to_sections(upstream, [(top, 0)], False)
            grad, message, *outs = call(
                step_kernel, [layer_here, mixing, upstream], [whole, whole] + sent, cost
            )
        elif section > 0:
            upstream, grad, message, *outs = call(
                functools.partial(close_step_kernel, count),
                [mask, total, *arrived, layer_here, mixing],
                [whole, whole, whole] + sent, cost,
            )
            results[section + 1] = upstream
        else:
            product = ((width, width), F32)
            halves = [((width // 2, width), BF16), ((width // 2, width), F32)] if splits else [product]
            upstream, total, *outs = call(
                functools.partial(bottom_kernel, count, top, splits[0][0] if splits else None),
                [mask, total, *arrived, turned, grads[top], fetch_home(grads), layer_here, mixing],
                [whole, ((total_rows, width), F32)] + sent + halves,
                cost + 2 * total_rows * width * (width + nodes),
                scratch=[pltpu.VMEM(*product)] * len(splits[:1]) + [pltpu.VMEM(*whole)] * 2,
            )
            outs, pieces = outs[:count], outs[count:]
            results[1] = upstream
        arrived = exchange(outs, lead)
        if section > 0:
            grads[section] = grad
            total = inner(upstream, message, mixing)

    scale = 1.0 / math.sqrt(total_rows * rows * columns)
    if splits:
        parcel, kept = pieces
        for (_, pairs), following in zip(splits, splits[1:]):
            got = lax.ppermute(parcel, AXES, pairs)
            half = (kept.shape[0] // 2, width)
            parcel, kept = call(
                functools.partial(halve_kernel, following[0]), [kept, got],
                [(half, BF16), (half, F32)], 0, scratch=[pltpu.VMEM(kept.shape, F32)],
            )
        got = lax.ppermute(parcel, AXES, splits[-1][1])
        result, summed = call(
            functools.partial(last_kernel, top, count, scale),
            [mask, total, *arrived, results[top], fetch_home(results, True), kept, got],
            [whole, (kept.shape, F32)], 0, jax.ShapeDtypeStruct,
        )
    else:
        summed = scale * lax.psum_scatter(pieces[0], ("tx", "ty"), scatter_dimension=0, tiled=True)
        result = call(
            functools.partial(last_kernel, top, count, None),
            [mask, total, *arrived, results[top], fetch_home(results, True)], [whole], 0,
            jax.ShapeDtypeStruct,
        )[0]
    return (summed[None], result.reshape(1, batches, 1, 1, nodes, width))


def solution(mesh):
    in_specs = (
        P("pipe", None, "tx", "ty", None, None),
        P(None, "tx", "ty", None, None),
        P("pipe", None, None),
        P(None, "tx", "ty", None, None, None, None),
        P(None, "tx", "ty", None, None, None, None),
        P(None, "tx", "ty", None, None),
        P(None, "tx", "ty", None),
    )
    out_specs = (P("pipe", ("tx", "ty"), None), P("pipe", None, "tx", "ty", None, None))
    return jax.shard_map(
        per_device, mesh=mesh, in_specs=in_specs, out_specs=out_specs, check_vma=False
    )
```

```python
import functools
import math

import jax
import jax.numpy as jnp
from jax import lax
from jax.experimental import pallas as pl
from jax.experimental.pallas import tpu as pltpu
from jax.sharding import PartitionSpec as P

AXES = ("pipe", "tx", "ty")
F32, BF16 = jnp.float32, jnp.bfloat16
IN_VMEM = pl.BlockSpec(memory_space=pltpu.VMEM)


def silu_slope(value):
    sigma = jax.nn.sigmoid(value)
    return sigma * (1.0 + value * (1.0 - sigma))


def swap_phases(count):
    phases = []
    for first in (0, 1):
        pairs = [(low, low + 1) for low in range(first, count - 1, 2)]
        if pairs:
            phases.append((first, pairs))
    return phases


def side(phase):
    axis, base, first, count = phase
    place = lax.axis_index(axis)
    is_low = lax.rem(place + first, 2) == 0
    return base, is_low, jnp.where(is_low, place < count - 1, place > 0)


def rows_dot(left, right):
    return lax.dot_general(left, right, (((1,), (0,)), ((), ())), preferred_element_type=F32)


def back_dot(left, right):
    return lax.dot_general(left, right, (((1,), (1,)), ((), ())), preferred_element_type=F32)


def send_blocks(grads, matrix, mixing_ref, message_ref, out_refs):
    batches, outgoing, nodes = mixing_ref.shape
    block = out_refs[0].shape[1]
    messages = back_dot(grads, matrix).astype(BF16)
    message_ref[...] = messages
    first = outgoing - block * len(out_refs)
    for batch in range(batches):
        mixed = rows_dot(
            mixing_ref[batch, first:, :], messages[batch * nodes : (batch + 1) * nodes]
        ).astype(BF16)
        for index, out_ref in enumerate(out_refs):
            out_ref[batch] = mixed[index * block : (index + 1) * block]


def first_kernel(phases, *refs):
    sources, refs = refs[:7], refs[7:]
    layer_ref, mixing_ref, mask_ref, grad_ref, message_ref = refs[:5]
    out_refs = refs[5 : 5 + len(phases)]
    held, sems = refs[5 + len(phases) : -1], refs[-1]
    copies = [
        pltpu.make_async_copy(source, target, sems.at[index])
        for index, (source, target) in enumerate(zip(sources, held))
    ]
    for copy in copies:
        copy.start()
    features_ref, matrix_ref, given_ref, pattern_ref, pick_ref, local_ref, halo_ref = held
    batches, blocks, _, block, _ = local_ref.shape
    sides = [side(phase) for phase in phases]
    copies[0].wait()
    copies[1].wait()
    pre_activation = rows_dot(features_ref[...], matrix_ref[...])
    slope = silu_slope(pre_activation).astype(BF16)
    layer_ref[0] = slope
    layer_ref[1] = matrix_ref[...]
    copies[2].wait()
    grads = (given_ref[...].astype(F32) * slope.astype(F32)).astype(BF16)
    grad_ref[...] = grads
    for copy in copies[3:]:
        copy.wait()
    for batch in range(batches):
        for source in range(blocks):
            columns = slice(source * block, (source + 1) * block)
            for target in range(blocks):
                present = pattern_ref[batch, source, target].astype(F32)
                edges = local_ref[batch, source, target].astype(F32) * present
                mixing_ref[batch, target * block : (target + 1) * block, columns] = edges.T.astype(BF16)
            for index, (base, is_low, _) in enumerate(sides):
                slot = jnp.where(is_low, base + 1, base)
                present = pattern_ref[batch, source, blocks + slot].astype(F32)
                edges = halo_ref[batch, slot, source].astype(F32) * present
                start = (blocks + index) * block
                mixing_ref[batch, start : start + block, columns] = edges.T.astype(BF16)
        for index, (base, is_low, paired) in enumerate(sides):
            chosen = pick_ref[batch, jnp.where(is_low, base, base + 1)]
            for target in range(blocks):
                here = ((chosen == target) & paired).astype(F32)
                entry = (batch * blocks + target) * len(sides) + index
                mask_ref[entry] = jnp.full(mask_ref.shape[1:], here, F32)
    send_blocks(grads, matrix_ref[...], mixing_ref, message_ref, out_refs)


def inner_kernel(upstream_ref, message_ref, mixing_ref, total_ref):
    batches, _, nodes = mixing_ref.shape
    for batch in range(batches):
        rows = slice(batch * nodes, (batch + 1) * nodes)
        total_ref[rows] = upstream_ref[rows].astype(F32) + rows_dot(
            mixing_ref[batch, :nodes, :], message_ref[rows]
        )


def turn_kernel(features_ref, turned_ref):
    turned_ref[...] = features_ref[...].T


def choose_kernel(top, top_ref, other_ref, chosen_ref):
    at_top = lax.axis_index("pipe") == top

    @pl.when(at_top)
    def _():
        chosen_ref[...] = top_ref[...]

    @pl.when(jnp.logical_not(at_top))
    def _():
        chosen_ref[...] = other_ref[...]


def close_blocks(mask_ref, total_ref, arrived_refs, result_ref):
    batches, block, _ = arrived_refs[0].shape
    count = len(arrived_refs)
    for batch in range(batches):
        arrived = [ref[batch].astype(F32) for ref in arrived_refs]
        for target in range(total_ref.shape[0] // batches // block):
            order = batch * (total_ref.shape[0] // batches // block) + target
            rows = slice(order * block, (order + 1) * block)
            value = total_ref[rows]
            for index in range(count):
                value = value + arrived[index] * mask_ref[order * count + index]
            result_ref[rows] = value.astype(BF16)


def close_kernel(mask_ref, total_ref, *refs):
    close_blocks(mask_ref, total_ref, refs[:-1], refs[-1])


def last_kernel(top, count, scale, mask_ref, total_ref, *refs):
    arrived_refs = refs[:count]
    top_ref, got_ref = refs[count : count + 2]
    result_ref = refs[-1]
    here = lax.axis_index("pipe")
    if scale is not None:
        kept_ref, piece_ref, result_ref, sum_ref = refs[count + 2 :]
        sum_ref[...] = (kept_ref[...] + piece_ref[...].astype(F32)) * scale

    @pl.when(here == 0)
    def _():
        close_blocks(mask_ref, total_ref, arrived_refs, result_ref)

    @pl.when(here == top)
    def _():
        result_ref[...] = top_ref[...]

    @pl.when((here != 0) & (here != top))
    def _():
        result_ref[...] = got_ref[...]


def step_kernel(layer_ref, mixing_ref, upstream_ref, grad_ref, message_ref, *out_refs):
    grads = (upstream_ref[...].astype(F32) * layer_ref[0].astype(F32)).astype(BF16)
    grad_ref[...] = grads
    send_blocks(grads, layer_ref[1], mixing_ref, message_ref, out_refs)


def close_step_kernel(count, mask_ref, total_ref, *refs):
    layer_ref, mixing_ref, result_ref, grad_ref, message_ref, *out_refs = refs[count:]
    close_blocks(mask_ref, total_ref, refs[:count], result_ref)
    step_kernel(layer_ref, mixing_ref, result_ref, grad_ref, message_ref, *out_refs)


def weight_product(top, turned_ref, grad_ref, top_ref, got_ref, product_ref):
    here = lax.axis_index("pipe")

    def product(ref):
        product_ref[...] = rows_dot(turned_ref[...], ref[...])

    @pl.when(here == 0)
    def _():
        product(grad_ref)

    @pl.when(here == top)
    def _():
        product(top_ref)

    @pl.when((here != 0) & (here != top))
    def _():
        product(got_ref)


def split_halves(steps, product_ref, sent_ref, kept_ref):
    def split(axis, distance, groups):
        size = kept_ref.shape[0] // groups
        place = lax.rem(lax.axis_index(axis) // distance, 2)
        for group in range(groups):
            start = 2 * group * size
            rows = slice(group * size, (group + 1) * size)
            kept = pl.ds(pl.multiple_of(start + place * size, size), size)
            sent = pl.ds(pl.multiple_of(start + (1 - place) * size, size), size)
            kept_ref[rows] = product_ref[kept]
            sent_ref[rows] = product_ref[sent].astype(BF16)

    if steps[0] == steps[1]:
        split(*steps[0])
    else:
        odd = lax.rem(lax.axis_index("pipe"), 2) == 1

        @pl.when(odd)
        def _():
            split(*steps[1])

        @pl.when(jnp.logical_not(odd))
        def _():
            split(*steps[0])


def halve_kernel(step, kept_ref, got_ref, sent_ref, next_ref, sum_ref):
    sum_ref[...] = kept_ref[...] + got_ref[...].astype(F32)
    split_halves(step, sum_ref, sent_ref, next_ref)


def bottom_kernel(count, top, step, mask_ref, total_ref, *refs):
    turned_ref, top_ref, got_ref, layer_ref, mixing_ref = refs[count : count + 5]
    result_ref, next_ref = refs[count + 5 : count + 7]
    out_refs = refs[count + 7 : 2 * count + 7]
    grad_ref, message_ref = refs[-2:]
    close_step_kernel(
        count, mask_ref, total_ref, *refs[:count], layer_ref, mixing_ref,
        result_ref, grad_ref, message_ref, *out_refs
    )
    if step is None:
        weight_product(top, turned_ref, grad_ref, top_ref, got_ref, refs[2 * count + 7])
    else:
        sent_ref, kept_ref, product_ref = refs[2 * count + 7 : -2]
        weight_product(top, turned_ref, grad_ref, top_ref, got_ref, product_ref)
        split_halves(step, product_ref, sent_ref, kept_ref)
    inner_kernel(result_ref, message_ref, mixing_ref, next_ref)


def call(body, inputs, outputs, flops, kind=pltpu.VMEM, source=IN_VMEM, scratch=()):
    size = sum(math.prod(shape) * jnp.dtype(dtype).itemsize for shape, dtype in outputs)
    size += sum(value.size * value.dtype.itemsize for value in inputs)
    return pl.pallas_call(
        body,
        out_shape=[kind(shape, dtype) for shape, dtype in outputs],
        in_specs=[source] * len(inputs),
        out_specs=[IN_VMEM] * len(outputs),
        scratch_shapes=scratch,
        compiler_params=pltpu.CompilerParams(vmem_limit_bytes=16 * 1024 * 1024),
        cost_estimate=pl.CostEstimate(flops=flops, bytes_accessed=size, transcendentals=0),
    )(*inputs)


def per_device(stored, cotangent, weight, local_edges, halo_edges, pattern, pick):
    sections, rows, columns = (lax.axis_size(name) for name in AXES)
    here = lax.axis_index("pipe")
    lower = sections // 2
    upper = sections - lower
    top = sections - 1

    def flat(section, x, y):
        return (section * rows + x) * columns + y

    def to_sections(value, moves, back=True, crossed=False):
        if back:
            returns = [source for source, _ in moves]
            returns = returns[::-1] if crossed else returns
            moves = moves + [(target, source) for (_, target), source in zip(moves, returns)]
        pairs = [
            (flat(source, x, y), flat(target, x, y))
            for source, target in moves
            for x in range(rows)
            for y in range(columns)
        ]
        return lax.ppermute(value, AXES, pairs)

    def beside(axis):
        def other(x, y):
            if axis == "tx":
                return (x ^ 1, y) if rows % 2 == 0 else (x, y)
            return (x, y ^ 1) if columns % 2 == 0 else (x, y)

        return other

    def tile_swaps(axis, first, couples, lead):
        places = {}
        for low, high in couples:
            places[low], places[high] = high, low
        across = beside("ty" if axis == "tx" else "tx")

        def swapped(x, y):
            if axis == "tx":
                return (places[x], y) if x in places else across(x, y)
            return (x, places[y]) if y in places else across(x, y)

        def same(x, y):
            return (x, y)

        others = [p for p in range(sections) if p != lead]
        moves = [(lead, lead, swapped)]
        if sections == 4:
            buddy, inner, outer = lead ^ 1, 3 - (lead ^ 1), 3 - lead
            if axis == "tx":
                moves += [(buddy, inner, same), (inner, buddy, same)]
                moves += [(outer, outer, beside("tx") if first else across)]
            else:
                moves += [(inner, outer, same), (outer, inner, same), (buddy, buddy, across)]
        else:
            moves += [(p, q, same) for p, q in zip(others, others[1:] + others[:1])]
        return [
            (flat(source, x, y), flat(target, *place(x, y)))
            for source, target, place in moves
            for x in range(rows)
            for y in range(columns)
        ]

    batches, nodes, width = stored.shape[1], stored.shape[4], stored.shape[5]
    blocks, block = local_edges.shape[3], local_edges.shape[5]
    total_rows = batches * nodes
    features = stored.reshape(total_rows, width)
    matrix = weight[0]
    picks = pick[:, 0, 0]

    phases, routes = [], []
    for axis, base, count in (("tx", 0, rows), ("ty", 2, columns)):
        for first, couples in swap_phases(count):
            phases.append((axis, base, first, count))
            route = {lead: tile_swaps(axis, first, couples, lead) for lead in {0, top}}
            routes.append(route)
    phases = tuple(phases)
    splits, left = [], rows * columns
    if left & (left - 1) == 0 and width // left % 16 == 0:
        along = {"tx": [], "ty": []}
        for axis, count in (("tx", rows), ("ty", columns)):
            while 1 << len(along[axis]) < count:
                along[axis].append((axis, 1 << len(along[axis])))
        orders = [
            along["ty"][::-1] + along["tx"], along["tx"][:1] + along["ty"][::-1] + along["tx"][1:]
        ]
        levels = [along["tx"][::-1] + along["ty"][::-1] for _ in orders]
        for index in range(len(orders[0])):
            steps, pairs = [], []
            for order, level in zip(orders, levels):
                steps.append((*order[index], 1 << level.index(order[index])))
                level.remove(order[index])
            for p in range(sections):
                axis, distance, _ = steps[p % 2]
                pairs += [
                    (flat(p, x, y), flat(p, x, y ^ distance) if axis == "ty" else flat(p, x ^ distance, y))
                    for x in range(rows)
                    for y in range(columns)
                ]
            splits.append((tuple(steps), pairs))
    sent = [((batches, block, width), BF16)] * len(phases)
    whole = ((total_rows, width), BF16)
    mix_rows = (blocks + len(phases)) * block
    cost = 2 * total_rows * width * (width + len(phases) * block)

    def exchange(outs, lead):
        return [lax.ppermute(out, AXES, route[lead]) for out, route in zip(outs, routes)]

    def inner(upstream, message, mixing):
        return call(
            inner_kernel, [upstream, message, mixing], [((total_rows, width), F32)],
            2 * total_rows * width * nodes,
        )[0]

    given = cotangent.reshape(total_rows, width)
    operands = [
        features, matrix, given, pattern[:, 0, 0], picks, local_edges[:, 0, 0], halo_edges[:, 0, 0]
    ]
    layer, mixing, mask, grad, message, *outs = call(
        functools.partial(first_kernel, phases),
        [pltpu.with_memory_space_constraint(value, pltpu.HBM) for value in operands],
        [
            ((2, total_rows, width), BF16), ((batches, mix_rows, nodes), BF16),
            ((batches * blocks * len(phases), 1, width), F32), whole, whole,
        ] + sent,
        cost + 2 * total_rows * width * width,
        source=pl.BlockSpec(memory_space=pltpu.HBM),
        scratch=[
            (pltpu.VMEM if value.dtype == BF16 else pltpu.SMEM)(value.shape, value.dtype)
            for value in operands
        ] + [pltpu.SemaphoreType.DMA((len(operands),))],
    )
    arrived = exchange(outs, top)
    total = inner(given, message, mixing)
    turned = call(turn_kernel, [features], [((width, total_rows), BF16)], 0)[0]

    layers = [layer]
    for step in range(1, upper):
        moves = [(top - step, top)] + ([(step, 0)] if step < lower else [])
        layers.append(to_sections(layer, moves))

    def fetch_home(values, crossed=False):
        got = None
        for step in range(1, upper):
            moves = [(top, top - step)]
            value = values[top - step]
            if step < lower:
                moves.append((0, step))
                value = call(
                    functools.partial(choose_kernel, top), [value, values[step]], [whole], 0
                )[0]
            new = to_sections(value, moves, crossed=crossed)
            takes = here == top - step
            if step < lower:
                takes = takes | (here == step)
            got = new if step == 1 else jnp.where(takes, new, got)
        return got

    count = len(phases)
    grads, results = {top: grad}, {}
    for section in reversed(range(top)):
        lead = top if section >= lower else 0
        steps = top - section if section >= lower else section
        layer_here = layers[steps]
        if section == lower - 1:
            upstream = call(close_kernel, [mask, total, *arrived], [whole], 0)[0]
            results[section + 1] = upstream
            upstream = to_sections(upstream, [(top, 0)], False)
            grad, message, *outs = call(
                step_kernel, [layer_here, mixing, upstream], [whole, whole] + sent, cost
            )
        elif section > 0:
            upstream, grad, message, *outs = call(
                functools.partial(close_step_kernel, count),
                [mask, total, *arrived, layer_here, mixing],
                [whole, whole, whole] + sent, cost,
            )
            results[section + 1] = upstream
        else:
            product = ((width, width), F32)
            halves = [((width // 2, width), BF16), ((width // 2, width), F32)] if splits else [product]
            upstream, total, *outs = call(
                functools.partial(bottom_kernel, count, top, splits[0][0] if splits else None),
                [mask, total, *arrived, turned, grads[top], fetch_home(grads), layer_here, mixing],
                [whole, ((total_rows, width), F32)] + sent + halves,
                cost + 2 * total_rows * width * (width + nodes),
                scratch=[pltpu.VMEM(*product)] * len(splits[:1]) + [pltpu.VMEM(*whole)] * 2,
            )
            outs, pieces = outs[:count], outs[count:]
            results[1] = upstream
        arrived = exchange(outs, lead)
        if section > 0:
            grads[section] = grad
            total = inner(upstream, message, mixing)

    scale = 1.0 / math.sqrt(total_rows * rows * columns)
    if splits:
        parcel, kept = pieces
        for (_, pairs), following in zip(splits, splits[1:]):
            got = lax.ppermute(parcel, AXES, pairs)
            half = (kept.shape[0] // 2, width)
            parcel, kept = call(
                functools.partial(halve_kernel, following[0]), [kept, got],
                [(half, BF16), (half, F32)], 0, scratch=[pltpu.VMEM(kept.shape, F32)],
            )
        got = lax.ppermute(parcel, AXES, splits[-1][1])
        result, summed = call(
            functools.partial(last_kernel, top, count, scale),
            [mask, total, *arrived, results[top], fetch_home(results, True), kept, got],
            [whole, (kept.shape, F32)], 0, jax.ShapeDtypeStruct,
        )
    else:
        summed = scale * lax.psum_scatter(pieces[0], ("tx", "ty"), scatter_dimension=0, tiled=True)
        result = call(
            functools.partial(last_kernel, top, count, None),
            [mask, total, *arrived, results[top], fetch_home(results, True)], [whole], 0,
            jax.ShapeDtypeStruct,
        )[0]
    return (summed[None], result.reshape(1, batches, 1, 1, nodes, width))


def solution(mesh):
    in_specs = (
        P("pipe", None, "tx", "ty", None, None),
        P(None, "tx", "ty", None, None),
        P("pipe", None, None),
        P(None, "tx", "ty", None, None, None, None),
        P(None, "tx", "ty", None, None, None, None),
        P(None, "tx", "ty", None, None),
        P(None, "tx", "ty", None),
    )
    out_specs = (P("pipe", ("tx", "ty"), None), P("pipe", None, "tx", "ty", None, None))
    return jax.shard_map(
        per_device, mesh=mesh, in_specs=in_specs, out_specs=out_specs, check_vma=False
    )
```

```python
import functools
import math

import jax
import jax.numpy as jnp
from jax import lax
from jax.experimental import pallas as pl
from jax.experimental.pallas import tpu as pltpu
from jax.sharding import PartitionSpec as P

AXES = ("pipe", "tx", "ty")
F32, BF16 = jnp.float32, jnp.bfloat16
IN_VMEM = pl.BlockSpec(memory_space=pltpu.VMEM)


def silu_slope(value):
    sigma = jax.nn.sigmoid(value)
    return sigma * (1.0 + value * (1.0 - sigma))


def swap_phases(count):
    phases = []
    for first in (0, 1):
        pairs = [(low, low + 1) for low in range(first, count - 1, 2)]
        if pairs:
            phases.append((first, pairs))
    return phases


def side(phase):
    axis, base, first, count = phase
    place = lax.axis_index(axis)
    is_low = lax.rem(place + first, 2) == 0
    return base, is_low, jnp.where(is_low, place < count - 1, place > 0)


def rows_dot(left, right):
    return lax.dot_general(left, right, (((1,), (0,)), ((), ())), preferred_element_type=F32)


def back_dot(left, right):
    return lax.dot_general(left, right, (((1,), (1,)), ((), ())), preferred_element_type=F32)


def send_blocks(grads, matrix, mixing_ref, message_ref, out_refs):
    batches, outgoing, nodes = mixing_ref.shape
    block = out_refs[0].shape[1]
    messages = back_dot(grads, matrix).astype(BF16)
    message_ref[...] = messages
    first = outgoing - block * len(out_refs)
    for batch in range(batches):
        mixed = rows_dot(
            mixing_ref[batch, first:, :], messages[batch * nodes : (batch + 1) * nodes]
        ).astype(BF16)
        for index, out_ref in enumerate(out_refs):
            out_ref[batch] = mixed[index * block : (index + 1) * block]


def first_kernel(phases, *refs):
    sources, refs = refs[:7], refs[7:]
    layer_ref, mixing_ref, mask_ref, grad_ref, message_ref = refs[:5]
    out_refs = refs[5 : 5 + len(phases)]
    held, sems = refs[5 + len(phases) : -1], refs[-1]
    copies = [
        pltpu.make_async_copy(source, target, sems.at[index])
        for index, (source, target) in enumerate(zip(sources, held))
    ]
    for copy in copies:
        copy.start()
    features_ref, matrix_ref, given_ref, pattern_ref, pick_ref, local_ref, halo_ref = held
    batches, blocks, _, block, _ = local_ref.shape
    sides = [side(phase) for phase in phases]
    copies[0].wait()
    copies[1].wait()
    pre_activation = rows_dot(features_ref[...], matrix_ref[...])
    slope = silu_slope(pre_activation).astype(BF16)
    layer_ref[0] = slope
    layer_ref[1] = matrix_ref[...]
    copies[2].wait()
    grads = (given_ref[...].astype(F32) * slope.astype(F32)).astype(BF16)
    grad_ref[...] = grads
    for copy in copies[3:]:
        copy.wait()
    for batch in range(batches):
        for source in range(blocks):
            columns = slice(source * block, (source + 1) * block)
            for target in range(blocks):
                present = pattern_ref[batch, source, target].astype(F32)
                edges = local_ref[batch, source, target].astype(F32) * present
                mixing_ref[batch, target * block : (target + 1) * block, columns] = edges.T.astype(BF16)
            for index, (base, is_low, _) in enumerate(sides):
                slot = jnp.where(is_low, base + 1, base)
                present = pattern_ref[batch, source, blocks + slot].astype(F32)
                edges = halo_ref[batch, slot, source].astype(F32) * present
                start = (blocks + index) * block
                mixing_ref[batch, start : start + block, columns] = edges.T.astype(BF16)
        for index, (base, is_low, paired) in enumerate(sides):
            chosen = pick_ref[batch, jnp.where(is_low, base, base + 1)]
            for target in range(blocks):
                here = ((chosen == target) & paired).astype(F32)
                entry = (batch * blocks + target) * len(sides) + index
                mask_ref[entry] = jnp.full(mask_ref.shape[1:], here, F32)
    send_blocks(grads, matrix_ref[...], mixing_ref, message_ref, out_refs)


def inner_kernel(upstream_ref, message_ref, mixing_ref, total_ref):
    batches, _, nodes = mixing_ref.shape
    for batch in range(batches):
        rows = slice(batch * nodes, (batch + 1) * nodes)
        total_ref[rows] = upstream_ref[rows].astype(F32) + rows_dot(
            mixing_ref[batch, :nodes, :], message_ref[rows]
        )


def turn_kernel(features_ref, turned_ref):
    turned_ref[...] = features_ref[...].T


def choose_kernel(top, top_ref, other_ref, chosen_ref):
    at_top = lax.axis_index("pipe") == top

    @pl.when(at_top)
    def _():
        chosen_ref[...] = top_ref[...]

    @pl.when(jnp.logical_not(at_top))
    def _():
        chosen_ref[...] = other_ref[...]


def close_blocks(mask_ref, total_ref, arrived_refs, result_ref):
    batches, block, _ = arrived_refs[0].shape
    count = len(arrived_refs)
    for batch in range(batches):
        arrived = [ref[batch].astype(F32) for ref in arrived_refs]
        for target in range(total_ref.shape[0] // batches // block):
            order = batch * (total_ref.shape[0] // batches // block) + target
            rows = slice(order * block, (order + 1) * block)
            value = total_ref[rows]
            for index in range(count):
                value = value + arrived[index] * mask_ref[order * count + index]
            result_ref[rows] = value.astype(BF16)


def close_kernel(mask_ref, total_ref, *refs):
    close_blocks(mask_ref, total_ref, refs[:-1], refs[-1])


def last_kernel(top, count, scale, mask_ref, total_ref, *refs):
    arrived_refs = refs[:count]
    top_ref, got_ref = refs[count : count + 2]
    result_ref = refs[-1]
    here = lax.axis_index("pipe")
    if scale is not None:
        kept_ref, piece_ref, result_ref, sum_ref = refs[count + 2 :]
        sum_ref[...] = (kept_ref[...] + piece_ref[...].astype(F32)) * scale

    @pl.when(here == 0)
    def _():
        close_blocks(mask_ref, total_ref, arrived_refs, result_ref)

    @pl.when(here == top)
    def _():
        result_ref[...] = top_ref[...]

    @pl.when((here != 0) & (here != top))
    def _():
        result_ref[...] = got_ref[...]


def step_kernel(layer_ref, mixing_ref, upstream_ref, grad_ref, message_ref, *out_refs):
    grads = (upstream_ref[...].astype(F32) * layer_ref[0].astype(F32)).astype(BF16)
    grad_ref[...] = grads
    send_blocks(grads, layer_ref[1], mixing_ref, message_ref, out_refs)


def close_step_kernel(count, mask_ref, total_ref, *refs):
    layer_ref, mixing_ref, result_ref, grad_ref, message_ref, *out_refs = refs[count:]
    close_blocks(mask_ref, total_ref, refs[:count], result_ref)
    step_kernel(layer_ref, mixing_ref, result_ref, grad_ref, message_ref, *out_refs)


def weight_product(top, turned_ref, grad_ref, top_ref, got_ref, product_ref):
    here = lax.axis_index("pipe")

    def product(ref):
        product_ref[...] = rows_dot(turned_ref[...], ref[...])

    @pl.when(here == 0)
    def _():
        product(grad_ref)

    @pl.when(here == top)
    def _():
        product(top_ref)

    @pl.when((here != 0) & (here != top))
    def _():
        product(got_ref)


def split_halves(steps, product_ref, sent_ref, kept_ref):
    def split(axis, distance, groups):
        size = kept_ref.shape[0] // groups
        place = lax.rem(lax.axis_index(axis) // distance, 2)
        for group in range(groups):
            start = 2 * group * size
            rows = slice(group * size, (group + 1) * size)
            kept = pl.ds(pl.multiple_of(start + place * size, size), size)
            sent = pl.ds(pl.multiple_of(start + (1 - place) * size, size), size)
            kept_ref[rows] = product_ref[kept]
            sent_ref[rows] = product_ref[sent].astype(BF16)

    if steps[0] == steps[1]:
        split(*steps[0])
    else:
        odd = lax.rem(lax.axis_index("pipe"), 2) == 1

        @pl.when(odd)
        def _():
            split(*steps[1])

        @pl.when(jnp.logical_not(odd))
        def _():
            split(*steps[0])


def halve_kernel(step, kept_ref, got_ref, sent_ref, next_ref, sum_ref):
    sum_ref[...] = kept_ref[...] + got_ref[...].astype(F32)
    split_halves(step, sum_ref, sent_ref, next_ref)


def bottom_kernel(count, top, step, mask_ref, total_ref, *refs):
    turned_ref, top_ref, got_ref, layer_ref, mixing_ref = refs[count : count + 5]
    result_ref, next_ref = refs[count + 5 : count + 7]
    out_refs = refs[count + 7 : 2 * count + 7]
    grad_ref, message_ref = refs[-2:]
    close_step_kernel(
        count, mask_ref, total_ref, *refs[:count], layer_ref, mixing_ref,
        result_ref, grad_ref, message_ref, *out_refs
    )
    if step is None:
        weight_product(top, turned_ref, grad_ref, top_ref, got_ref, refs[2 * count + 7])
    else:
        sent_ref, kept_ref, product_ref = refs[2 * count + 7 : -2]
        weight_product(top, turned_ref, grad_ref, top_ref, got_ref, product_ref)
        split_halves(step, product_ref, sent_ref, kept_ref)
    inner_kernel(result_ref, message_ref, mixing_ref, next_ref)


def call(body, inputs, outputs, flops, kind=pltpu.VMEM, source=IN_VMEM, scratch=()):
    size = sum(math.prod(shape) * jnp.dtype(dtype).itemsize for shape, dtype in outputs)
    size += sum(value.size * value.dtype.itemsize for value in inputs)
    return pl.pallas_call(
        body,
        out_shape=[kind(shape, dtype) for shape, dtype in outputs],
        in_specs=[source] * len(inputs),
        out_specs=[IN_VMEM] * len(outputs),
        scratch_shapes=scratch,
        compiler_params=pltpu.CompilerParams(vmem_limit_bytes=16 * 1024 * 1024),
        cost_estimate=pl.CostEstimate(flops=flops, bytes_accessed=size, transcendentals=0),
    )(*inputs)


def per_device(stored, cotangent, weight, local_edges, halo_edges, pattern, pick):
    sections, rows, columns = (lax.axis_size(name) for name in AXES)
    here = lax.axis_index("pipe")
    lower = sections // 2
    upper = sections - lower
    top = sections - 1

    def flat(section, x, y):
        return (section * rows + x) * columns + y

    def to_sections(value, moves, back=True):
        if back:
            moves = moves + [(target, source) for source, target in moves]
        pairs = [
            (flat(source, x, y), flat(target, x, y))
            for source, target in moves
            for x in range(rows)
            for y in range(columns)
        ]
        return lax.ppermute(value, AXES, pairs)

    def tile_swaps(axis, couples, lead):
        places = {}
        for low, high in couples:
            places[low], places[high] = high, low
        others = [p for p in range(sections) if p != lead]
        buddy, inner, outer = lead ^ 1, 3 - (lead ^ 1), 3 - lead
        pairs = []
        for x in range(rows):
            for y in range(columns):
                place = x if axis == "tx" else y
                paired = place in places
                facing = places.get(place, place)
                near = (facing, y) if axis == "tx" else (x, facing)
                aside = (x, y ^ 1) if axis == "tx" else (x ^ 1, y)
                if aside[0] >= rows or aside[1] >= columns:
                    aside = (x, y)
                moves = {}
                if paired or sections != 4:
                    moves[lead] = (lead, near)
                if sections != 4:
                    moves.update((p, (q, (x, y))) for p, q in zip(others, others[1:] + others[:1]))
                elif paired:
                    moves.update({buddy: (inner, (x, y)), inner: (buddy, (x, y)), outer: (outer, aside)})
                else:
                    for p, q in ((lead, buddy), (inner, outer)):
                        moves.update({p: (q, (x, y)), q: (p, (x, y))})
                pairs += [(flat(p, x, y), flat(q, *tile)) for p, (q, tile) in moves.items()]
        return pairs

    batches, nodes, width = stored.shape[1], stored.shape[4], stored.shape[5]
    blocks, block = local_edges.shape[3], local_edges.shape[5]
    total_rows = batches * nodes
    features = stored.reshape(total_rows, width)
    matrix = weight[0]
    picks = pick[:, 0, 0]

    phases, routes = [], []
    for axis, base, count in (("tx", 0, rows), ("ty", 2, columns)):
        for first, couples in swap_phases(count):
            phases.append((axis, base, first, count))
            route = {lead: tile_swaps(axis, couples, lead) for lead in {0, top}}
            routes.append(route)
    phases = tuple(phases)
    splits, left = [], rows * columns
    if left & (left - 1) == 0 and width // left % 16 == 0:
        along = {"tx": [], "ty": []}
        for axis, count in (("tx", rows), ("ty", columns)):
            while 1 << len(along[axis]) < count:
                along[axis].append((axis, 1 << len(along[axis])))
        orders = [
            along["ty"][::-1] + along["tx"], along["tx"][:1] + along["ty"][::-1] + along["tx"][1:]
        ]
        levels = [along["tx"][::-1] + along["ty"][::-1] for _ in orders]
        for index in range(len(orders[0])):
            steps, pairs = [], []
            for order, level in zip(orders, levels):
                steps.append((*order[index], 1 << level.index(order[index])))
                level.remove(order[index])
            for p in range(sections):
                axis, distance, _ = steps[p % 2]
                pairs += [
                    (flat(p, x, y), flat(p, x, y ^ distance) if axis == "ty" else flat(p, x ^ distance, y))
                    for x in range(rows)
                    for y in range(columns)
                ]
            splits.append((tuple(steps), pairs))
    sent = [((batches, block, width), BF16)] * len(phases)
    whole = ((total_rows, width), BF16)
    mix_rows = (blocks + len(phases)) * block
    cost = 2 * total_rows * width * (width + len(phases) * block)

    def exchange(outs, lead):
        return [lax.ppermute(out, AXES, route[lead]) for out, route in zip(outs, routes)]

    def inner(upstream, message, mixing):
        return call(
            inner_kernel, [upstream, message, mixing], [((total_rows, width), F32)],
            2 * total_rows * width * nodes,
        )[0]

    given = cotangent.reshape(total_rows, width)
    operands = [
        features, matrix, given, pattern[:, 0, 0], picks, local_edges[:, 0, 0], halo_edges[:, 0, 0]
    ]
    layer, mixing, mask, grad, message, *outs = call(
        functools.partial(first_kernel, phases),
        [pltpu.with_memory_space_constraint(value, pltpu.HBM) for value in operands],
        [
            ((2, total_rows, width), BF16), ((batches, mix_rows, nodes), BF16),
            ((batches * blocks * len(phases), 1, width), F32), whole, whole,
        ] + sent,
        cost + 2 * total_rows * width * width,
        source=pl.BlockSpec(memory_space=pltpu.HBM),
        scratch=[
            (pltpu.VMEM if value.dtype == BF16 else pltpu.SMEM)(value.shape, value.dtype)
            for value in operands
        ] + [pltpu.SemaphoreType.DMA((len(operands),))],
    )
    arrived = exchange(outs, top)
    total = inner(given, message, mixing)
    turned = call(turn_kernel, [features], [((width, total_rows), BF16)], 0)[0]

    layers = [layer]
    for step in range(1, upper):
        moves = [(top - step, top)] + ([(step, 0)] if step < lower else [])
        layers.append(to_sections(layer, moves))

    def fetch_home(values):
        got = None
        for step in range(1, upper):
            moves = [(top, top - step)]
            value = values[top - step]
            if step < lower:
                moves.append((0, step))
                value = call(
                    functools.partial(choose_kernel, top), [value, values[step]], [whole], 0
                )[0]
            new = to_sections(value, moves)
            takes = here == top - step
            if step < lower:
                takes = takes | (here == step)
            got = new if step == 1 else jnp.where(takes, new, got)
        return got

    count = len(phases)
    grads, results = {top: grad}, {}
    for section in reversed(range(top)):
        lead = top if section >= lower else 0
        steps = top - section if section >= lower else section
        layer_here = layers[steps]
        if section == lower - 1:
            upstream = call(close_kernel, [mask, total, *arrived], [whole], 0)[0]
            results[section + 1] = upstream
            upstream = to_sections(upstream, [(top, 0)], False)
            grad, message, *outs = call(
                step_kernel, [layer_here, mixing, upstream], [whole, whole] + sent, cost
            )
        elif section > 0:
            upstream, grad, message, *outs = call(
                functools.partial(close_step_kernel, count),
                [mask, total, *arrived, layer_here, mixing],
                [whole, whole, whole] + sent, cost,
            )
            results[section + 1] = upstream
        else:
            product = ((width, width), F32)
            halves = [((width // 2, width), BF16), ((width // 2, width), F32)] if splits else [product]
            upstream, total, *outs = call(
                functools.partial(bottom_kernel, count, top, splits[0][0] if splits else None),
                [mask, total, *arrived, turned, grads[top], fetch_home(grads), layer_here, mixing],
                [whole, ((total_rows, width), F32)] + sent + halves,
                cost + 2 * total_rows * width * (width + nodes),
                scratch=[pltpu.VMEM(*product)] * len(splits[:1]) + [pltpu.VMEM(*whole)] * 2,
            )
            outs, pieces = outs[:count], outs[count:]
            results[1] = upstream
        arrived = exchange(outs, lead)
        if section > 0:
            grads[section] = grad
            total = inner(upstream, message, mixing)

    scale = 1.0 / math.sqrt(total_rows * rows * columns)
    if splits:
        parcel, kept = pieces
        for (_, pairs), following in zip(splits, splits[1:]):
            got = lax.ppermute(parcel, AXES, pairs)
            half = (kept.shape[0] // 2, width)
            parcel, kept = call(
                functools.partial(halve_kernel, following[0]), [kept, got],
                [(half, BF16), (half, F32)], 0, scratch=[pltpu.VMEM(kept.shape, F32)],
            )
        got = lax.ppermute(parcel, AXES, splits[-1][1])
        result, summed = call(
            functools.partial(last_kernel, top, count, scale),
            [mask, total, *arrived, results[top], fetch_home(results), kept, got],
            [whole, (kept.shape, F32)], 0, jax.ShapeDtypeStruct,
        )
    else:
        summed = scale * lax.psum_scatter(pieces[0], ("tx", "ty"), scatter_dimension=0, tiled=True)
        result = call(
            functools.partial(last_kernel, top, count, None),
            [mask, total, *arrived, results[top], fetch_home(results)], [whole], 0,
            jax.ShapeDtypeStruct,
        )[0]
    return (summed[None], result.reshape(1, batches, 1, 1, nodes, width))


def solution(mesh):
    in_specs = (
        P("pipe", None, "tx", "ty", None, None),
        P(None, "tx", "ty", None, None),
        P("pipe", None, None),
        P(None, "tx", "ty", None, None, None, None),
        P(None, "tx", "ty", None, None, None, None),
        P(None, "tx", "ty", None, None),
        P(None, "tx", "ty", None),
    )
    out_specs = (P("pipe", ("tx", "ty"), None), P("pipe", None, "tx", "ty", None, None))
    return jax.shard_map(
        per_device, mesh=mesh, in_specs=in_specs, out_specs=out_specs, check_vma=False
    )
```

```python
import functools
import math

import jax
import jax.numpy as jnp
from jax import lax
from jax.experimental import pallas as pl
from jax.experimental.pallas import tpu as pltpu
from jax.sharding import PartitionSpec as P

AXES = ("pipe", "tx", "ty")
F32, BF16 = jnp.float32, jnp.bfloat16
IN_VMEM = pl.BlockSpec(memory_space=pltpu.VMEM)


def silu_slope(value):
    sigma = jax.nn.sigmoid(value)
    return sigma * (1.0 + value * (1.0 - sigma))


def swap_phases(count):
    phases = []
    for first in (0, 1):
        pairs = [(low, low + 1) for low in range(first, count - 1, 2)]
        if pairs:
            phases.append((first, pairs))
    return phases


def side(phase):
    axis, base, first, count = phase
    place = lax.axis_index(axis)
    is_low = lax.rem(place + first, 2) == 0
    return base, is_low, jnp.where(is_low, place < count - 1, place > 0)


def rows_dot(left, right):
    return lax.dot_general(left, right, (((1,), (0,)), ((), ())), preferred_element_type=F32)


def back_dot(left, right):
    return lax.dot_general(left, right, (((1,), (1,)), ((), ())), preferred_element_type=F32)


def send_blocks(grads, matrix, mixing_ref, message_ref, out_refs):
    batches, outgoing, nodes = mixing_ref.shape
    block = out_refs[0].shape[1]
    messages = back_dot(grads, matrix).astype(BF16)
    message_ref[...] = messages
    first = outgoing - block * len(out_refs)
    for batch in range(batches):
        mixed = rows_dot(
            mixing_ref[batch, first:, :], messages[batch * nodes : (batch + 1) * nodes]
        ).astype(BF16)
        for index, out_ref in enumerate(out_refs):
            out_ref[batch] = mixed[index * block : (index + 1) * block]


def first_kernel(phases, *refs):
    sources, refs = refs[:7], refs[7:]
    layer_ref, mixing_ref, mask_ref, grad_ref, message_ref = refs[:5]
    out_refs = refs[5 : 5 + len(phases)]
    held, sems = refs[5 + len(phases) : -1], refs[-1]
    copies = [
        pltpu.make_async_copy(source, target, sems.at[index])
        for index, (source, target) in enumerate(zip(sources, held))
    ]
    for copy in copies:
        copy.start()
    features_ref, matrix_ref, given_ref, pattern_ref, pick_ref, local_ref, halo_ref = held
    batches, blocks, _, block, _ = local_ref.shape
    sides = [side(phase) for phase in phases]
    copies[0].wait()
    copies[1].wait()
    pre_activation = rows_dot(features_ref[...], matrix_ref[...])
    slope = silu_slope(pre_activation).astype(BF16)
    layer_ref[0] = slope
    layer_ref[1] = matrix_ref[...]
    copies[2].wait()
    grads = (given_ref[...].astype(F32) * slope.astype(F32)).astype(BF16)
    grad_ref[...] = grads
    for copy in copies[3:]:
        copy.wait()
    for batch in range(batches):
        for source in range(blocks):
            columns = slice(source * block, (source + 1) * block)
            for target in range(blocks):
                present = pattern_ref[batch, source, target].astype(F32)
                edges = local_ref[batch, source, target].astype(F32) * present
                mixing_ref[batch, target * block : (target + 1) * block, columns] = edges.T.astype(BF16)
            for index, (base, is_low, _) in enumerate(sides):
                slot = jnp.where(is_low, base + 1, base)
                present = pattern_ref[batch, source, blocks + slot].astype(F32)
                edges = halo_ref[batch, slot, source].astype(F32) * present
                start = (blocks + index) * block
                mixing_ref[batch, start : start + block, columns] = edges.T.astype(BF16)
        for index, (base, is_low, paired) in enumerate(sides):
            chosen = pick_ref[batch, jnp.where(is_low, base, base + 1)]
            for target in range(blocks):
                here = ((chosen == target) & paired).astype(F32)
                entry = (batch * blocks + target) * len(sides) + index
                mask_ref[entry] = jnp.full(mask_ref.shape[1:], here, F32)
    send_blocks(grads, matrix_ref[...], mixing_ref, message_ref, out_refs)


def inner_kernel(upstream_ref, message_ref, mixing_ref, total_ref):
    batches, _, nodes = mixing_ref.shape
    for batch in range(batches):
        rows = slice(batch * nodes, (batch + 1) * nodes)
        total_ref[rows] = upstream_ref[rows].astype(F32) + rows_dot(
            mixing_ref[batch, :nodes, :], message_ref[rows]
        )


def turn_kernel(features_ref, turned_ref):
    turned_ref[...] = features_ref[...].T


def choose_kernel(top, top_ref, other_ref, chosen_ref):
    at_top = lax.axis_index("pipe") == top

    @pl.when(at_top)
    def _():
        chosen_ref[...] = top_ref[...]

    @pl.when(jnp.logical_not(at_top))
    def _():
        chosen_ref[...] = other_ref[...]


def close_blocks(mask_ref, total_ref, arrived_refs, result_ref):
    batches, block, _ = arrived_refs[0].shape
    count = len(arrived_refs)
    for batch in range(batches):
        arrived = [ref[batch].astype(F32) for ref in arrived_refs]
        for target in range(total_ref.shape[0] // batches // block):
            order = batch * (total_ref.shape[0] // batches // block) + target
            rows = slice(order * block, (order + 1) * block)
            value = total_ref[rows]
            for index in range(count):
                value = value + arrived[index] * mask_ref[order * count + index]
            result_ref[rows] = value.astype(BF16)


def close_kernel(mask_ref, total_ref, *refs):
    close_blocks(mask_ref, total_ref, refs[:-1], refs[-1])


def last_kernel(top, count, scale, mask_ref, total_ref, *refs):
    arrived_refs = refs[:count]
    top_ref, got_ref = refs[count : count + 2]
    result_ref = refs[-1]
    here = lax.axis_index("pipe")
    if scale is not None:
        kept_ref, piece_ref, result_ref, sum_ref = refs[count + 2 :]
        sum_ref[...] = (kept_ref[...] + piece_ref[...].astype(F32)) * scale

    @pl.when(here == 0)
    def _():
        close_blocks(mask_ref, total_ref, arrived_refs, result_ref)

    @pl.when(here == top)
    def _():
        result_ref[...] = top_ref[...]

    @pl.when((here != 0) & (here != top))
    def _():
        result_ref[...] = got_ref[...]


def step_kernel(layer_ref, mixing_ref, upstream_ref, grad_ref, message_ref, *out_refs):
    grads = (upstream_ref[...].astype(F32) * layer_ref[0].astype(F32)).astype(BF16)
    grad_ref[...] = grads
    send_blocks(grads, layer_ref[1], mixing_ref, message_ref, out_refs)


def close_step_kernel(count, mask_ref, total_ref, *refs):
    layer_ref, mixing_ref, result_ref, grad_ref, message_ref, *out_refs = refs[count:]
    close_blocks(mask_ref, total_ref, refs[:count], result_ref)
    step_kernel(layer_ref, mixing_ref, result_ref, grad_ref, message_ref, *out_refs)


def weight_product(top, turned_ref, grad_ref, top_ref, got_ref, product_ref):
    here = lax.axis_index("pipe")

    def product(ref):
        product_ref[...] = rows_dot(turned_ref[...], ref[...])

    @pl.when(here == 0)
    def _():
        product(grad_ref)

    @pl.when(here == top)
    def _():
        product(top_ref)

    @pl.when((here != 0) & (here != top))
    def _():
        product(got_ref)


def split_halves(steps, product_ref, sent_ref, kept_ref):
    def split(axis, distance, groups):
        size = kept_ref.shape[0] // groups
        place = lax.rem(lax.axis_index(axis) // distance, 2)
        for group in range(groups):
            start = 2 * group * size
            rows = slice(group * size, (group + 1) * size)
            kept = pl.ds(pl.multiple_of(start + place * size, size), size)
            sent = pl.ds(pl.multiple_of(start + (1 - place) * size, size), size)
            kept_ref[rows] = product_ref[kept]
            sent_ref[rows] = product_ref[sent].astype(BF16)

    if steps[0] == steps[1]:
        split(*steps[0])
    else:
        odd = lax.rem(lax.axis_index("pipe"), 2) == 1

        @pl.when(odd)
        def _():
            split(*steps[1])

        @pl.when(jnp.logical_not(odd))
        def _():
            split(*steps[0])


def halve_kernel(step, kept_ref, got_ref, sent_ref, next_ref, sum_ref):
    sum_ref[...] = kept_ref[...] + got_ref[...].astype(F32)
    split_halves(step, sum_ref, sent_ref, next_ref)


def bottom_kernel(count, top, step, mask_ref, total_ref, *refs):
    turned_ref, top_ref, got_ref, layer_ref, mixing_ref = refs[count : count + 5]
    result_ref, next_ref = refs[count + 5 : count + 7]
    out_refs = refs[count + 7 : 2 * count + 7]
    grad_ref, message_ref = refs[-2:]
    close_step_kernel(
        count, mask_ref, total_ref, *refs[:count], layer_ref, mixing_ref,
        result_ref, grad_ref, message_ref, *out_refs
    )
    if step is None:
        weight_product(top, turned_ref, grad_ref, top_ref, got_ref, refs[2 * count + 7])
    else:
        sent_ref, kept_ref, product_ref = refs[2 * count + 7 : -2]
        weight_product(top, turned_ref, grad_ref, top_ref, got_ref, product_ref)
        split_halves(step, product_ref, sent_ref, kept_ref)
    inner_kernel(result_ref, message_ref, mixing_ref, next_ref)


def call(body, inputs, outputs, flops, kind=pltpu.VMEM, source=IN_VMEM, scratch=()):
    size = sum(math.prod(shape) * jnp.dtype(dtype).itemsize for shape, dtype in outputs)
    size += sum(value.size * value.dtype.itemsize for value in inputs)
    return pl.pallas_call(
        body,
        out_shape=[kind(shape, dtype) for shape, dtype in outputs],
        in_specs=[source] * len(inputs),
        out_specs=[IN_VMEM] * len(outputs),
        scratch_shapes=scratch,
        compiler_params=pltpu.CompilerParams(vmem_limit_bytes=16 * 1024 * 1024),
        cost_estimate=pl.CostEstimate(flops=flops, bytes_accessed=size, transcendentals=0),
    )(*inputs)


def per_device(stored, cotangent, weight, local_edges, halo_edges, pattern, pick):
    sections, rows, columns = (lax.axis_size(name) for name in AXES)
    here = lax.axis_index("pipe")
    lower = sections // 2
    upper = sections - lower
    top = sections - 1

    def flat(section, x, y):
        return (section * rows + x) * columns + y

    def to_sections(value, moves, back=True):
        if back:
            moves = moves + [(target, source) for source, target in moves]
        pairs = [
            (flat(source, x, y), flat(target, x, y))
            for source, target in moves
            for x in range(rows)
            for y in range(columns)
        ]
        return lax.ppermute(value, AXES, pairs)

    def tile_swaps(axis, first, couples, lead):
        places = {}
        for low, high in couples:
            places[low], places[high] = high, low
        others = [p for p in range(sections) if p != lead]
        buddy, inner, outer = lead ^ 1, 3 - (lead ^ 1), 3 - lead
        pairs = []
        for x in range(rows):
            for y in range(columns):
                place = x if axis == "tx" else y
                paired = place in places
                facing = places.get(place, place)
                near = (facing, y) if axis == "tx" else (x, facing)
                aside = (x, y ^ 1) if columns % 2 == 0 else (x, y)
                moves = {}
                if paired or sections != 4:
                    moves[lead] = (lead, near)
                if sections != 4:
                    moves.update((p, (q, (x, y))) for p, q in zip(others, others[1:] + others[:1]))
                elif paired and axis == "tx" and first == 0 and aside != (x, y):
                    moves.update({buddy: (buddy, aside), inner: (outer, (x, y)), outer: (inner, (x, y))})
                elif paired:
                    moves.update({buddy: (inner, (x, y)), inner: (buddy, (x, y)), outer: (outer, near)})
                else:
                    for p, q in ((lead, buddy), (inner, outer)):
                        moves.update({p: (q, (x, y)), q: (p, (x, y))})
                pairs += [(flat(p, x, y), flat(q, *tile)) for p, (q, tile) in moves.items()]
        return pairs

    batches, nodes, width = stored.shape[1], stored.shape[4], stored.shape[5]
    blocks, block = local_edges.shape[3], local_edges.shape[5]
    total_rows = batches * nodes
    features = stored.reshape(total_rows, width)
    matrix = weight[0]
    picks = pick[:, 0, 0]

    phases, routes = [], []
    for axis, base, count in (("tx", 0, rows), ("ty", 2, columns)):
        for first, couples in swap_phases(count):
            phases.append((axis, base, first, count))
            route = {lead: tile_swaps(axis, first, couples, lead) for lead in {0, top}}
            routes.append(route)
    phases = tuple(phases)
    splits, left = [], rows * columns
    if left & (left - 1) == 0 and width // left % 16 == 0:
        along = {"tx": [], "ty": []}
        for axis, count in (("tx", rows), ("ty", columns)):
            while 1 << len(along[axis]) < count:
                along[axis].append((axis, 1 << len(along[axis])))
        orders = [
            along["ty"][::-1] + along["tx"], along["tx"][:1] + along["ty"][::-1] + along["tx"][1:]
        ]
        levels = [along["tx"][::-1] + along["ty"][::-1] for _ in orders]
        for index in range(len(orders[0])):
            steps, pairs = [], []
            for order, level in zip(orders, levels):
                steps.append((*order[index], 1 << level.index(order[index])))
                level.remove(order[index])
            for p in range(sections):
                axis, distance, _ = steps[p % 2]
                pairs += [
                    (flat(p, x, y), flat(p, x, y ^ distance) if axis == "ty" else flat(p, x ^ distance, y))
                    for x in range(rows)
                    for y in range(columns)
                ]
            splits.append((tuple(steps), pairs))
    sent = [((batches, block, width), BF16)] * len(phases)
    whole = ((total_rows, width), BF16)
    mix_rows = (blocks + len(phases)) * block
    cost = 2 * total_rows * width * (width + len(phases) * block)

    def exchange(outs, lead):
        return [lax.ppermute(out, AXES, route[lead]) for out, route in zip(outs, routes)]

    def inner(upstream, message, mixing):
        return call(
            inner_kernel, [upstream, message, mixing], [((total_rows, width), F32)],
            2 * total_rows * width * nodes,
        )[0]

    given = cotangent.reshape(total_rows, width)
    operands = [
        features, matrix, given, pattern[:, 0, 0], picks, local_edges[:, 0, 0], halo_edges[:, 0, 0]
    ]
    layer, mixing, mask, grad, message, *outs = call(
        functools.partial(first_kernel, phases),
        [pltpu.with_memory_space_constraint(value, pltpu.HBM) for value in operands],
        [
            ((2, total_rows, width), BF16), ((batches, mix_rows, nodes), BF16),
            ((batches * blocks * len(phases), 1, width), F32), whole, whole,
        ] + sent,
        cost + 2 * total_rows * width * width,
        source=pl.BlockSpec(memory_space=pltpu.HBM),
        scratch=[
            (pltpu.VMEM if value.dtype == BF16 else pltpu.SMEM)(value.shape, value.dtype)
            for value in operands
        ] + [pltpu.SemaphoreType.DMA((len(operands),))],
    )
    arrived = exchange(outs, top)
    total = inner(given, message, mixing)
    turned = call(turn_kernel, [features], [((width, total_rows), BF16)], 0)[0]

    layers = [layer]
    for step in range(1, upper):
        moves = [(top - step, top)] + ([(step, 0)] if step < lower else [])
        layers.append(to_sections(layer, moves))

    def fetch_home(values):
        got = None
        for step in range(1, upper):
            moves = [(top, top - step)]
            value = values[top - step]
            if step < lower:
                moves.append((0, step))
                value = call(
                    functools.partial(choose_kernel, top), [value, values[step]], [whole], 0
                )[0]
            new = to_sections(value, moves)
            takes = here == top - step
            if step < lower:
                takes = takes | (here == step)
            got = new if step == 1 else jnp.where(takes, new, got)
        return got

    count = len(phases)
    grads, results = {top: grad}, {}
    for section in reversed(range(top)):
        lead = top if section >= lower else 0
        steps = top - section if section >= lower else section
        layer_here = layers[steps]
        if section == lower - 1:
            upstream = call(close_kernel, [mask, total, *arrived], [whole], 0)[0]
            results[section + 1] = upstream
            upstream = to_sections(upstream, [(top, 0)], False)
            grad, message, *outs = call(
                step_kernel, [layer_here, mixing, upstream], [whole, whole] + sent, cost
            )
        elif section > 0:
            upstream, grad, message, *outs = call(
                functools.partial(close_step_kernel, count),
                [mask, total, *arrived, layer_here, mixing],
                [whole, whole, whole] + sent, cost,
            )
            results[section + 1] = upstream
        else:
            product = ((width, width), F32)
            halves = [((width // 2, width), BF16), ((width // 2, width), F32)] if splits else [product]
            upstream, total, *outs = call(
                functools.partial(bottom_kernel, count, top, splits[0][0] if splits else None),
                [mask, total, *arrived, turned, grads[top], fetch_home(grads), layer_here, mixing],
                [whole, ((total_rows, width), F32)] + sent + halves,
                cost + 2 * total_rows * width * (width + nodes),
                scratch=[pltpu.VMEM(*product)] * len(splits[:1]) + [pltpu.VMEM(*whole)] * 2,
            )
            outs, pieces = outs[:count], outs[count:]
            results[1] = upstream
        arrived = exchange(outs, lead)
        if section > 0:
            grads[section] = grad
            total = inner(upstream, message, mixing)

    scale = 1.0 / math.sqrt(total_rows * rows * columns)
    if splits:
        parcel, kept = pieces
        for (_, pairs), following in zip(splits, splits[1:]):
            got = lax.ppermute(parcel, AXES, pairs)
            half = (kept.shape[0] // 2, width)
            parcel, kept = call(
                functools.partial(halve_kernel, following[0]), [kept, got],
                [(half, BF16), (half, F32)], 0, scratch=[pltpu.VMEM(kept.shape, F32)],
            )
        got = lax.ppermute(parcel, AXES, splits[-1][1])
        result, summed = call(
            functools.partial(last_kernel, top, count, scale),
            [mask, total, *arrived, results[top], fetch_home(results), kept, got],
            [whole, (kept.shape, F32)], 0, jax.ShapeDtypeStruct,
        )
    else:
        summed = scale * lax.psum_scatter(pieces[0], ("tx", "ty"), scatter_dimension=0, tiled=True)
        result = call(
            functools.partial(last_kernel, top, count, None),
            [mask, total, *arrived, results[top], fetch_home(results)], [whole], 0,
            jax.ShapeDtypeStruct,
        )[0]
    return (summed[None], result.reshape(1, batches, 1, 1, nodes, width))


def solution(mesh):
    in_specs = (
        P("pipe", None, "tx", "ty", None, None),
        P(None, "tx", "ty", None, None),
        P("pipe", None, None),
        P(None, "tx", "ty", None, None, None, None),
        P(None, "tx", "ty", None, None, None, None),
        P(None, "tx", "ty", None, None),
        P(None, "tx", "ty", None),
    )
    out_specs = (P("pipe", ("tx", "ty"), None), P("pipe", None, "tx", "ty", None, None))
    return jax.shard_map(
        per_device, mesh=mesh, in_specs=in_specs, out_specs=out_specs, check_vma=False
    )
```

```python
import functools
import math

import jax
import jax.numpy as jnp
from jax import lax
from jax.experimental import pallas as pl
from jax.experimental.pallas import tpu as pltpu
from jax.sharding import PartitionSpec as P

AXES = ("pipe", "tx", "ty")
F32, BF16 = jnp.float32, jnp.bfloat16
IN_VMEM = pl.BlockSpec(memory_space=pltpu.VMEM)


def silu_slope(value):
    sigma = jax.nn.sigmoid(value)
    return sigma * (1.0 + value * (1.0 - sigma))


def swap_phases(count):
    phases = []
    for first in (0, 1):
        pairs = [(low, low + 1) for low in range(first, count - 1, 2)]
        if pairs:
            phases.append((first, pairs))
    return phases


def side(phase):
    axis, base, first, count = phase
    place = lax.axis_index(axis)
    is_low = lax.rem(place + first, 2) == 0
    return base, is_low, jnp.where(is_low, place < count - 1, place > 0)


def rows_dot(left, right):
    return lax.dot_general(left, right, (((1,), (0,)), ((), ())), preferred_element_type=F32)


def back_dot(left, right):
    return lax.dot_general(left, right, (((1,), (1,)), ((), ())), preferred_element_type=F32)


def send_blocks(grads, matrix, mixing_ref, message_ref, out_refs):
    batches, outgoing, nodes = mixing_ref.shape
    block = out_refs[0].shape[1]
    messages = back_dot(grads, matrix).astype(BF16)
    message_ref[...] = messages
    first = outgoing - block * len(out_refs)
    for batch in range(batches):
        mixed = rows_dot(
            mixing_ref[batch, first:, :], messages[batch * nodes : (batch + 1) * nodes]
        ).astype(BF16)
        for index, out_ref in enumerate(out_refs):
            out_ref[batch] = mixed[index * block : (index + 1) * block]


def first_kernel(phases, *refs):
    sources, refs = refs[:7], refs[7:]
    layer_ref, mixing_ref, mask_ref, grad_ref, message_ref = refs[:5]
    out_refs = refs[5 : 5 + len(phases)]
    held, sems = refs[5 + len(phases) : -1], refs[-1]
    copies = [
        pltpu.make_async_copy(source, target, sems.at[index])
        for index, (source, target) in enumerate(zip(sources, held))
    ]
    for copy in copies:
        copy.start()
    features_ref, matrix_ref, given_ref, pattern_ref, pick_ref, local_ref, halo_ref = held
    batches, blocks, _, block, _ = local_ref.shape
    sides = [side(phase) for phase in phases]
    copies[0].wait()
    copies[1].wait()
    pre_activation = rows_dot(features_ref[...], matrix_ref[...])
    slope = silu_slope(pre_activation).astype(BF16)
    layer_ref[0] = slope
    layer_ref[1] = matrix_ref[...]
    copies[2].wait()
    grads = (given_ref[...].astype(F32) * slope.astype(F32)).astype(BF16)
    grad_ref[...] = grads
    for copy in copies[3:]:
        copy.wait()
    for batch in range(batches):
        for source in range(blocks):
            columns = slice(source * block, (source + 1) * block)
            for target in range(blocks):
                present = pattern_ref[batch, source, target].astype(F32)
                edges = local_ref[batch, source, target].astype(F32) * present
                mixing_ref[batch, target * block : (target + 1) * block, columns] = edges.T.astype(BF16)
            for index, (base, is_low, _) in enumerate(sides):
                slot = jnp.where(is_low, base + 1, base)
                present = pattern_ref[batch, source, blocks + slot].astype(F32)
                edges = halo_ref[batch, slot, source].astype(F32) * present
                start = (blocks + index) * block
                mixing_ref[batch, start : start + block, columns] = edges.T.astype(BF16)
        for index, (base, is_low, paired) in enumerate(sides):
            chosen = pick_ref[batch, jnp.where(is_low, base, base + 1)]
            for target in range(blocks):
                here = ((chosen == target) & paired).astype(F32)
                entry = (batch * blocks + target) * len(sides) + index
                mask_ref[entry] = jnp.full(mask_ref.shape[1:], here, F32)
    send_blocks(grads, matrix_ref[...], mixing_ref, message_ref, out_refs)


def inner_kernel(upstream_ref, message_ref, mixing_ref, total_ref):
    batches, _, nodes = mixing_ref.shape
    for batch in range(batches):
        rows = slice(batch * nodes, (batch + 1) * nodes)
        total_ref[rows] = upstream_ref[rows].astype(F32) + rows_dot(
            mixing_ref[batch, :nodes, :], message_ref[rows]
        )


def turn_kernel(features_ref, turned_ref):
    turned_ref[...] = features_ref[...].T


def choose_kernel(top, top_ref, other_ref, chosen_ref):
    at_top = lax.axis_index("pipe") == top

    @pl.when(at_top)
    def _():
        chosen_ref[...] = top_ref[...]

    @pl.when(jnp.logical_not(at_top))
    def _():
        chosen_ref[...] = other_ref[...]


def close_blocks(mask_ref, total_ref, arrived_refs, result_ref):
    batches, block, _ = arrived_refs[0].shape
    count = len(arrived_refs)
    for batch in range(batches):
        arrived = [ref[batch].astype(F32) for ref in arrived_refs]
        for target in range(total_ref.shape[0] // batches // block):
            order = batch * (total_ref.shape[0] // batches // block) + target
            rows = slice(order * block, (order + 1) * block)
            value = total_ref[rows]
            for index in range(count):
                value = value + arrived[index] * mask_ref[order * count + index]
            result_ref[rows] = value.astype(BF16)


def close_kernel(mask_ref, total_ref, *refs):
    close_blocks(mask_ref, total_ref, refs[:-1], refs[-1])


def last_kernel(top, count, scale, mask_ref, total_ref, *refs):
    arrived_refs = refs[:count]
    top_ref, got_ref = refs[count : count + 2]
    result_ref = refs[-1]
    here = lax.axis_index("pipe")
    if scale is not None:
        kept_ref, piece_ref, result_ref, sum_ref = refs[count + 2 :]
        sum_ref[...] = (kept_ref[...] + piece_ref[...].astype(F32)) * scale

    @pl.when(here == 0)
    def _():
        close_blocks(mask_ref, total_ref, arrived_refs, result_ref)

    @pl.when(here == top)
    def _():
        result_ref[...] = top_ref[...]

    @pl.when((here != 0) & (here != top))
    def _():
        result_ref[...] = got_ref[...]


def step_kernel(layer_ref, mixing_ref, upstream_ref, grad_ref, message_ref, *out_refs):
    grads = (upstream_ref[...].astype(F32) * layer_ref[0].astype(F32)).astype(BF16)
    grad_ref[...] = grads
    send_blocks(grads, layer_ref[1], mixing_ref, message_ref, out_refs)


def close_step_kernel(count, mask_ref, total_ref, *refs):
    layer_ref, mixing_ref, result_ref, grad_ref, message_ref, *out_refs = refs[count:]
    close_blocks(mask_ref, total_ref, refs[:count], result_ref)
    step_kernel(layer_ref, mixing_ref, result_ref, grad_ref, message_ref, *out_refs)


def weight_product(top, turned_ref, grad_ref, top_ref, got_ref, product_ref):
    here = lax.axis_index("pipe")

    def product(ref):
        product_ref[...] = rows_dot(turned_ref[...], ref[...])

    @pl.when(here == 0)
    def _():
        product(grad_ref)

    @pl.when(here == top)
    def _():
        product(top_ref)

    @pl.when((here != 0) & (here != top))
    def _():
        product(got_ref)


def split_halves(steps, product_ref, sent_ref, kept_ref):
    def split(axis, distance, groups):
        size = kept_ref.shape[0] // groups
        place = lax.rem(lax.axis_index(axis) // distance, 2)
        for group in range(groups):
            start = 2 * group * size
            rows = slice(group * size, (group + 1) * size)
            kept = pl.ds(pl.multiple_of(start + place * size, size), size)
            sent = pl.ds(pl.multiple_of(start + (1 - place) * size, size), size)
            kept_ref[rows] = product_ref[kept]
            sent_ref[rows] = product_ref[sent].astype(BF16)

    if steps[0] == steps[1]:
        split(*steps[0])
    else:
        odd = lax.rem(lax.axis_index("pipe"), 2) == 1

        @pl.when(odd)
        def _():
            split(*steps[1])

        @pl.when(jnp.logical_not(odd))
        def _():
            split(*steps[0])


def halve_kernel(step, kept_ref, got_ref, sent_ref, next_ref, sum_ref):
    sum_ref[...] = kept_ref[...] + got_ref[...].astype(F32)
    split_halves(step, sum_ref, sent_ref, next_ref)


def bottom_kernel(count, top, step, mask_ref, total_ref, *refs):
    turned_ref, top_ref, got_ref, layer_ref, mixing_ref = refs[count : count + 5]
    result_ref, next_ref = refs[count + 5 : count + 7]
    out_refs = refs[count + 7 : 2 * count + 7]
    grad_ref, message_ref = refs[-2:]
    close_step_kernel(
        count, mask_ref, total_ref, *refs[:count], layer_ref, mixing_ref,
        result_ref, grad_ref, message_ref, *out_refs
    )
    if step is None:
        weight_product(top, turned_ref, grad_ref, top_ref, got_ref, refs[2 * count + 7])
    else:
        sent_ref, kept_ref, product_ref = refs[2 * count + 7 : -2]
        weight_product(top, turned_ref, grad_ref, top_ref, got_ref, product_ref)
        split_halves(step, product_ref, sent_ref, kept_ref)
    inner_kernel(result_ref, message_ref, mixing_ref, next_ref)


def call(body, inputs, outputs, flops, kind=pltpu.VMEM, source=IN_VMEM, scratch=()):
    size = sum(math.prod(shape) * jnp.dtype(dtype).itemsize for shape, dtype in outputs)
    size += sum(value.size * value.dtype.itemsize for value in inputs)
    return pl.pallas_call(
        body,
        out_shape=[kind(shape, dtype) for shape, dtype in outputs],
        in_specs=[source] * len(inputs),
        out_specs=[IN_VMEM] * len(outputs),
        scratch_shapes=scratch,
        compiler_params=pltpu.CompilerParams(vmem_limit_bytes=16 * 1024 * 1024),
        cost_estimate=pl.CostEstimate(flops=flops, bytes_accessed=size, transcendentals=0),
    )(*inputs)


def per_device(stored, cotangent, weight, local_edges, halo_edges, pattern, pick):
    sections, rows, columns = (lax.axis_size(name) for name in AXES)
    here = lax.axis_index("pipe")
    lower = sections // 2
    upper = sections - lower
    top = sections - 1

    def flat(section, x, y):
        return (section * rows + x) * columns + y

    def to_sections(value, moves, back=True):
        if back:
            moves = moves + [(target, source) for source, target in moves]
        pairs = [
            (flat(source, x, y), flat(target, x, y))
            for source, target in moves
            for x in range(rows)
            for y in range(columns)
        ]
        return lax.ppermute(value, AXES, pairs)

    def tile_swaps(axis, first, couples, lead, spread):
        places = {}
        for low, high in couples:
            places[low], places[high] = high, low
        others = [p for p in range(sections) if p != lead]
        buddy, inner, outer = lead ^ 1, 3 - (lead ^ 1), 3 - lead
        pairs = []
        for x in range(rows):
            for y in range(columns):
                place = x if axis == "tx" else y
                paired = place in places
                facing = places.get(place, place)
                near = (facing, y) if axis == "tx" else (x, facing)
                aside = (x, y ^ 1) if columns % 2 == 0 else (x, y)
                moves = {}
                if paired or sections != 4:
                    moves[lead] = (lead, near)
                if sections != 4:
                    moves.update((p, (q, (x, y))) for p, q in zip(others, others[1:] + others[:1]))
                elif paired and spread and axis == "tx" and first == 0 and aside != (x, y):
                    moves.update({buddy: (buddy, aside), inner: (outer, (x, y)), outer: (inner, (x, y))})
                elif paired:
                    moves.update({buddy: (inner, (x, y)), inner: (buddy, (x, y)), outer: (outer, near)})
                else:
                    for p, q in ((lead, buddy), (inner, outer)):
                        moves.update({p: (q, (x, y)), q: (p, (x, y))})
                pairs += [(flat(p, x, y), flat(q, *tile)) for p, (q, tile) in moves.items()]
        return pairs

    batches, nodes, width = stored.shape[1], stored.shape[4], stored.shape[5]
    blocks, block = local_edges.shape[3], local_edges.shape[5]
    total_rows = batches * nodes
    features = stored.reshape(total_rows, width)
    matrix = weight[0]
    picks = pick[:, 0, 0]

    phases, routes = [], []
    for axis, base, count in (("tx", 0, rows), ("ty", 2, columns)):
        for first, couples in swap_phases(count):
            phases.append((axis, base, first, count))
            route = {
                section: tile_swaps(
                    axis, first, couples, top if section >= lower else 0, 0 < section < lower
                )
                for section in range(sections)
            }
            routes.append(route)
    phases = tuple(phases)
    splits, left = [], rows * columns
    if left & (left - 1) == 0 and width // left % 16 == 0:
        along = {"tx": [], "ty": []}
        for axis, count in (("tx", rows), ("ty", columns)):
            while 1 << len(along[axis]) < count:
                along[axis].append((axis, 1 << len(along[axis])))
        orders = [
            along["ty"][::-1] + along["tx"], along["tx"][:1] + along["ty"][::-1] + along["tx"][1:]
        ]
        levels = [along["tx"][::-1] + along["ty"][::-1] for _ in orders]
        for index in range(len(orders[0])):
            steps, pairs = [], []
            for order, level in zip(orders, levels):
                steps.append((*order[index], 1 << level.index(order[index])))
                level.remove(order[index])
            for p in range(sections):
                axis, distance, _ = steps[p % 2]
                pairs += [
                    (flat(p, x, y), flat(p, x, y ^ distance) if axis == "ty" else flat(p, x ^ distance, y))
                    for x in range(rows)
                    for y in range(columns)
                ]
            splits.append((tuple(steps), pairs))
    sent = [((batches, block, width), BF16)] * len(phases)
    whole = ((total_rows, width), BF16)
    mix_rows = (blocks + len(phases)) * block
    cost = 2 * total_rows * width * (width + len(phases) * block)

    def exchange(outs, section):
        return [lax.ppermute(out, AXES, route[section]) for out, route in zip(outs, routes)]

    def inner(upstream, message, mixing):
        return call(
            inner_kernel, [upstream, message, mixing], [((total_rows, width), F32)],
            2 * total_rows * width * nodes,
        )[0]

    given = cotangent.reshape(total_rows, width)
    operands = [
        features, matrix, given, pattern[:, 0, 0], picks, local_edges[:, 0, 0], halo_edges[:, 0, 0]
    ]
    layer, mixing, mask, grad, message, *outs = call(
        functools.partial(first_kernel, phases),
        [pltpu.with_memory_space_constraint(value, pltpu.HBM) for value in operands],
        [
            ((2, total_rows, width), BF16), ((batches, mix_rows, nodes), BF16),
            ((batches * blocks * len(phases), 1, width), F32), whole, whole,
        ] + sent,
        cost + 2 * total_rows * width * width,
        source=pl.BlockSpec(memory_space=pltpu.HBM),
        scratch=[
            (pltpu.VMEM if value.dtype == BF16 else pltpu.SMEM)(value.shape, value.dtype)
            for value in operands
        ] + [pltpu.SemaphoreType.DMA((len(operands),))],
    )
    arrived = exchange(outs, top)
    total = inner(given, message, mixing)
    turned = call(turn_kernel, [features], [((width, total_rows), BF16)], 0)[0]

    layers = [layer]
    for step in range(1, upper):
        moves = [(top - step, top)] + ([(step, 0)] if step < lower else [])
        layers.append(to_sections(layer, moves))

    def fetch_home(values):
        got = None
        for step in range(1, upper):
            moves = [(top, top - step)]
            value = values[top - step]
            if step < lower:
                moves.append((0, step))
                value = call(
                    functools.partial(choose_kernel, top), [value, values[step]], [whole], 0
                )[0]
            new = to_sections(value, moves)
            takes = here == top - step
            if step < lower:
                takes = takes | (here == step)
            got = new if step == 1 else jnp.where(takes, new, got)
        return got

    count = len(phases)
    grads, results = {top: grad}, {}
    for section in reversed(range(top)):
        steps = top - section if section >= lower else section
        layer_here = layers[steps]
        if section == lower - 1:
            upstream = call(close_kernel, [mask, total, *arrived], [whole], 0)[0]
            results[section + 1] = upstream
            upstream = to_sections(upstream, [(top, 0)], False)
            grad, message, *outs = call(
                step_kernel, [layer_here, mixing, upstream], [whole, whole] + sent, cost
            )
        elif section > 0:
            upstream, grad, message, *outs = call(
                functools.partial(close_step_kernel, count),
                [mask, total, *arrived, layer_here, mixing],
                [whole, whole, whole] + sent, cost,
            )
            results[section + 1] = upstream
        else:
            product = ((width, width), F32)
            halves = [((width // 2, width), BF16), ((width // 2, width), F32)] if splits else [product]
            upstream, total, *outs = call(
                functools.partial(bottom_kernel, count, top, splits[0][0] if splits else None),
                [mask, total, *arrived, turned, grads[top], fetch_home(grads), layer_here, mixing],
                [whole, ((total_rows, width), F32)] + sent + halves,
                cost + 2 * total_rows * width * (width + nodes),
                scratch=[pltpu.VMEM(*product)] * len(splits[:1]) + [pltpu.VMEM(*whole)] * 2,
            )
            outs, pieces = outs[:count], outs[count:]
            results[1] = upstream
        arrived = exchange(outs, section)
        if section > 0:
            grads[section] = grad
            total = inner(upstream, message, mixing)

    scale = 1.0 / math.sqrt(total_rows * rows * columns)
    if splits:
        parcel, kept = pieces
        for (_, pairs), following in zip(splits, splits[1:]):
            got = lax.ppermute(parcel, AXES, pairs)
            half = (kept.shape[0] // 2, width)
            parcel, kept = call(
                functools.partial(halve_kernel, following[0]), [kept, got],
                [(half, BF16), (half, F32)], 0, scratch=[pltpu.VMEM(kept.shape, F32)],
            )
        got = lax.ppermute(parcel, AXES, splits[-1][1])
        result, summed = call(
            functools.partial(last_kernel, top, count, scale),
            [mask, total, *arrived, results[top], fetch_home(results), kept, got],
            [whole, (kept.shape, F32)], 0, jax.ShapeDtypeStruct,
        )
    else:
        summed = scale * lax.psum_scatter(pieces[0], ("tx", "ty"), scatter_dimension=0, tiled=True)
        result = call(
            functools.partial(last_kernel, top, count, None),
            [mask, total, *arrived, results[top], fetch_home(results)], [whole], 0,
            jax.ShapeDtypeStruct,
        )[0]
    return (summed[None], result.reshape(1, batches, 1, 1, nodes, width))


def solution(mesh):
    in_specs = (
        P("pipe", None, "tx", "ty", None, None),
        P(None, "tx", "ty", None, None),
        P("pipe", None, None),
        P(None, "tx", "ty", None, None, None, None),
        P(None, "tx", "ty", None, None, None, None),
        P(None, "tx", "ty", None, None),
        P(None, "tx", "ty", None),
    )
    out_specs = (P("pipe", ("tx", "ty"), None), P("pipe", None, "tx", "ty", None, None))
    return jax.shard_map(
        per_device, mesh=mesh, in_specs=in_specs, out_specs=out_specs, check_vma=False
    )
```

```python
import functools
import math

import jax
import jax.numpy as jnp
from jax import lax
from jax.experimental import pallas as pl
from jax.experimental.pallas import tpu as pltpu
from jax.sharding import PartitionSpec as P

AXES = ("pipe", "tx", "ty")
F32, BF16 = jnp.float32, jnp.bfloat16
IN_VMEM = pl.BlockSpec(memory_space=pltpu.VMEM)


def silu_slope(value):
    sigma = jax.nn.sigmoid(value)
    return sigma * (1.0 + value * (1.0 - sigma))


def swap_phases(count):
    phases = []
    for first in (0, 1):
        pairs = [(low, low + 1) for low in range(first, count - 1, 2)]
        if pairs:
            phases.append((first, pairs))
    return phases


def side(phase):
    axis, base, first, count = phase
    place = lax.axis_index(axis)
    is_low = lax.rem(place + first, 2) == 0
    return base, is_low, jnp.where(is_low, place < count - 1, place > 0)


def rows_dot(left, right):
    return lax.dot_general(left, right, (((1,), (0,)), ((), ())), preferred_element_type=F32)


def back_dot(left, right):
    return lax.dot_general(left, right, (((1,), (1,)), ((), ())), preferred_element_type=F32)


def send_blocks(grads, matrix, mixing_ref, message_ref, out_refs):
    batches, outgoing, nodes = mixing_ref.shape
    block = out_refs[0].shape[1]
    messages = back_dot(grads, matrix).astype(BF16)
    message_ref[...] = messages
    first = outgoing - block * len(out_refs)
    for batch in range(batches):
        mixed = rows_dot(
            mixing_ref[batch, first:, :], messages[batch * nodes : (batch + 1) * nodes]
        ).astype(BF16)
        for index, out_ref in enumerate(out_refs):
            out_ref[batch] = mixed[index * block : (index + 1) * block]


def first_kernel(phases, *refs):
    sources, refs = refs[:7], refs[7:]
    layer_ref, mixing_ref, mask_ref, grad_ref, message_ref = refs[:5]
    out_refs = refs[5 : 5 + len(phases)]
    held, sems = refs[5 + len(phases) : -1], refs[-1]
    copies = [
        pltpu.make_async_copy(source, target, sems.at[index])
        for index, (source, target) in enumerate(zip(sources, held))
    ]
    for copy in copies:
        copy.start()
    features_ref, matrix_ref, given_ref, pattern_ref, pick_ref, local_ref, halo_ref = held
    batches, blocks, _, block, _ = local_ref.shape
    sides = [side(phase) for phase in phases]
    copies[0].wait()
    copies[1].wait()
    pre_activation = rows_dot(features_ref[...], matrix_ref[...])
    slope = silu_slope(pre_activation).astype(BF16)
    layer_ref[0] = slope
    layer_ref[1] = matrix_ref[...]
    copies[2].wait()
    grads = (given_ref[...].astype(F32) * slope.astype(F32)).astype(BF16)
    grad_ref[...] = grads
    for copy in copies[3:]:
        copy.wait()
    for batch in range(batches):
        for source in range(blocks):
            columns = slice(source * block, (source + 1) * block)
            for target in range(blocks):
                present = pattern_ref[batch, source, target].astype(F32)
                edges = local_ref[batch, source, target].astype(F32) * present
                mixing_ref[batch, target * block : (target + 1) * block, columns] = edges.T.astype(BF16)
            for index, (base, is_low, _) in enumerate(sides):
                slot = jnp.where(is_low, base + 1, base)
                present = pattern_ref[batch, source, blocks + slot].astype(F32)
                edges = halo_ref[batch, slot, source].astype(F32) * present
                start = (blocks + index) * block
                mixing_ref[batch, start : start + block, columns] = edges.T.astype(BF16)
        for index, (base, is_low, paired) in enumerate(sides):
            chosen = pick_ref[batch, jnp.where(is_low, base, base + 1)]
            for target in range(blocks):
                here = ((chosen == target) & paired).astype(F32)
                entry = (batch * blocks + target) * len(sides) + index
                mask_ref[entry] = jnp.full(mask_ref.shape[1:], here, F32)
    send_blocks(grads, matrix_ref[...], mixing_ref, message_ref, out_refs)


def inner_kernel(upstream_ref, message_ref, mixing_ref, total_ref):
    batches, _, nodes = mixing_ref.shape
    for batch in range(batches):
        rows = slice(batch * nodes, (batch + 1) * nodes)
        total_ref[rows] = upstream_ref[rows].astype(F32) + rows_dot(
            mixing_ref[batch, :nodes, :], message_ref[rows]
        )


def turn_kernel(features_ref, turned_ref):
    turned_ref[...] = features_ref[...].T


def choose_kernel(top, top_ref, other_ref, chosen_ref):
    at_top = lax.axis_index("pipe") == top

    @pl.when(at_top)
    def _():
        chosen_ref[...] = top_ref[...]

    @pl.when(jnp.logical_not(at_top))
    def _():
        chosen_ref[...] = other_ref[...]


def close_blocks(mask_ref, total_ref, arrived_refs, result_ref):
    batches, block, _ = arrived_refs[0].shape
    count = len(arrived_refs)
    for batch in range(batches):
        arrived = [ref[batch].astype(F32) for ref in arrived_refs]
        for target in range(total_ref.shape[0] // batches // block):
            order = batch * (total_ref.shape[0] // batches // block) + target
            rows = slice(order * block, (order + 1) * block)
            value = total_ref[rows]
            for index in range(count):
                value = value + arrived[index] * mask_ref[order * count + index]
            result_ref[rows] = value.astype(BF16)


def close_kernel(mask_ref, total_ref, *refs):
    close_blocks(mask_ref, total_ref, refs[:-1], refs[-1])


def last_kernel(top, count, scale, mask_ref, total_ref, *refs):
    arrived_refs = refs[:count]
    top_ref, got_ref = refs[count : count + 2]
    result_ref = refs[-1]
    here = lax.axis_index("pipe")
    if scale is not None:
        kept_ref, piece_ref, result_ref, sum_ref = refs[count + 2 :]
        sum_ref[...] = (kept_ref[...] + piece_ref[...].astype(F32)) * scale

    @pl.when(here == 0)
    def _():
        close_blocks(mask_ref, total_ref, arrived_refs, result_ref)

    @pl.when(here == top)
    def _():
        result_ref[...] = top_ref[...]

    @pl.when((here != 0) & (here != top))
    def _():
        result_ref[...] = got_ref[...]


def step_kernel(layer_ref, mixing_ref, upstream_ref, grad_ref, message_ref, *out_refs):
    grads = (upstream_ref[...].astype(F32) * layer_ref[0].astype(F32)).astype(BF16)
    grad_ref[...] = grads
    send_blocks(grads, layer_ref[1], mixing_ref, message_ref, out_refs)


def close_step_kernel(count, mask_ref, total_ref, *refs):
    layer_ref, mixing_ref, result_ref, grad_ref, message_ref, *out_refs = refs[count:]
    close_blocks(mask_ref, total_ref, refs[:count], result_ref)
    step_kernel(layer_ref, mixing_ref, result_ref, grad_ref, message_ref, *out_refs)


def weight_product(top, turned_ref, grad_ref, top_ref, got_ref, product_ref):
    here = lax.axis_index("pipe")

    def product(ref):
        product_ref[...] = rows_dot(turned_ref[...], ref[...])

    @pl.when(here == 0)
    def _():
        product(grad_ref)

    @pl.when(here == top)
    def _():
        product(top_ref)

    @pl.when((here != 0) & (here != top))
    def _():
        product(got_ref)


def split_halves(steps, product_ref, sent_ref, kept_ref):
    def split(axis, distance, groups):
        size = kept_ref.shape[0] // groups
        place = lax.rem(lax.axis_index(axis) // distance, 2)
        for group in range(groups):
            start = 2 * group * size
            rows = slice(group * size, (group + 1) * size)
            kept = pl.ds(pl.multiple_of(start + place * size, size), size)
            sent = pl.ds(pl.multiple_of(start + (1 - place) * size, size), size)
            kept_ref[rows] = product_ref[kept]
            sent_ref[rows] = product_ref[sent].astype(BF16)

    if steps[0] == steps[1]:
        split(*steps[0])
    else:
        odd = lax.rem(lax.axis_index("pipe"), 2) == 1

        @pl.when(odd)
        def _():
            split(*steps[1])

        @pl.when(jnp.logical_not(odd))
        def _():
            split(*steps[0])


def halve_kernel(step, kept_ref, got_ref, sent_ref, next_ref, sum_ref):
    sum_ref[...] = kept_ref[...] + got_ref[...].astype(F32)
    split_halves(step, sum_ref, sent_ref, next_ref)


def bottom_kernel(count, top, step, mask_ref, total_ref, *refs):
    turned_ref, top_ref, got_ref, layer_ref, mixing_ref = refs[count : count + 5]
    result_ref, next_ref = refs[count + 5 : count + 7]
    out_refs = refs[count + 7 : 2 * count + 7]
    grad_ref, message_ref = refs[-2:]
    close_step_kernel(
        count, mask_ref, total_ref, *refs[:count], layer_ref, mixing_ref,
        result_ref, grad_ref, message_ref, *out_refs
    )
    if step is None:
        weight_product(top, turned_ref, grad_ref, top_ref, got_ref, refs[2 * count + 7])
    else:
        sent_ref, kept_ref, product_ref = refs[2 * count + 7 : -2]
        weight_product(top, turned_ref, grad_ref, top_ref, got_ref, product_ref)
        split_halves(step, product_ref, sent_ref, kept_ref)
    inner_kernel(result_ref, message_ref, mixing_ref, next_ref)


def call(body, inputs, outputs, flops, kind=pltpu.VMEM, source=IN_VMEM, scratch=()):
    size = sum(math.prod(shape) * jnp.dtype(dtype).itemsize for shape, dtype in outputs)
    size += sum(value.size * value.dtype.itemsize for value in inputs)
    return pl.pallas_call(
        body,
        out_shape=[kind(shape, dtype) for shape, dtype in outputs],
        in_specs=[source] * len(inputs),
        out_specs=[IN_VMEM] * len(outputs),
        scratch_shapes=scratch,
        compiler_params=pltpu.CompilerParams(vmem_limit_bytes=16 * 1024 * 1024),
        cost_estimate=pl.CostEstimate(flops=flops, bytes_accessed=size, transcendentals=0),
    )(*inputs)


def per_device(stored, cotangent, weight, local_edges, halo_edges, pattern, pick):
    sections, rows, columns = (lax.axis_size(name) for name in AXES)
    here = lax.axis_index("pipe")
    lower = sections // 2
    upper = sections - lower
    top = sections - 1

    def flat(section, x, y):
        return (section * rows + x) * columns + y

    def to_sections(value, moves, back=True):
        if back:
            moves = moves + [(target, source) for source, target in moves]
        pairs = [
            (flat(source, x, y), flat(target, x, y))
            for source, target in moves
            for x in range(rows)
            for y in range(columns)
        ]
        return lax.ppermute(value, AXES, pairs)

    def tile_swaps(axis, first, couples, lead, spread):
        places = {}
        for low, high in couples:
            places[low], places[high] = high, low
        others = [p for p in range(sections) if p != lead]
        buddy, inner, outer = lead ^ 1, 3 - (lead ^ 1), 3 - lead
        pairs = []
        for x in range(rows):
            for y in range(columns):
                place = x if axis == "tx" else y
                paired = place in places
                facing = places.get(place, place)
                near = (facing, y) if axis == "tx" else (x, facing)
                aside = (x, y ^ 1) if axis == "tx" else (x ^ 1, y)
                if aside[0] >= rows or aside[1] >= columns:
                    aside = (x, y)
                moves = {}
                if paired or sections != 4:
                    moves[lead] = (lead, near)
                if sections != 4:
                    moves.update((p, (q, (x, y))) for p, q in zip(others, others[1:] + others[:1]))
                elif paired and spread and axis == "tx" and first == 0 and aside != (x, y):
                    moves.update({buddy: (buddy, aside), inner: (outer, (x, y)), outer: (inner, (x, y))})
                elif paired:
                    moves.update({buddy: (inner, (x, y)), inner: (buddy, (x, y)), outer: (outer, near)})
                else:
                    moves.update({lead: (buddy, (x, y)), buddy: (lead, (x, y))})
                    moves.update({inner: (inner, aside), outer: (outer, aside)})
                pairs += [(flat(p, x, y), flat(q, *tile)) for p, (q, tile) in moves.items()]
        return pairs

    batches, nodes, width = stored.shape[1], stored.shape[4], stored.shape[5]
    blocks, block = local_edges.shape[3], local_edges.shape[5]
    total_rows = batches * nodes
    features = stored.reshape(total_rows, width)
    matrix = weight[0]
    picks = pick[:, 0, 0]

    phases, routes = [], []
    for axis, base, count in (("tx", 0, rows), ("ty", 2, columns)):
        for first, couples in swap_phases(count):
            phases.append((axis, base, first, count))
            route = {
                section: tile_swaps(
                    axis, first, couples, top if section >= lower else 0, 0 < section < lower
                )
                for section in range(sections)
            }
            routes.append(route)
    phases = tuple(phases)
    splits, left = [], rows * columns
    if left & (left - 1) == 0 and width // left % 16 == 0:
        along = {"tx": [], "ty": []}
        for axis, count in (("tx", rows), ("ty", columns)):
            while 1 << len(along[axis]) < count:
                along[axis].append((axis, 1 << len(along[axis])))
        orders = [
            along["ty"][::-1] + along["tx"], along["tx"][:1] + along["ty"][::-1] + along["tx"][1:]
        ]
        levels = [along["tx"][::-1] + along["ty"][::-1] for _ in orders]
        for index in range(len(orders[0])):
            steps, pairs = [], []
            for order, level in zip(orders, levels):
                steps.append((*order[index], 1 << level.index(order[index])))
                level.remove(order[index])
            for p in range(sections):
                axis, distance, _ = steps[p % 2]
                pairs += [
                    (flat(p, x, y), flat(p, x, y ^ distance) if axis == "ty" else flat(p, x ^ distance, y))
                    for x in range(rows)
                    for y in range(columns)
                ]
            splits.append((tuple(steps), pairs))
    sent = [((batches, block, width), BF16)] * len(phases)
    whole = ((total_rows, width), BF16)
    mix_rows = (blocks + len(phases)) * block
    cost = 2 * total_rows * width * (width + len(phases) * block)

    def exchange(outs, section):
        return [lax.ppermute(out, AXES, route[section]) for out, route in zip(outs, routes)]

    def inner(upstream, message, mixing):
        return call(
            inner_kernel, [upstream, message, mixing], [((total_rows, width), F32)],
            2 * total_rows * width * nodes,
        )[0]

    given = cotangent.reshape(total_rows, width)
    operands = [
        features, matrix, given, pattern[:, 0, 0], picks, local_edges[:, 0, 0], halo_edges[:, 0, 0]
    ]
    layer, mixing, mask, grad, message, *outs = call(
        functools.partial(first_kernel, phases),
        [pltpu.with_memory_space_constraint(value, pltpu.HBM) for value in operands],
        [
            ((2, total_rows, width), BF16), ((batches, mix_rows, nodes), BF16),
            ((batches * blocks * len(phases), 1, width), F32), whole, whole,
        ] + sent,
        cost + 2 * total_rows * width * width,
        source=pl.BlockSpec(memory_space=pltpu.HBM),
        scratch=[
            (pltpu.VMEM if value.dtype == BF16 else pltpu.SMEM)(value.shape, value.dtype)
            for value in operands
        ] + [pltpu.SemaphoreType.DMA((len(operands),))],
    )
    arrived = exchange(outs, top)
    total = inner(given, message, mixing)
    turned = call(turn_kernel, [features], [((width, total_rows), BF16)], 0)[0]

    layers = [layer]
    for step in range(1, upper):
        moves = [(top - step, top)] + ([(step, 0)] if step < lower else [])
        layers.append(to_sections(layer, moves))

    def fetch_home(values):
        got = None
        for step in range(1, upper):
            moves = [(top, top - step)]
            value = values[top - step]
            if step < lower:
                moves.append((0, step))
                value = call(
                    functools.partial(choose_kernel, top), [value, values[step]], [whole], 0
                )[0]
            new = to_sections(value, moves)
            takes = here == top - step
            if step < lower:
                takes = takes | (here == step)
            got = new if step == 1 else jnp.where(takes, new, got)
        return got

    count = len(phases)
    grads, results = {top: grad}, {}
    for section in reversed(range(top)):
        steps = top - section if section >= lower else section
        layer_here = layers[steps]
        if section == lower - 1:
            upstream = call(close_kernel, [mask, total, *arrived], [whole], 0)[0]
            results[section + 1] = upstream
            upstream = to_sections(upstream, [(top, 0)], False)
            grad, message, *outs = call(
                step_kernel, [layer_here, mixing, upstream], [whole, whole] + sent, cost
            )
        elif section > 0:
            upstream, grad, message, *outs = call(
                functools.partial(close_step_kernel, count),
                [mask, total, *arrived, layer_here, mixing],
                [whole, whole, whole] + sent, cost,
            )
            results[section + 1] = upstream
        else:
            product = ((width, width), F32)
            halves = [((width // 2, width), BF16), ((width // 2, width), F32)] if splits else [product]
            upstream, total, *outs = call(
                functools.partial(bottom_kernel, count, top, splits[0][0] if splits else None),
                [mask, total, *arrived, turned, grads[top], fetch_home(grads), layer_here, mixing],
                [whole, ((total_rows, width), F32)] + sent + halves,
                cost + 2 * total_rows * width * (width + nodes),
                scratch=[pltpu.VMEM(*product)] * len(splits[:1]) + [pltpu.VMEM(*whole)] * 2,
            )
            outs, pieces = outs[:count], outs[count:]
            if splits:
                halved = lax.ppermute(pieces[0], AXES, splits[0][1])
                outs[-1], halved = lax.optimization_barrier((outs[-1], halved))
            results[1] = upstream
        arrived = exchange(outs, section)
        if section > 0:
            grads[section] = grad
            total = inner(upstream, message, mixing)

    scale = 1.0 / math.sqrt(total_rows * rows * columns)
    if splits:
        parcel, kept = pieces
        for (_, pairs), following in zip(splits, splits[1:]):
            got = halved if parcel is pieces[0] else lax.ppermute(parcel, AXES, pairs)
            half = (kept.shape[0] // 2, width)
            parcel, kept = call(
                functools.partial(halve_kernel, following[0]), [kept, got],
                [(half, BF16), (half, F32)], 0, scratch=[pltpu.VMEM(kept.shape, F32)],
            )
        got = halved if parcel is pieces[0] else lax.ppermute(parcel, AXES, splits[-1][1])
        result, summed = call(
            functools.partial(last_kernel, top, count, scale),
            [mask, total, *arrived, results[top], fetch_home(results), kept, got],
            [whole, (kept.shape, F32)], 0, jax.ShapeDtypeStruct,
        )
    else:
        summed = scale * lax.psum_scatter(pieces[0], ("tx", "ty"), scatter_dimension=0, tiled=True)
        result = call(
            functools.partial(last_kernel, top, count, None),
            [mask, total, *arrived, results[top], fetch_home(results)], [whole], 0,
            jax.ShapeDtypeStruct,
        )[0]
    return (summed[None], result.reshape(1, batches, 1, 1, nodes, width))


def solution(mesh):
    in_specs = (
        P("pipe", None, "tx", "ty", None, None),
        P(None, "tx", "ty", None, None),
        P("pipe", None, None),
        P(None, "tx", "ty", None, None, None, None),
        P(None, "tx", "ty", None, None, None, None),
        P(None, "tx", "ty", None, None),
        P(None, "tx", "ty", None),
    )
    out_specs = (P("pipe", ("tx", "ty"), None), P("pipe", None, "tx", "ty", None, None))
    return jax.shard_map(
        per_device, mesh=mesh, in_specs=in_specs, out_specs=out_specs, check_vma=False
    )
```

```python
import functools
import math

import jax
import jax.numpy as jnp
from jax import lax
from jax.experimental import pallas as pl
from jax.experimental.pallas import tpu as pltpu
from jax.sharding import PartitionSpec as P

AXES = ("pipe", "tx", "ty")
F32, BF16 = jnp.float32, jnp.bfloat16
IN_VMEM = pl.BlockSpec(memory_space=pltpu.VMEM)


def silu_slope(value):
    sigma = jax.nn.sigmoid(value)
    return sigma * (1.0 + value * (1.0 - sigma))


def swap_phases(count):
    phases = []
    for first in (0, 1):
        pairs = [(low, low + 1) for low in range(first, count - 1, 2)]
        if pairs:
            phases.append((first, pairs))
    return phases


def side(phase):
    axis, base, first, count = phase
    place = lax.axis_index(axis)
    is_low = lax.rem(place + first, 2) == 0
    return base, is_low, jnp.where(is_low, place < count - 1, place > 0)


def rows_dot(left, right):
    return lax.dot_general(left, right, (((1,), (0,)), ((), ())), preferred_element_type=F32)


def back_dot(left, right):
    return lax.dot_general(left, right, (((1,), (1,)), ((), ())), preferred_element_type=F32)


def send_blocks(grads, matrix, mixing_ref, message_ref, out_refs):
    batches, outgoing, nodes = mixing_ref.shape
    block = out_refs[0].shape[1]
    messages = back_dot(grads, matrix).astype(BF16)
    message_ref[...] = messages
    first = outgoing - block * len(out_refs)
    for batch in range(batches):
        mixed = rows_dot(
            mixing_ref[batch, first:, :], messages[batch * nodes : (batch + 1) * nodes]
        ).astype(BF16)
        for index, out_ref in enumerate(out_refs):
            out_ref[batch] = mixed[index * block : (index + 1) * block]


def first_kernel(phases, *refs):
    sources, refs = refs[:7], refs[7:]
    layer_ref, mixing_ref, mask_ref, grad_ref, message_ref = refs[:5]
    out_refs = refs[5 : 5 + len(phases)]
    held, sems = refs[5 + len(phases) : -1], refs[-1]
    copies = [
        pltpu.make_async_copy(source, target, sems.at[index])
        for index, (source, target) in enumerate(zip(sources, held))
    ]
    for copy in copies:
        copy.start()
    features_ref, matrix_ref, given_ref, pattern_ref, pick_ref, local_ref, halo_ref = held
    batches, blocks, _, block, _ = local_ref.shape
    sides = [side(phase) for phase in phases]
    copies[0].wait()
    copies[1].wait()
    pre_activation = rows_dot(features_ref[...], matrix_ref[...])
    slope = silu_slope(pre_activation).astype(BF16)
    layer_ref[0] = slope
    layer_ref[1] = matrix_ref[...]
    copies[2].wait()
    grads = (given_ref[...].astype(F32) * slope.astype(F32)).astype(BF16)
    grad_ref[...] = grads
    for copy in copies[3:]:
        copy.wait()
    for batch in range(batches):
        for source in range(blocks):
            columns = slice(source * block, (source + 1) * block)
            for target in range(blocks):
                present = pattern_ref[batch, source, target].astype(F32)
                edges = local_ref[batch, source, target].astype(F32) * present
                mixing_ref[batch, target * block : (target + 1) * block, columns] = edges.T.astype(BF16)
            for index, (base, is_low, _) in enumerate(sides):
                slot = jnp.where(is_low, base + 1, base)
                present = pattern_ref[batch, source, blocks + slot].astype(F32)
                edges = halo_ref[batch, slot, source].astype(F32) * present
                start = (blocks + index) * block
                mixing_ref[batch, start : start + block, columns] = edges.T.astype(BF16)
        for index, (base, is_low, paired) in enumerate(sides):
            chosen = pick_ref[batch, jnp.where(is_low, base, base + 1)]
            for target in range(blocks):
                here = ((chosen == target) & paired).astype(F32)
                entry = (batch * blocks + target) * len(sides) + index
                mask_ref[entry] = jnp.full(mask_ref.shape[1:], here, F32)
    send_blocks(grads, matrix_ref[...], mixing_ref, message_ref, out_refs)


def inner_kernel(upstream_ref, message_ref, mixing_ref, total_ref):
    batches, _, nodes = mixing_ref.shape
    for batch in range(batches):
        rows = slice(batch * nodes, (batch + 1) * nodes)
        total_ref[rows] = upstream_ref[rows].astype(F32) + rows_dot(
            mixing_ref[batch, :nodes, :], message_ref[rows]
        )


def turn_kernel(features_ref, turned_ref):
    turned_ref[...] = features_ref[...].T


def choose_kernel(top, top_ref, other_ref, chosen_ref):
    at_top = lax.axis_index("pipe") == top

    @pl.when(at_top)
    def _():
        chosen_ref[...] = top_ref[...]

    @pl.when(jnp.logical_not(at_top))
    def _():
        chosen_ref[...] = other_ref[...]


def close_blocks(mask_ref, total_ref, arrived_refs, result_ref):
    batches, block, _ = arrived_refs[0].shape
    count = len(arrived_refs)
    for batch in range(batches):
        arrived = [ref[batch].astype(F32) for ref in arrived_refs]
        for target in range(total_ref.shape[0] // batches // block):
            order = batch * (total_ref.shape[0] // batches // block) + target
            rows = slice(order * block, (order + 1) * block)
            value = total_ref[rows]
            for index in range(count):
                value = value + arrived[index] * mask_ref[order * count + index]
            result_ref[rows] = value.astype(BF16)


def close_kernel(mask_ref, total_ref, *refs):
    close_blocks(mask_ref, total_ref, refs[:-1], refs[-1])


def last_kernel(top, count, scale, mask_ref, total_ref, *refs):
    arrived_refs = refs[:count]
    top_ref, got_ref = refs[count : count + 2]
    result_ref = refs[-1]
    here = lax.axis_index("pipe")
    if scale is not None:
        kept_ref, piece_ref, result_ref, sum_ref = refs[count + 2 :]
        sum_ref[...] = (kept_ref[...] + piece_ref[...].astype(F32)) * scale

    @pl.when(here == 0)
    def _():
        close_blocks(mask_ref, total_ref, arrived_refs, result_ref)

    @pl.when(here == top)
    def _():
        result_ref[...] = top_ref[...]

    @pl.when((here != 0) & (here != top))
    def _():
        result_ref[...] = got_ref[...]


def step_kernel(layer_ref, mixing_ref, upstream_ref, grad_ref, message_ref, *out_refs):
    grads = (upstream_ref[...].astype(F32) * layer_ref[0].astype(F32)).astype(BF16)
    grad_ref[...] = grads
    send_blocks(grads, layer_ref[1], mixing_ref, message_ref, out_refs)


def close_step_kernel(count, mask_ref, total_ref, *refs):
    layer_ref, mixing_ref, result_ref, grad_ref, message_ref, *out_refs = refs[count:]
    close_blocks(mask_ref, total_ref, refs[:count], result_ref)
    step_kernel(layer_ref, mixing_ref, result_ref, grad_ref, message_ref, *out_refs)


def weight_product(top, turned_ref, grad_ref, top_ref, got_ref, product_ref):
    here = lax.axis_index("pipe")

    def product(ref):
        product_ref[...] = rows_dot(turned_ref[...], ref[...])

    @pl.when(here == 0)
    def _():
        product(grad_ref)

    @pl.when(here == top)
    def _():
        product(top_ref)

    @pl.when((here != 0) & (here != top))
    def _():
        product(got_ref)


def split_halves(steps, product_ref, sent_ref, kept_ref):
    def split(axis, distance, groups):
        size = kept_ref.shape[0] // groups
        place = lax.rem(lax.axis_index(axis) // distance, 2)
        for group in range(groups):
            start = 2 * group * size
            rows = slice(group * size, (group + 1) * size)
            kept = pl.ds(pl.multiple_of(start + place * size, size), size)
            sent = pl.ds(pl.multiple_of(start + (1 - place) * size, size), size)
            kept_ref[rows] = product_ref[kept]
            sent_ref[rows] = product_ref[sent].astype(BF16)

    if steps[0] == steps[1]:
        split(*steps[0])
    else:
        odd = lax.rem(lax.axis_index("pipe"), 2) == 1

        @pl.when(odd)
        def _():
            split(*steps[1])

        @pl.when(jnp.logical_not(odd))
        def _():
            split(*steps[0])


def halve_kernel(step, kept_ref, got_ref, sent_ref, next_ref, sum_ref):
    sum_ref[...] = kept_ref[...] + got_ref[...].astype(F32)
    split_halves(step, sum_ref, sent_ref, next_ref)


def bottom_kernel(count, top, step, mask_ref, total_ref, *refs):
    turned_ref, top_ref, got_ref, layer_ref, mixing_ref = refs[count : count + 5]
    result_ref, next_ref = refs[count + 5 : count + 7]
    out_refs = refs[count + 7 : 2 * count + 7]
    grad_ref, message_ref = refs[-2:]
    close_step_kernel(
        count, mask_ref, total_ref, *refs[:count], layer_ref, mixing_ref,
        result_ref, grad_ref, message_ref, *out_refs
    )
    if step is None:
        weight_product(top, turned_ref, grad_ref, top_ref, got_ref, refs[2 * count + 7])
    else:
        sent_ref, kept_ref, product_ref = refs[2 * count + 7 : -2]
        weight_product(top, turned_ref, grad_ref, top_ref, got_ref, product_ref)
        split_halves(step, product_ref, sent_ref, kept_ref)
    inner_kernel(result_ref, message_ref, mixing_ref, next_ref)


def call(body, inputs, outputs, flops, kind=pltpu.VMEM, source=IN_VMEM, scratch=()):
    size = sum(math.prod(shape) * jnp.dtype(dtype).itemsize for shape, dtype in outputs)
    size += sum(value.size * value.dtype.itemsize for value in inputs)
    return pl.pallas_call(
        body,
        out_shape=[kind(shape, dtype) for shape, dtype in outputs],
        in_specs=[source] * len(inputs),
        out_specs=[IN_VMEM] * len(outputs),
        scratch_shapes=scratch,
        compiler_params=pltpu.CompilerParams(vmem_limit_bytes=16 * 1024 * 1024),
        cost_estimate=pl.CostEstimate(flops=flops, bytes_accessed=size, transcendentals=0),
    )(*inputs)


def per_device(stored, cotangent, weight, local_edges, halo_edges, pattern, pick):
    sections, rows, columns = (lax.axis_size(name) for name in AXES)
    here = lax.axis_index("pipe")
    lower = sections // 2
    upper = sections - lower
    top = sections - 1

    def flat(section, x, y):
        return (section * rows + x) * columns + y

    def to_sections(value, moves, back=True, crossed=False):
        if back:
            returns = [source for source, _ in moves]
            returns = returns[::-1] if crossed else returns
            moves = moves + [(target, source) for (_, target), source in zip(moves, returns)]
        pairs = [
            (flat(source, x, y), flat(target, x, y))
            for source, target in moves
            for x in range(rows)
            for y in range(columns)
        ]
        return lax.ppermute(value, AXES, pairs)

    def tile_swaps(axis, first, couples, lead, spread):
        places = {}
        for low, high in couples:
            places[low], places[high] = high, low
        others = [p for p in range(sections) if p != lead]
        buddy, inner, outer = lead ^ 1, 3 - (lead ^ 1), 3 - lead
        pairs = []
        for x in range(rows):
            for y in range(columns):
                place = x if axis == "tx" else y
                paired = place in places
                facing = places.get(place, place)
                near = (facing, y) if axis == "tx" else (x, facing)
                aside = (x, y ^ 1) if axis == "tx" else (x ^ 1, y)
                if aside[0] >= rows or aside[1] >= columns:
                    aside = (x, y)
                beside = (x ^ 1, y) if rows % 2 == 0 else (x, y)
                here = (x, y)
                moves = {lead: (lead, near if paired else aside)}
                if sections != 4:
                    moves.update((p, (q, here)) for p, q in zip(others, others[1:] + others[:1]))
                elif not spread and axis == "tx":
                    moves.update({buddy: (inner, here), inner: (buddy, here)})
                    moves[outer] = (outer, beside if first else aside)
                elif not spread:
                    moves.update({inner: (outer, here), outer: (inner, here), buddy: (buddy, beside)})
                elif not paired:
                    for p, q in ((lead, buddy), (inner, outer)):
                        moves.update({p: (q, here), q: (p, here)})
                elif axis == "tx" and first == 0 and aside != here:
                    moves.update({buddy: (buddy, aside), inner: (outer, here), outer: (inner, here)})
                else:
                    moves.update({buddy: (inner, here), inner: (buddy, here), outer: (outer, near)})
                pairs += [(flat(p, x, y), flat(q, *tile)) for p, (q, tile) in moves.items()]
        return pairs

    batches, nodes, width = stored.shape[1], stored.shape[4], stored.shape[5]
    blocks, block = local_edges.shape[3], local_edges.shape[5]
    total_rows = batches * nodes
    features = stored.reshape(total_rows, width)
    matrix = weight[0]
    picks = pick[:, 0, 0]

    phases, routes = [], []
    for axis, base, count in (("tx", 0, rows), ("ty", 2, columns)):
        for first, couples in swap_phases(count):
            phases.append((axis, base, first, count))
            route = {
                section: tile_swaps(
                    axis, first, couples, top if section >= lower else 0, 0 < section < lower
                )
                for section in range(sections)
            }
            routes.append(route)
    phases = tuple(phases)
    splits, left = [], rows * columns
    if left & (left - 1) == 0 and width // left % 16 == 0:
        along = {"tx": [], "ty": []}
        for axis, count in (("tx", rows), ("ty", columns)):
            while 1 << len(along[axis]) < count:
                along[axis].append((axis, 1 << len(along[axis])))
        orders = [
            along["ty"][::-1] + along["tx"], along["tx"][:1] + along["ty"][::-1] + along["tx"][1:]
        ]
        levels = [along["tx"][::-1] + along["ty"][::-1] for _ in orders]
        for index in range(len(orders[0])):
            steps, pairs = [], []
            for order, level in zip(orders, levels):
                steps.append((*order[index], 1 << level.index(order[index])))
                level.remove(order[index])
            for p in range(sections):
                axis, distance, _ = steps[p % 2]
                pairs += [
                    (flat(p, x, y), flat(p, x, y ^ distance) if axis == "ty" else flat(p, x ^ distance, y))
                    for x in range(rows)
                    for y in range(columns)
                ]
            splits.append((tuple(steps), pairs))
    sent = [((batches, block, width), BF16)] * len(phases)
    whole = ((total_rows, width), BF16)
    mix_rows = (blocks + len(phases)) * block
    cost = 2 * total_rows * width * (width + len(phases) * block)

    def exchange(outs, section):
        return [lax.ppermute(out, AXES, route[section]) for out, route in zip(outs, routes)]

    def inner(upstream, message, mixing):
        return call(
            inner_kernel, [upstream, message, mixing], [((total_rows, width), F32)],
            2 * total_rows * width * nodes,
        )[0]

    given = cotangent.reshape(total_rows, width)
    operands = [
        features, matrix, given, pattern[:, 0, 0], picks, local_edges[:, 0, 0], halo_edges[:, 0, 0]
    ]
    layer, mixing, mask, grad, message, *outs = call(
        functools.partial(first_kernel, phases),
        [pltpu.with_memory_space_constraint(value, pltpu.HBM) for value in operands],
        [
            ((2, total_rows, width), BF16), ((batches, mix_rows, nodes), BF16),
            ((batches * blocks * len(phases), 1, width), F32), whole, whole,
        ] + sent,
        cost + 2 * total_rows * width * width,
        source=pl.BlockSpec(memory_space=pltpu.HBM),
        scratch=[
            (pltpu.VMEM if value.dtype == BF16 else pltpu.SMEM)(value.shape, value.dtype)
            for value in operands
        ] + [pltpu.SemaphoreType.DMA((len(operands),))],
    )
    arrived = exchange(outs, top)
    total = inner(given, message, mixing)
    turned = call(turn_kernel, [features], [((width, total_rows), BF16)], 0)[0]

    layers = [layer]
    for step in range(1, upper):
        moves = [(top - step, top)] + ([(step, 0)] if step < lower else [])
        layers.append(to_sections(layer, moves))

    def fetch_home(values, crossed=False):
        got = None
        for step in range(1, upper):
            moves = [(top, top - step)]
            value = values[top - step]
            if step < lower:
                moves.append((0, step))
                value = call(
                    functools.partial(choose_kernel, top), [value, values[step]], [whole], 0
                )[0]
            new = to_sections(value, moves, crossed=crossed)
            takes = here == top - step
            if step < lower:
                takes = takes | (here == step)
            got = new if step == 1 else jnp.where(takes, new, got)
        return got

    count = len(phases)
    grads, results = {top: grad}, {}
    for section in reversed(range(top)):
        steps = top - section if section >= lower else section
        layer_here = layers[steps]
        if section == lower - 1:
            upstream = call(close_kernel, [mask, total, *arrived], [whole], 0)[0]
            results[section + 1] = upstream
            upstream = to_sections(upstream, [(top, 0)], False)
            grad, message, *outs = call(
                step_kernel, [layer_here, mixing, upstream], [whole, whole] + sent, cost
            )
        elif section > 0:
            upstream, grad, message, *outs = call(
                functools.partial(close_step_kernel, count),
                [mask, total, *arrived, layer_here, mixing],
                [whole, whole, whole] + sent, cost,
            )
            results[section + 1] = upstream
        else:
            product = ((width, width), F32)
            halves = [((width // 2, width), BF16), ((width // 2, width), F32)] if splits else [product]
            upstream, total, *outs = call(
                functools.partial(bottom_kernel, count, top, splits[0][0] if splits else None),
                [mask, total, *arrived, turned, grads[top], fetch_home(grads), layer_here, mixing],
                [whole, ((total_rows, width), F32)] + sent + halves,
                cost + 2 * total_rows * width * (width + nodes),
                scratch=[pltpu.VMEM(*product)] * len(splits[:1]) + [pltpu.VMEM(*whole)] * 2,
            )
            outs, pieces = outs[:count], outs[count:]
            results[1] = upstream
        arrived = exchange(outs, section)
        if section > 0:
            grads[section] = grad
            total = inner(upstream, message, mixing)

    scale = 1.0 / math.sqrt(total_rows * rows * columns)
    if splits:
        parcel, kept = pieces
        for (_, pairs), following in zip(splits, splits[1:]):
            got = lax.ppermute(parcel, AXES, pairs)
            half = (kept.shape[0] // 2, width)
            parcel, kept = call(
                functools.partial(halve_kernel, following[0]), [kept, got],
                [(half, BF16), (half, F32)], 0, scratch=[pltpu.VMEM(kept.shape, F32)],
            )
        got = lax.ppermute(parcel, AXES, splits[-1][1])
        result, summed = call(
            functools.partial(last_kernel, top, count, scale),
            [mask, total, *arrived, results[top], fetch_home(results, True), kept, got],
            [whole, (kept.shape, F32)], 0, jax.ShapeDtypeStruct,
        )
    else:
        summed = scale * lax.psum_scatter(pieces[0], ("tx", "ty"), scatter_dimension=0, tiled=True)
        result = call(
            functools.partial(last_kernel, top, count, None),
            [mask, total, *arrived, results[top], fetch_home(results, True)], [whole], 0,
            jax.ShapeDtypeStruct,
        )[0]
    return (summed[None], result.reshape(1, batches, 1, 1, nodes, width))


def solution(mesh):
    in_specs = (
        P("pipe", None, "tx", "ty", None, None),
        P(None, "tx", "ty", None, None),
        P("pipe", None, None),
        P(None, "tx", "ty", None, None, None, None),
        P(None, "tx", "ty", None, None, None, None),
        P(None, "tx", "ty", None, None),
        P(None, "tx", "ty", None),
    )
    out_specs = (P("pipe", ("tx", "ty"), None), P("pipe", None, "tx", "ty", None, None))
    return jax.shard_map(
        per_device, mesh=mesh, in_specs=in_specs, out_specs=out_specs, check_vma=False
    )
```

```python
import functools
import math

import jax
import jax.numpy as jnp
from jax import lax
from jax.experimental import pallas as pl
from jax.experimental.pallas import tpu as pltpu
from jax.sharding import PartitionSpec as P

AXES = ("pipe", "tx", "ty")
F32, BF16 = jnp.float32, jnp.bfloat16
IN_VMEM = pl.BlockSpec(memory_space=pltpu.VMEM)


def silu_slope(value):
    sigma = jax.nn.sigmoid(value)
    return sigma * (1.0 + value * (1.0 - sigma))


def swap_phases(count):
    phases = []
    for first in (0, 1):
        pairs = [(low, low + 1) for low in range(first, count - 1, 2)]
        if pairs:
            phases.append((first, pairs))
    return phases


def side(phase):
    axis, base, first, count = phase
    place = lax.axis_index(axis)
    is_low = lax.rem(place + first, 2) == 0
    return base, is_low, jnp.where(is_low, place < count - 1, place > 0)


def rows_dot(left, right):
    return lax.dot_general(left, right, (((1,), (0,)), ((), ())), preferred_element_type=F32)


def back_dot(left, right):
    return lax.dot_general(left, right, (((1,), (1,)), ((), ())), preferred_element_type=F32)


def send_blocks(grads, matrix, mixing_ref, message_ref, out_refs):
    batches, outgoing, nodes = mixing_ref.shape
    block = out_refs[0].shape[1]
    messages = back_dot(grads, matrix).astype(BF16)
    message_ref[...] = messages
    first = outgoing - block * len(out_refs)
    for batch in range(batches):
        mixed = rows_dot(
            mixing_ref[batch, first:, :], messages[batch * nodes : (batch + 1) * nodes]
        ).astype(BF16)
        for index, out_ref in enumerate(out_refs):
            out_ref[batch] = mixed[index * block : (index + 1) * block]


def first_kernel(phases, *refs):
    sources, refs = refs[:7], refs[7:]
    layer_ref, mixing_ref, mask_ref, grad_ref, message_ref = refs[:5]
    out_refs = refs[5 : 5 + len(phases)]
    held, sems = refs[5 + len(phases) : -1], refs[-1]
    copies = [
        pltpu.make_async_copy(source, target, sems.at[index])
        for index, (source, target) in enumerate(zip(sources, held))
    ]
    for copy in copies:
        copy.start()
    features_ref, matrix_ref, given_ref, pattern_ref, pick_ref, local_ref, halo_ref = held
    batches, blocks, _, block, _ = local_ref.shape
    sides = [side(phase) for phase in phases]
    copies[0].wait()
    copies[1].wait()
    pre_activation = rows_dot(features_ref[...], matrix_ref[...])
    slope = silu_slope(pre_activation).astype(BF16)
    layer_ref[0] = slope
    layer_ref[1] = matrix_ref[...]
    copies[2].wait()
    grads = (given_ref[...].astype(F32) * slope.astype(F32)).astype(BF16)
    grad_ref[...] = grads
    for copy in copies[3:]:
        copy.wait()
    for batch in range(batches):
        for source in range(blocks):
            columns = slice(source * block, (source + 1) * block)
            for target in range(blocks):
                present = pattern_ref[batch, source, target].astype(F32)
                edges = local_ref[batch, source, target].astype(F32) * present
                mixing_ref[batch, target * block : (target + 1) * block, columns] = edges.T.astype(BF16)
            for index, (base, is_low, _) in enumerate(sides):
                slot = jnp.where(is_low, base + 1, base)
                present = pattern_ref[batch, source, blocks + slot].astype(F32)
                edges = halo_ref[batch, slot, source].astype(F32) * present
                start = (blocks + index) * block
                mixing_ref[batch, start : start + block, columns] = edges.T.astype(BF16)
        for index, (base, is_low, paired) in enumerate(sides):
            chosen = pick_ref[batch, jnp.where(is_low, base, base + 1)]
            for target in range(blocks):
                here = ((chosen == target) & paired).astype(F32)
                entry = (batch * blocks + target) * len(sides) + index
                mask_ref[entry] = jnp.full(mask_ref.shape[1:], here, F32)
    send_blocks(grads, matrix_ref[...], mixing_ref, message_ref, out_refs)


def inner_kernel(upstream_ref, message_ref, mixing_ref, total_ref):
    batches, _, nodes = mixing_ref.shape
    for batch in range(batches):
        rows = slice(batch * nodes, (batch + 1) * nodes)
        total_ref[rows] = upstream_ref[rows].astype(F32) + rows_dot(
            mixing_ref[batch, :nodes, :], message_ref[rows]
        )


def turn_kernel(features_ref, turned_ref):
    turned_ref[...] = features_ref[...].T


def choose_kernel(top, top_ref, other_ref, chosen_ref):
    at_top = lax.axis_index("pipe") == top

    @pl.when(at_top)
    def _():
        chosen_ref[...] = top_ref[...]

    @pl.when(jnp.logical_not(at_top))
    def _():
        chosen_ref[...] = other_ref[...]


def close_blocks(mask_ref, total_ref, arrived_refs, result_ref):
    batches, block, _ = arrived_refs[0].shape
    count = len(arrived_refs)
    for batch in range(batches):
        arrived = [ref[batch].astype(F32) for ref in arrived_refs]
        for target in range(total_ref.shape[0] // batches // block):
            order = batch * (total_ref.shape[0] // batches // block) + target
            rows = slice(order * block, (order + 1) * block)
            value = total_ref[rows]
            for index in range(count):
                value = value + arrived[index] * mask_ref[order * count + index]
            result_ref[rows] = value.astype(BF16)


def close_kernel(mask_ref, total_ref, *refs):
    close_blocks(mask_ref, total_ref, refs[:-1], refs[-1])


def last_kernel(top, count, scale, mask_ref, total_ref, *refs):
    arrived_refs = refs[:count]
    top_ref, got_ref = refs[count : count + 2]
    result_ref = refs[-1]
    here = lax.axis_index("pipe")
    if scale is not None:
        kept_ref, piece_ref, result_ref, sum_ref = refs[count + 2 :]
        sum_ref[...] = (kept_ref[...] + piece_ref[...].astype(F32)) * scale

    @pl.when(here == 0)
    def _():
        close_blocks(mask_ref, total_ref, arrived_refs, result_ref)

    @pl.when(here == top)
    def _():
        result_ref[...] = top_ref[...]

    @pl.when((here != 0) & (here != top))
    def _():
        result_ref[...] = got_ref[...]


def step_kernel(layer_ref, mixing_ref, upstream_ref, grad_ref, message_ref, *out_refs):
    grads = (upstream_ref[...].astype(F32) * layer_ref[0].astype(F32)).astype(BF16)
    grad_ref[...] = grads
    send_blocks(grads, layer_ref[1], mixing_ref, message_ref, out_refs)


def close_step_kernel(count, mask_ref, total_ref, *refs):
    layer_ref, mixing_ref, result_ref, grad_ref, message_ref, *out_refs = refs[count:]
    close_blocks(mask_ref, total_ref, refs[:count], result_ref)
    step_kernel(layer_ref, mixing_ref, result_ref, grad_ref, message_ref, *out_refs)


def weight_product(top, turned_ref, grad_ref, top_ref, got_ref, product_ref):
    here = lax.axis_index("pipe")

    def product(ref):
        product_ref[...] = rows_dot(turned_ref[...], ref[...])

    @pl.when(here == 0)
    def _():
        product(grad_ref)

    @pl.when(here == top)
    def _():
        product(top_ref)

    @pl.when((here != 0) & (here != top))
    def _():
        product(got_ref)


def split_halves(steps, product_ref, sent_ref, kept_ref):
    def split(axis, distance, groups):
        size = kept_ref.shape[0] // groups
        place = lax.rem(lax.axis_index(axis) // distance, 2)
        for group in range(groups):
            start = 2 * group * size
            rows = slice(group * size, (group + 1) * size)
            kept = pl.ds(pl.multiple_of(start + place * size, size), size)
            sent = pl.ds(pl.multiple_of(start + (1 - place) * size, size), size)
            kept_ref[rows] = product_ref[kept]
            sent_ref[rows] = product_ref[sent].astype(BF16)

    if steps[0] == steps[1]:
        split(*steps[0])
    else:
        odd = lax.rem(lax.axis_index("pipe"), 2) == 1

        @pl.when(odd)
        def _():
            split(*steps[1])

        @pl.when(jnp.logical_not(odd))
        def _():
            split(*steps[0])


def halve_kernel(step, kept_ref, got_ref, sent_ref, next_ref, sum_ref):
    sum_ref[...] = kept_ref[...] + got_ref[...].astype(F32)
    split_halves(step, sum_ref, sent_ref, next_ref)


def bottom_kernel(count, top, step, mask_ref, total_ref, *refs):
    turned_ref, top_ref, got_ref, layer_ref, mixing_ref = refs[count : count + 5]
    result_ref, next_ref = refs[count + 5 : count + 7]
    out_refs = refs[count + 7 : 2 * count + 7]
    grad_ref, message_ref = refs[-2:]
    close_step_kernel(
        count, mask_ref, total_ref, *refs[:count], layer_ref, mixing_ref,
        result_ref, grad_ref, message_ref, *out_refs
    )
    if step is None:
        weight_product(top, turned_ref, grad_ref, top_ref, got_ref, refs[2 * count + 7])
    else:
        sent_ref, kept_ref, product_ref = refs[2 * count + 7 : -2]
        weight_product(top, turned_ref, grad_ref, top_ref, got_ref, product_ref)
        split_halves(step, product_ref, sent_ref, kept_ref)
    inner_kernel(result_ref, message_ref, mixing_ref, next_ref)


def call(body, inputs, outputs, flops, kind=pltpu.VMEM, source=IN_VMEM, scratch=()):
    size = sum(math.prod(shape) * jnp.dtype(dtype).itemsize for shape, dtype in outputs)
    size += sum(value.size * value.dtype.itemsize for value in inputs)
    return pl.pallas_call(
        body,
        out_shape=[kind(shape, dtype) for shape, dtype in outputs],
        in_specs=[source] * len(inputs),
        out_specs=[IN_VMEM] * len(outputs),
        scratch_shapes=scratch,
        compiler_params=pltpu.CompilerParams(vmem_limit_bytes=16 * 1024 * 1024),
        cost_estimate=pl.CostEstimate(flops=flops, bytes_accessed=size, transcendentals=0),
    )(*inputs)


def per_device(stored, cotangent, weight, local_edges, halo_edges, pattern, pick):
    sections, rows, columns = (lax.axis_size(name) for name in AXES)
    here = lax.axis_index("pipe")
    lower = sections // 2
    upper = sections - lower
    top = sections - 1

    def flat(section, x, y):
        return (section * rows + x) * columns + y

    def to_sections(value, moves, back=True, crossed=False):
        if back:
            returns = [source for source, _ in moves]
            returns = returns[::-1] if crossed else returns
            moves = moves + [(target, source) for (_, target), source in zip(moves, returns)]
        pairs = [
            (flat(source, x, y), flat(target, x, y))
            for source, target in moves
            for x in range(rows)
            for y in range(columns)
        ]
        return lax.ppermute(value, AXES, pairs)

    def tile_swaps(axis, first, couples, lead, spread):
        places = {}
        for low, high in couples:
            places[low], places[high] = high, low
        others = [p for p in range(sections) if p != lead]
        buddy, inner, outer = lead ^ 1, 3 - (lead ^ 1), 3 - lead
        pairs = []
        for x in range(rows):
            for y in range(columns):
                place = x if axis == "tx" else y
                paired = place in places
                facing = places.get(place, place)
                near = (facing, y) if axis == "tx" else (x, facing)
                aside = (x, y ^ 1) if axis == "tx" else (x ^ 1, y)
                if aside[0] >= rows or aside[1] >= columns:
                    aside = (x, y)
                beside = (x ^ 1, y) if rows % 2 == 0 else (x, y)
                here = (x, y)
                moves = {lead: (lead, near if paired else aside)}
                if sections != 4:
                    moves.update((p, (q, here)) for p, q in zip(others, others[1:] + others[:1]))
                elif not spread and axis == "tx":
                    moves.update({buddy: (inner, here), inner: (buddy, here)})
                    moves[outer] = (outer, beside if first else aside)
                elif not spread:
                    moves.update({inner: (outer, here), outer: (inner, here), buddy: (buddy, beside)})
                elif not paired:
                    for p, q in ((lead, buddy), (inner, outer)):
                        moves.update({p: (q, here), q: (p, here)})
                elif axis == "tx" and first == 0 and aside != here:
                    moves.update({buddy: (buddy, aside), inner: (outer, here), outer: (inner, here)})
                else:
                    moves.update({buddy: (inner, here), inner: (buddy, here), outer: (outer, near)})
                pairs += [(flat(p, x, y), flat(q, *tile)) for p, (q, tile) in moves.items()]
        return pairs

    batches, nodes, width = stored.shape[1], stored.shape[4], stored.shape[5]
    blocks, block = local_edges.shape[3], local_edges.shape[5]
    total_rows = batches * nodes
    features = stored.reshape(total_rows, width)
    matrix = weight[0]
    picks = pick[:, 0, 0]

    phases, routes = [], []
    for axis, base, count in (("tx", 0, rows), ("ty", 2, columns)):
        for first, couples in swap_phases(count):
            phases.append((axis, base, first, count))
            route = {
                section: tile_swaps(
                    axis, first, couples, top if section >= lower else 0, 0 < section < lower
                )
                for section in range(sections)
            }
            routes.append(route)
    phases = tuple(phases)
    splits, left = [], rows * columns
    if left & (left - 1) == 0 and width // left % 16 == 0:
        along = {"tx": [], "ty": []}
        for axis, count in (("tx", rows), ("ty", columns)):
            while 1 << len(along[axis]) < count:
                along[axis].append((axis, 1 << len(along[axis])))
        orders = [
            along["ty"][::-1] + along["tx"], along["tx"][:1] + along["ty"][::-1] + along["tx"][1:]
        ]
        levels = [along["tx"][::-1] + along["ty"][::-1] for _ in orders]
        for index in range(len(orders[0])):
            steps, pairs = [], []
            for order, level in zip(orders, levels):
                steps.append((*order[index], 1 << level.index(order[index])))
                level.remove(order[index])
            for p in range(sections):
                axis, distance, _ = steps[p % 2]
                pairs += [
                    (flat(p, x, y), flat(p, x, y ^ distance) if axis == "ty" else flat(p, x ^ distance, y))
                    for x in range(rows)
                    for y in range(columns)
                ]
            splits.append((tuple(steps), pairs))
    sent = [((batches, block, width), BF16)] * len(phases)
    whole = ((total_rows, width), BF16)
    mix_rows = (blocks + len(phases)) * block
    cost = 2 * total_rows * width * (width + len(phases) * block)

    def exchange(outs, section):
        return [lax.ppermute(out, AXES, route[section]) for out, route in zip(outs, routes)]

    def inner(upstream, message, mixing):
        return call(
            inner_kernel, [upstream, message, mixing], [((total_rows, width), F32)],
            2 * total_rows * width * nodes,
        )[0]

    given = cotangent.reshape(total_rows, width)
    operands = [
        features, matrix, given, pattern[:, 0, 0], picks, local_edges[:, 0, 0], halo_edges[:, 0, 0]
    ]
    layer, mixing, mask, grad, message, *outs = call(
        functools.partial(first_kernel, phases),
        [pltpu.with_memory_space_constraint(value, pltpu.HBM) for value in operands],
        [
            ((2, total_rows, width), BF16), ((batches, mix_rows, nodes), BF16),
            ((batches * blocks * len(phases), 1, width), F32), whole, whole,
        ] + sent,
        cost + 2 * total_rows * width * width,
        source=pl.BlockSpec(memory_space=pltpu.HBM),
        scratch=[
            (pltpu.VMEM if value.dtype == BF16 else pltpu.SMEM)(value.shape, value.dtype)
            for value in operands
        ] + [pltpu.SemaphoreType.DMA((len(operands),))],
    )
    arrived = exchange(outs, top)
    total = inner(given, message, mixing)
    turned = call(turn_kernel, [features], [((width, total_rows), BF16)], 0)[0]

    layers = [layer]
    for step in range(1, upper):
        moves = [(top - step, top)] + ([(step, 0)] if step < lower else [])
        layers.append(to_sections(layer, moves))

    def fetch_home(values, crossed=False):
        got = None
        for step in range(1, upper):
            moves = [(top, top - step)]
            value = values[top - step]
            if step < lower:
                moves.append((0, step))
                value = call(
                    functools.partial(choose_kernel, top), [value, values[step]], [whole], 0
                )[0]
            new = to_sections(value, moves, crossed=crossed)
            takes = here == top - step
            if step < lower:
                takes = takes | (here == step)
            got = new if step == 1 else jnp.where(takes, new, got)
        return got

    count = len(phases)
    grads, results = {top: grad}, {}
    for section in reversed(range(top)):
        steps = top - section if section >= lower else section
        layer_here = layers[steps]
        if section == lower - 1:
            upstream = call(close_kernel, [mask, total, *arrived], [whole], 0)[0]
            results[section + 1] = upstream
            upstream = to_sections(upstream, [(top, 0)], False)
            grad, message, *outs = call(
                step_kernel, [layer_here, mixing, upstream], [whole, whole] + sent, cost
            )
        elif section > 0:
            upstream, grad, message, *outs = call(
                functools.partial(close_step_kernel, count),
                [mask, total, *arrived, layer_here, mixing],
                [whole, whole, whole] + sent, cost,
            )
            results[section + 1] = upstream
        else:
            product = ((width, width), F32)
            halves = [((width // 2, width), BF16), ((width // 2, width), F32)] if splits else [product]
            upstream, total, *outs = call(
                functools.partial(bottom_kernel, count, top, splits[0][0] if splits else None),
                [mask, total, *arrived, turned, grads[top], fetch_home(grads), layer_here, mixing],
                [whole, ((total_rows, width), F32)] + sent + halves,
                cost + 2 * total_rows * width * (width + nodes),
                scratch=[pltpu.VMEM(*product)] * len(splits[:1]) + [pltpu.VMEM(*whole)] * 2,
            )
            outs, pieces = outs[:count], outs[count:]
            results[1] = upstream
        arrived = exchange(outs, section)
        if section > 0:
            grads[section] = grad
            total = inner(upstream, message, mixing)

    scale = 1.0 / math.sqrt(total_rows * rows * columns)
    if splits:
        parcel, kept = pieces
        for (_, pairs), following in zip(splits, splits[1:]):
            got = lax.ppermute(parcel, AXES, pairs)
            half = (kept.shape[0] // 2, width)
            parcel, kept = call(
                functools.partial(halve_kernel, following[0]), [kept, got],
                [(half, BF16), (half, F32)], 0, scratch=[pltpu.VMEM(kept.shape, F32)],
            )
        got = lax.ppermute(parcel, AXES, splits[-1][1])
        result, summed = call(
            functools.partial(last_kernel, top, count, scale),
            [mask, total, *arrived, results[top], fetch_home(results), kept, got],
            [whole, (kept.shape, F32)], 0, jax.ShapeDtypeStruct,
        )
    else:
        summed = scale * lax.psum_scatter(pieces[0], ("tx", "ty"), scatter_dimension=0, tiled=True)
        result = call(
            functools.partial(last_kernel, top, count, None),
            [mask, total, *arrived, results[top], fetch_home(results)], [whole], 0,
            jax.ShapeDtypeStruct,
        )[0]
    return (summed[None], result.reshape(1, batches, 1, 1, nodes, width))


def solution(mesh):
    in_specs = (
        P("pipe", None, "tx", "ty", None, None),
        P(None, "tx", "ty", None, None),
        P("pipe", None, None),
        P(None, "tx", "ty", None, None, None, None),
        P(None, "tx", "ty", None, None, None, None),
        P(None, "tx", "ty", None, None),
        P(None, "tx", "ty", None),
    )
    out_specs = (P("pipe", ("tx", "ty"), None), P("pipe", None, "tx", "ty", None, None))
    return jax.shard_map(
        per_device, mesh=mesh, in_specs=in_specs, out_specs=out_specs, check_vma=False
    )
```
